32 devices in a mesh: dp: 4 (over y, x), fsdp: 8 (over z, core).
Axes of the slice: x: 2, y: 2, z: 4, core: 2. Of those that a mesh axis runs over, the one named last changes fastest.
Arguments:
- frames: bfloat16 [8192, 1024], P(('dp', 'fsdp')), may hold values from -6 to 6
- lengths: int32 [32, 4], P(('dp', 'fsdp')), may hold values from 1 to 160, 256 in all within a row
- languages: int32 [32, 4], P(('dp', 'fsdp')), may hold values from 0 to 101
- embedding: bfloat16 [102, 1024], P(None, 'fsdp'), may hold values from -3 to 3
- gains: bfloat16 [6, 1024], P(None, 'fsdp'), may hold values from 0.25 to 1.75
- shifts: bfloat16 [6, 1024], P(None, 'fsdp'), may hold values from -2 to 2
- firstup: bfloat16 [1024, 4096], P('fsdp'), may hold values from -0.1875 to 0.1875
- firstdown: bfloat16 [1024, 4096], P('fsdp'), may hold values from -0.09375 to 0.09375
- projection: bfloat16 [1024, 3072], P('fsdp'), may hold values from -0.1875 to 0.1875
- merger: bfloat16 [1024, 1024], P('fsdp'), may hold values from -0.5 to 0.5
- gating: bfloat16 [1024, 2048], P('fsdp'), may hold values from -0.1875 to 0.1875
- kernel: bfloat16 [5, 1024], P(None, 'fsdp'), may hold values from -2.5 to 2.5
- pointwise: bfloat16 [1024, 1024], P('fsdp'), may hold values from -0.1875 to 0.1875
- secondup: bfloat16 [1024, 4096], P('fsdp'), may hold values from -0.1875 to 0.1875
- seconddown: bfloat16 [1024, 4096], P('fsdp'), may hold values from -0.09375 to 0.09375
- cotangent: bfloat16 [8192, 1024], P(('dp', 'fsdp')), may hold values from -6 to 6
Outputs:
- encoded: bfloat16 [8192, 1024], P(('dp', 'fsdp'))
- frames_grad: float32 [8192, 1024], P(('dp', 'fsdp'))
- embedding_grad: float32 [102, 1024], P(None, 'fsdp')
- gains_grad: float32 [6, 1024], P(None, 'fsdp')
- shifts_grad: float32 [6, 1024], P(None, 'fsdp')
- firstup_grad: float32 [1024, 4096], P('fsdp')
- firstdown_grad: float32 [1024, 4096], P('fsdp')
- projection_grad: float32 [1024, 3072], P('fsdp')
- merger_grad: float32 [1024, 1024], P('fsdp')
- gating_grad: float32 [1024, 2048], P('fsdp')
- kernel_grad: float32 [5, 1024], P(None, 'fsdp')
- pointwise_grad: float32 [1024, 1024], P('fsdp')
- secondup_grad: float32 [1024, 4096], P('fsdp')
- seconddown_grad: float32 [1024, 4096], P('fsdp')
The draws below stay inside these ranges and needn't reach their ends.
Inputs may be any that keep to these rules, and one draw needn't show every extreme that they name: Each row of lengths sums to 256 and has exactly 160 as its largest entry.
All inputs are finite; a program needn't handle non-finite values.
Results may differ from the reference program's by a relative error of at most 0.019.
Values may be sent and summed in bfloat16 or wider, within the bound.
No kernel may reach another device: no remote copies, remote signals or barrier semaphores. Data moves between devices by JAX's collectives and lax.ppermute only.
A program may use at most 256 MiB of HBM per device.

```python
import math
import jax
import jax.numpy as jnp
import numpy as np
from jax import lax

D = 1024
HEADS = 8
HEAD_DIM = 128
FF = 4096
KERN = 5
LANGS = 102
TOK_DEV = 256
UTT_DEV = 4
LONGEST = 160
TOKENS = 8192
N_DP = 4
N_FSDP = 8


def place_ends(values, own_key, least, high):
    shape = values.shape
    spot = [jax.random.randint(jax.random.fold_in(own_key, axis), (), 0, shape[axis]) for axis in range(len(shape))]
    values = values.at[tuple(spot)].set(least)
    longest = shape.index(max(shape))
    spot[longest] = (spot[longest] + 1) % shape[longest]
    return values.at[tuple(spot)].set(high)


def block_levels(own_key, shape, split, low, largest):
    loudness = 1.0
    for axis_at, blocks in split:
        draws = jax.random.uniform(jax.random.fold_in(jax.random.fold_in(own_key, 6), axis_at), (blocks,), jnp.float32, low / len(split), largest / len(split))
        loudness = loudness * jnp.repeat(jnp.exp(draws), shape[axis_at] // blocks).reshape((-1,) + (1,) * (len(shape) - 1 - axis_at))
    return loudness


def split_up(amount, total, reach, slope):
    weights = [(1 << 20) // math.isqrt(rank ** slope) + 1 for rank in range(2, amount + 1)]
    rest, counts = total - reach - (amount - 1), [1] * (amount - 1)
    while rest > 0:
        candidates = [i for i in range(amount - 1) if counts[i] < reach]
        pool, left = sum([weights[i] for i in candidates]), rest
        for i in candidates:
            extra = min(reach - counts[i], max(1, left * weights[i] // pool), rest)
            counts[i] = counts[i] + extra
            rest = rest - extra
    return np.array([reach] + counts)


def uneven_parts(own_key, count, total, reach, slope):
    if count == 2:
        one = jax.random.randint(own_key, (), max(1, total - reach), min(reach, total - 1) + 1)
        return jnp.stack([one, total - one])
    sizes = jnp.asarray(split_up(count, total, reach, slope), jnp.int32)
    twos = (count - 1) // 2
    donor, receiver = sizes[1:1 + 2 * twos:2], sizes[2:2 + 2 * twos:2]
    margin = jnp.minimum(donor - 1, reach - receiver)
    passed = jax.random.randint(jax.random.fold_in(own_key, 1), (twos,), 0, 1 << 20) % (margin + 1)
    sizes = sizes.at[1:1 + 2 * twos:2].set(donor - passed).at[2:2 + 2 * twos:2].set(receiver + passed)
    return sizes[jax.random.permutation(jax.random.fold_in(own_key, 2), count)]


def scatter_about(stream_key, extent, scale, limit, pieces=(), held_as=jnp.bfloat16):
    drawn = scale * jax.random.normal(stream_key, extent, jnp.float32)
    if pieces:
        drawn = drawn * block_levels(stream_key, extent, pieces, -0.22, 0.18)
    return jnp.clip(drawn, -limit, limit).astype(held_as)


def setup_inputs(seed: int = 0) -> dict:
    splits = jax.random.split(jax.random.key(seed), 17)
    frames = scatter_about(splits[0], (TOKENS, D), 1.0, 6.0, ((0, 32),))
    lengths = jax.vmap(lambda own: uneven_parts(own, UTT_DEV, TOK_DEV, LONGEST, 2))(jax.random.split(splits[1], (N_DP * N_FSDP))).reshape((N_DP * N_FSDP, UTT_DEV)).astype(jnp.int32)
    languages = place_ends(jax.random.randint(splits[2], (N_DP * N_FSDP, UTT_DEV), 0, LANGS), jax.random.fold_in(splits[2], 1), 0, LANGS - 1).astype(jnp.int32)
    embedding = scatter_about(splits[3], (LANGS, D), 0.5, 3.0, ((1, 8),))
    gains = jnp.clip(1.0 + 0.15 * jax.random.normal(splits[4], (6, D), jnp.float32), 0.25, 1.75).astype(jnp.bfloat16)
    shifts = scatter_about(splits[5], (6, D), 0.3, 2.0, ((1, 8),))
    firstup = scatter_about(splits[6], (D, FF), D ** -0.5, 0.1875, ((0, 8),))
    firstdown = scatter_about(splits[7], (D, FF), FF ** -0.5, 0.09375, ((0, 8),))
    projection = scatter_about(splits[8], (D, 3 * D), D ** -0.5, 0.1875, ((0, 8),))
    merger = scatter_about(splits[9], (D, D), (D // 8) ** -0.5, 0.5, ((0, 8),))
    gating = scatter_about(splits[10], (D, 2 * D), D ** -0.5, 0.1875, ((0, 8),))
    kernel = scatter_about(splits[11], (KERN, D), KERN ** -0.5, 2.5, ((1, 8),))
    pointwise = scatter_about(splits[12], (D, D), D ** -0.5, 0.1875, ((0, 8),))
    secondup = scatter_about(splits[13], (D, FF), D ** -0.5, 0.1875, ((0, 8),))
    seconddown = scatter_about(splits[14], (D, FF), FF ** -0.5, 0.09375, ((0, 8),))
    cotangent = scatter_about(splits[15], (TOKENS, D), 1.0, 6.0, ((0, 32),))
    return dict(frames=frames, lengths=lengths, languages=languages, embedding=embedding, gains=gains, shifts=shifts, firstup=firstup, firstdown=firstdown, projection=projection, merger=merger, gating=gating, kernel=kernel, pointwise=pointwise, secondup=secondup, seconddown=seconddown, cotangent=cotangent)


@jax.custom_vjp
def low(v):
    return lax.optimization_barrier(v.astype(jnp.bfloat16)).astype(jnp.float32)

@jax.custom_vjp
def low_back(v):
    return v

def low_keep(v):
    return (low(v), None)

def low_pass(kept, grad):
    return (grad,)

def back_keep(v):
    return (v, None)

def back_low(kept, grad):
    return (low(grad),)
low.defvjp(low_keep, low_pass)
low_back.defvjp(back_keep, back_low)
norm_epsilon = 1e-05
masked_score = -1000000000.0
highest = lax.Precision.HIGHEST

def norm_rows(values, gain_row, shift_row):
    centred = values - lax.optimization_barrier(jnp.mean(values, axis=-1, keepdims=True))
    spread = lax.optimization_barrier(jnp.mean(centred * centred, axis=-1, keepdims=True))
    return centred * lax.rsqrt(spread + norm_epsilon) * gain_row + shift_row

def rotate(values, cosine, sine):
    half_dim = values.shape[-1] // 2
    first_half = values[..., :half_dim]
    second_half = values[..., half_dim:]
    return jnp.concatenate([first_half * cosine - second_half * sine, second_half * cosine + first_half * sine], axis=-1)

def depthwise_time(values, kernel, segment):
    half_kernel = kernel.shape[0] // 2
    length = values.shape[-2]
    leading = values.ndim - 2
    padded = jnp.pad(values, [(0, 0)] * leading + [(half_kernel, half_kernel), (0, 0)])
    segment_pad = jnp.pad(segment, [(0, 0)] * leading + [(half_kernel, half_kernel)], constant_values=-1)
    summed = jnp.zeros_like(values)
    for tap_index in range(kernel.shape[0]):
        keeping = (segment_pad[..., tap_index:tap_index + length] == segment)[..., None]
        summed = summed + jnp.where(keeping, padded[..., tap_index:tap_index + length, :], 0.0) * kernel[tap_index]
    return summed

def layout(lengths, languages, frame_count):
    finish = jnp.cumsum(lengths, axis=-1).astype(jnp.int32)
    begins = (finish - lengths).astype(jnp.int32)
    indices = jnp.arange(frame_count, dtype=jnp.int32)
    segment = lax.optimization_barrier(jnp.sum((indices[None, :, None] >= finish[:, None, :]).astype(jnp.int32), axis=-1)).astype(jnp.int32)
    owners = segment[:, :, None] == jnp.arange(lengths.shape[-1], dtype=jnp.int32)[None, None, :]
    first_row = lax.optimization_barrier(jnp.sum(jnp.where(owners, begins[:, None, :], 0), axis=-1)).astype(jnp.int32)
    language_row = lax.optimization_barrier(jnp.sum(jnp.where(owners, languages[:, None, :], 0), axis=-1)).astype(jnp.int32)
    return (segment, (indices[None, :] - first_row).astype(jnp.int32), language_row)

def angles(position):
    half_dim = HEAD_DIM // 2
    frequency = 10000.0 ** (-jnp.arange(half_dim, dtype=jnp.float32) / half_dim)
    turned = position.astype(jnp.float32)[..., None] * frequency
    return (jnp.cos(turned)[..., None, :], jnp.sin(turned)[..., None, :])

def feed_forward(values, gain_row, shift_row, upward, downward):
    hidden = low(norm_rows(values, gain_row, shift_row))
    expanded = low_back(jnp.matmul(hidden, upward, precision=highest))
    activated = low(jax.nn.silu(expanded))
    return low_back(jnp.matmul(activated, downward.T, precision=highest))

def attention(values, gain_row, shift_row, projection, merger, segment, cosine, sine):
    hidden = low(norm_rows(values, gain_row, shift_row))
    projected = low_back(jnp.matmul(hidden, projection, precision=highest))
    shaped = projected.reshape(projected.shape[:-1] + (3, HEADS, HEAD_DIM))
    queries = low(rotate(shaped[..., 0, :, :], cosine, sine) * HEAD_DIM ** (-0.5))
    keys_rot = low(rotate(shaped[..., 1, :, :], cosine, sine))
    values_low = low(shaped[..., 2, :, :])
    scores = low_back(jnp.einsum('gqhd,gkhd->ghqk', queries, keys_rot, precision=highest))
    matching = segment[:, None, :, None] == segment[:, None, None, :]
    weights = jax.nn.softmax(jnp.where(matching, scores, masked_score), axis=-1)
    mixed = low(low_back(jnp.einsum('ghqk,gkhd->gqhd', low(weights), values_low, precision=highest)))
    flat = mixed.reshape(mixed.shape[:2] + (HEADS * HEAD_DIM,))
    return low_back(jnp.matmul(flat, merger, precision=highest))

def convolution(values, gains, shifts, gating, kernel, pointwise, segment):
    hidden = low(norm_rows(values, gains[2], shifts[2]))
    doubled = low_back(jnp.matmul(hidden, gating, precision=highest))
    half_width = doubled.shape[-1] // 2
    gated = doubled[..., :half_width] * jax.nn.sigmoid(doubled[..., half_width:])
    filtered = depthwise_time(gated, kernel, segment)
    activated = low(jax.nn.silu(norm_rows(filtered, gains[3], shifts[3])))
    return low_back(jnp.matmul(activated, pointwise, precision=highest))

def layer(frames_in, embedding, gains, shifts, firstup, firstdown, projection, merger, gating, kernel, pointwise, secondup, seconddown, segment, cosine, sine, language_row):
    start_sum = frames_in + jnp.take(embedding, language_row, axis=0)
    after_first = start_sum + 0.5 * feed_forward(start_sum, gains[0], shifts[0], firstup, firstdown)
    after_attention = after_first + attention(after_first, gains[1], shifts[1], projection, merger, segment, cosine, sine)
    after_conv = after_attention + convolution(after_attention, gains, shifts, gating, kernel, pointwise, segment)
    after_second = after_conv + 0.5 * feed_forward(after_conv, gains[4], shifts[4], secondup, seconddown)
    return norm_rows(after_second, gains[5], shifts[5])

def reference(frames, lengths, languages, embedding, gains, shifts, firstup, firstdown, projection, merger, gating, kernel, pointwise, secondup, seconddown, cotangent):
    devices = N_DP * N_FSDP
    grouped = math.gcd(devices, 8)
    blocks = devices // grouped
    segment, position, language_row = layout(lengths, languages, TOK_DEV)
    cosine, sine = angles(position)
    weights = tuple((matrix.astype(jnp.float32) for matrix in (embedding, gains, shifts, firstup, firstdown, projection, merger, gating, kernel, pointwise, secondup, seconddown)))

    def blocked(array):
        return array.reshape((blocks, grouped) + array.shape[1:])
    frame_blocks = blocked(frames.astype(jnp.float32).reshape(devices, TOK_DEV, frames.shape[1]))
    cot_blocks = blocked(cotangent.astype(jnp.float32).reshape(devices, TOK_DEV, frames.shape[1]))

    def advance(sums, inputs):
        frame_block, cot_block, seg_block, cos_block, sin_block, lang_block = inputs

        def forward(frame_in, *params):
            return layer(frame_in, *params, seg_block, cos_block, sin_block, lang_block)
        result, pullback = jax.vjp(forward, frame_block, *weights)
        gradients = pullback(cot_block)
        updated = tuple((running + fresh for running, fresh in zip(sums, gradients[1:])))
        return (updated, (result.astype(jnp.bfloat16), gradients[0]))
    starting = tuple((jnp.zeros_like(matrix) for matrix in weights))
    sums, (encoded, frames_grad) = lax.scan(advance, starting, (frame_blocks, cot_blocks, blocked(segment), blocked(cosine), blocked(sine), blocked(language_row)))
    return (encoded.reshape(frames.shape), frames_grad.reshape(frames.shape), sums[0], sums[1], sums[2], sums[3], sums[4], sums[5], sums[6], sums[7], sums[8], sums[9], sums[10], sums[11])
```

```python
import functools

import jax
import jax.numpy as jnp
import numpy as np
from jax import lax
from jax.experimental import pallas as pl
from jax.experimental.pallas import tpu as pltpu
from jax.sharding import Mesh
from jax.sharding import PartitionSpec as P

HEAD_DIM = 128


norm_epsilon = 1e-05
masked_score = -1000000000.0


def norm_rows(values, gain_row, shift_row):
    centred = values - jnp.mean(values, axis=-1, keepdims=True)
    spread = jnp.mean(centred * centred, axis=-1, keepdims=True)
    return centred * lax.rsqrt(spread + norm_epsilon) * gain_row + shift_row


def rotate(values, cosine, sine):
    half_dim = values.shape[-1] // 2
    first_half = values[..., :half_dim]
    second_half = values[..., half_dim:]
    return jnp.concatenate(
        [first_half * cosine - second_half * sine, second_half * cosine + first_half * sine],
        axis=-1,
    )


def depthwise_time(values, kernel, segment):
    half_kernel = kernel.shape[0] // 2
    length = values.shape[-2]
    padded = jnp.pad(values, ((half_kernel, half_kernel), (0, 0)))
    segment_pad = jnp.pad(segment, (half_kernel, half_kernel), constant_values=-1)
    summed = jnp.zeros_like(values)
    for tap_index in range(kernel.shape[0]):
        keeping = (segment_pad[tap_index : tap_index + length] == segment)[:, None]
        summed = (
            summed
            + jnp.where(keeping, padded[tap_index : tap_index + length, :], 0.0) * kernel[tap_index]
        )
    return summed


def layout(lengths, languages, frame_count):
    utterances = jnp.arange(lengths.shape[-1], dtype=jnp.int32)
    earlier = utterances[:, None] <= utterances[None, :]
    finish = jnp.sum(jnp.where(earlier[None], lengths[:, :, None], 0), axis=1)
    begins = finish - lengths
    indices = jnp.arange(frame_count, dtype=jnp.int32)
    segment = jnp.sum((indices[None, :, None] >= finish[:, None, :]).astype(jnp.int32), axis=-1)
    owners = segment[:, :, None] == jnp.arange(lengths.shape[-1], dtype=jnp.int32)[None, None, :]
    first_row = jnp.sum(jnp.where(owners, begins[:, None, :], 0), axis=-1)
    language_row = jnp.sum(jnp.where(owners, languages[:, None, :], 0), axis=-1)
    return (segment, indices[None, :] - first_row, language_row)


def angles(position):
    half_dim = HEAD_DIM // 2
    frequency = 10000.0 ** (-jnp.arange(half_dim, dtype=jnp.float32) / half_dim)
    turned = position.astype(jnp.float32)[..., None] * frequency
    return (jnp.cos(turned)[..., None, :], jnp.sin(turned)[..., None, :])


def tie(value, *others):
    return lax.optimization_barrier((value, *others))[0]


def rows_dot(inputs, weight):
    return jnp.dot(inputs, weight, preferred_element_type=jnp.float32)


VMEM_LIMIT = 60 * 1024 * 1024
QUARTERS = 4
BITS = (0, 1)


def swap_dp(value, bit, size):
    return lax.ppermute(value, "dp", [(i, i ^ (1 << bit)) for i in range(size)])


def swap_core(value):
    return lax.ppermute(value, "core", [(0, 1), (1, 0)])


def last_bit(index, order):
    return [bit for bit in order if index >> bit & 1][-1]


def assemble_kernel(layers, widths, place, *refs):
    count = len(widths)
    own, other = refs[:count], refs[count : 2 * count]
    gathered = refs[2 * count]
    pieces = refs[2 * count + 1 : 2 * count + QUARTERS]
    others = refs[2 * count + QUARTERS : 2 * count + 2 * QUARTERS - 1]
    outs = refs[2 * count + 2 * QUARTERS - 1 : -1]
    sems = refs[-1]
    quarter, layer, core = place[0], place[1], place[2]
    copies = []

    def move(source, target):
        copy = pltpu.make_async_copy(source, target, sems.at[len(copies)])
        copy.start()
        copies.append(copy)

    base = 0
    for i, width in enumerate(widths):
        part = width // QUARTERS
        span = pl.ds(base, part)
        mine = pl.ds(pl.multiple_of(quarter * part, part), part)
        move(gathered.at[:, :, span], outs[i].at[:, :, mine])
        for r in range(1, QUARTERS):
            column = pl.ds(pl.multiple_of((quarter ^ r) * part, part), part)
            for source, lane in ((own[i], core), (other[i], 1 - core)):
                move(source.at[:, column], outs[i].at[2 * layer + lane, :, column])
            for source, lane in ((pieces[r - 1], core), (others[r - 1], 1 - core)):
                for k in range(1, layers):
                    row = lax.rem(layer + k, layers) * 2 + lane
                    move(source.at[k - 1, :, span], outs[i].at[row, :, column])
        base += part
    for copy in copies:
        copy.wait()


def assemble(place, layers, own, other, gathered, pieces, others):
    widths = [w.shape[1] for w in own]
    rows = own[0].shape[0]
    copies = len(widths) * (1 + (QUARTERS - 1) * 2 * layers)
    operands = [*own, *other, gathered, *pieces, *others]
    outs = pl.pallas_call(
        functools.partial(assemble_kernel, layers, widths),
        out_shape=[jax.ShapeDtypeStruct((2 * layers, rows, w), jnp.bfloat16) for w in widths],
        in_specs=[pl.BlockSpec(memory_space=pltpu.SMEM)]
        + [pl.BlockSpec(memory_space=pl.ANY)] * len(operands),
        out_specs=[pl.BlockSpec(memory_space=pl.ANY)] * len(widths),
        scratch_shapes=[pltpu.SemaphoreType.DMA((copies,))],
    )(place, *operands)
    return [out.reshape(2 * layers * rows, w) for out, w in zip(outs, widths)]


def weight_terms_kernel(widths, wanted, whole, given, place, *refs):
    count = len(widths)
    lefts, rights = refs[:count], refs[count : 2 * count]
    arrived = refs[2 * count : -1]
    out = refs[-1]
    quarter, core = place[0], place[2]
    side = 1 - core if whole else core
    base = 0
    for i, width in enumerate(widths):
        part = width // QUARTERS
        layers, _, rows, tokens = lefts[i].shape
        left = lefts[i][:, pl.ds(side, 1)].reshape(layers * rows, tokens)
        tile = min(part, 256)

        def tiles(n, body):
            if n == 1:
                body(0)
            else:
                pl.loop(0, n)(body)

        if whole:

            def step(t, i=i, left=left, base=base, tile=tile):
                column = pl.multiple_of(t * tile, tile)
                product = jnp.dot(
                    left, rights[i][:, pl.ds(column, tile)], preferred_element_type=jnp.float32
                )
                out[:, pl.ds(QUARTERS * base + column, tile)] = product.astype(out.dtype)

            tiles(width // tile, step)
        else:
            for at, r in enumerate(wanted):
                start = (quarter ^ r) * part

                def step(t, i=i, left=left, base=base, part=part, tile=tile, at=at, r=r, start=start):
                    column = pl.multiple_of(t * tile, tile)
                    source = pl.multiple_of(start + column, tile)
                    product = jnp.dot(
                        left, rights[i][:, pl.ds(source, tile)], preferred_element_type=jnp.float32
                    )
                    full = pl.ds(pl.multiple_of(QUARTERS * base + source, tile), tile)
                    product += arrived[0][:, full].astype(jnp.float32)
                    narrow = pl.ds(pl.multiple_of(base + column, tile), tile)
                    for ref, holds in zip(arrived[1:], given):
                        product += ref[holds.index(r), :, narrow].astype(jnp.float32)
                    out[at, :, narrow] = product.astype(out.dtype)

                tiles(part // tile, step)
        base += part


def weight_terms(place, lefts, rights, arrived=(), wanted=None, given=()):
    widths = [right.shape[1] for right in rights]
    layers, _, rows, tokens = lefts[0].shape
    whole = wanted is None
    if whole:
        shape = (layers * rows, sum(widths))
        flops = 2 * tokens * layers * rows * sum(widths)
    else:
        shape = (len(wanted), layers * rows, sum(widths) // QUARTERS)
        flops = 2 * tokens * layers * rows * sum(widths) // QUARTERS * len(wanted)
    operands = [*lefts, *rights, *arrived]
    return pl.pallas_call(
        functools.partial(weight_terms_kernel, widths, wanted, whole, given),
        out_shape=jax.ShapeDtypeStruct(shape, jnp.bfloat16),
        in_specs=[pl.BlockSpec(memory_space=pltpu.SMEM)]
        + [pl.BlockSpec(memory_space=pltpu.VMEM)] * len(operands),
        out_specs=pl.BlockSpec(memory_space=pltpu.VMEM),
        compiler_params=pltpu.CompilerParams(vmem_limit_bytes=VMEM_LIMIT),
        cost_estimate=pl.CostEstimate(
            flops=flops,
            bytes_accessed=2 * sum(int(np.prod(x.shape)) for x in operands) + 2 * int(np.prod(shape)),
            transcendentals=0,
        ),
    )(place, *operands)


def spread_kernel(widths, place, *refs):
    pieces, outs = refs[:QUARTERS], refs[QUARTERS:]
    quarter = place[0]
    base = 0
    for i, width in enumerate(widths):
        part = width // QUARTERS
        for r in range(QUARTERS):
            column = pl.ds(pl.multiple_of((quarter ^ r) * part, part), part)
            outs[i][:, column] = pieces[r][:, pl.ds(base, part)].astype(jnp.float32)
        base += part


def spread(place, widths, pieces):
    rows = pieces[0].shape[0]
    return pl.pallas_call(
        functools.partial(spread_kernel, widths),
        out_shape=[jax.ShapeDtypeStruct((rows, w), jnp.float32) for w in widths],
        in_specs=[pl.BlockSpec(memory_space=pltpu.SMEM)]
        + [pl.BlockSpec(memory_space=pltpu.VMEM)] * QUARTERS,
        out_specs=[pl.BlockSpec(memory_space=pltpu.VMEM)] * len(widths),
        compiler_params=pltpu.CompilerParams(vmem_limit_bytes=VMEM_LIMIT),
    )(place, *pieces)


def gather_weights(place, sizes, groups):
    dp_size, layers = sizes
    quarter, layer, core = place[0], place[1], place[2]
    gathered = []
    for group in groups:
        mine = jnp.concatenate(
            [
                lax.dynamic_slice_in_dim(w, quarter * (w.shape[1] // QUARTERS), w.shape[1] // QUARTERS, 1)
                for w in group
            ],
            axis=1,
        )
        gathered.append(lax.all_gather(mine, ("z", "core"), axis=0, tiled=False))
    fulls = []
    for index, group in enumerate(groups):
        order = BITS if index % 2 == 0 else BITS[::-1]
        other = [swap_core(w) for w in group]
        rows, width = gathered[index].shape[1:]
        grid = gathered[index].reshape(layers, 2, rows, width)
        held = {
            0: jnp.stack(
                [
                    lax.dynamic_slice(
                        grid, (lax.rem(layer + k, layers), core, 0, 0), (1, 1, rows, width)
                    )[0, 0]
                    for k in range(1, layers)
                ]
            )
        }
        for r in range(1, QUARTERS):
            bit = last_bit(r, order)
            held[r] = swap_dp(held[r ^ (1 << bit)], bit, dp_size)
        pieces = [held[r] for r in range(1, QUARTERS)]
        others = [swap_core(piece) for piece in pieces]
        fulls.append(assemble(place, layers, group, other, gathered[index], pieces, others))
    return fulls


def weight_grads(place, sizes, pairs, flip):
    dp_size, layers = sizes
    first, second = BITS if not flip else BITS[::-1]
    lefts = []
    for left, _ in pairs:
        tokens, features = left.shape
        lefts.append(left.T.reshape(layers, 2, features // (2 * layers), tokens))
    rights = [right for _, right in pairs]
    widths = [right.shape[1] for right in rights]
    across = swap_core(weight_terms(place, lefts, rights))
    sent = [r for r in range(QUARTERS) if r >> first & 1]
    first_sums = swap_dp(weight_terms(place, lefts, rights, (across,), sent), first, dp_size)
    first_given = [r ^ (1 << first) for r in sent]
    second_sums = swap_dp(
        weight_terms(place, lefts, rights, (across, first_sums), [1 << second], (first_given,)),
        second,
        dp_size,
    )
    own = weight_terms(
        place, lefts, rights, (across, first_sums, second_sums), [0], (first_given, [0])
    )[0]
    summed = lax.psum_scatter(own, "z", scatter_dimension=0, tiled=True)
    bit = len(BITS)
    while 1 << bit < dp_size:
        summed = summed + swap_dp(summed, bit, dp_size)
        bit += 1
    held = {0: summed}
    for r in range(1, QUARTERS):
        bit = last_bit(r, (second, first))
        held[r] = swap_dp(held[r ^ (1 << bit)], bit, dp_size)
    return spread(place, widths, [held[r] for r in range(QUARTERS)])


def gather_small(arrays):
    rows = [a.shape[0] for a in arrays]
    packed = jnp.concatenate(arrays, axis=0)
    packed = jnp.pad(packed, ((0, -packed.shape[0] % 16), (0, 0)))
    full = lax.all_gather(packed, ("z", "core"), axis=0, tiled=False)
    full = full.transpose(1, 0, 2).reshape(packed.shape[0], -1)
    pieces, start = [], 0
    for count in rows:
        pieces.append(full[start : start + count])
        start += count
    return pieces


def sum_small(place, sizes, arrays):
    rows = [a.shape[0] for a in arrays]
    packed = jnp.concatenate(arrays, axis=0)
    width = packed.shape[1] // (2 * sizes[1])
    total = lax.psum(packed, ("dp", "z", "core"))
    mine = lax.dynamic_slice_in_dim(total, (place[1] * 2 + place[2]) * width, width, 1)
    pieces, start = [], 0
    for count in rows:
        pieces.append(mine[start : start + count])
        start += count
    return pieces


def times_transposed(left_side, right_side):
    return lax.dot_general(
        left_side, right_side, (((1,), (1,)), ((), ())), preferred_element_type=jnp.float32
    )


def feed_forward(values, gain_row, shift_row, upward, downward):
    normed, norm_pull = jax.vjp(norm_rows, values, gain_row, shift_row)
    hidden = normed.astype(jnp.bfloat16)
    expanded = rows_dot(hidden, upward)
    activated, silu_pull = jax.vjp(jax.nn.silu, expanded)
    active_low = activated.astype(jnp.bfloat16)
    return (times_transposed(active_low, downward), (norm_pull, hidden, silu_pull, active_low))


def feed_backward(gradient, stored, upward, downward):
    norm_pull, hidden, silu_pull, active_low = stored
    grad_low = gradient.astype(jnp.bfloat16)
    active_grad = rows_dot(grad_low, downward)
    expand_grad = silu_pull(active_grad)[0].astype(jnp.bfloat16)
    hidden_grad = times_transposed(expand_grad, upward)
    values_grad, gain_grad, shift_grad = norm_pull(hidden_grad)
    return (
        values_grad,
        gain_grad,
        shift_grad,
        (hidden, expand_grad),
        (grad_low, active_low),
    )


def attention_forward(values, gain_row, shift_row, projection, merger, matching, cosine, sine):
    normed, norm_pull = jax.vjp(norm_rows, values, gain_row, shift_row)
    hidden = normed.astype(jnp.bfloat16)
    projected = rows_dot(hidden, projection)
    frame_count = projected.shape[0]
    head_count = projected.shape[1] // (3 * HEAD_DIM)
    shaped = projected.reshape(frame_count, 3, head_count, HEAD_DIM)

    def turning(query_raw, key_raw):
        return (rotate(query_raw, cosine, sine) * HEAD_DIM ** (-0.5), rotate(key_raw, cosine, sine))

    (query_rot, key_rot), turn_pull = jax.vjp(turning, shaped[:, 0], shaped[:, 1])
    query_low = query_rot.astype(jnp.bfloat16)
    key_low = key_rot.astype(jnp.bfloat16)
    value_low = shaped[:, 2].astype(jnp.bfloat16)
    scores = jnp.where(
        matching,
        jnp.einsum("qhd,khd->hqk", query_low, key_low, preferred_element_type=jnp.float32),
        masked_score,
    )
    highest_score = jnp.max(scores, axis=-1, keepdims=True)
    log_total = highest_score + jnp.log(
        jnp.sum(jnp.exp(scores - highest_score), axis=-1, keepdims=True)
    )
    probs_low = jnp.exp(scores - log_total).astype(jnp.bfloat16)
    mixed = jnp.einsum("hqk,khd->qhd", probs_low, value_low, preferred_element_type=jnp.float32)
    mixed_low = mixed.reshape(frame_count, head_count * HEAD_DIM).astype(jnp.bfloat16)
    return (
        rows_dot(mixed_low, merger),
        (norm_pull, hidden, turn_pull, query_low, key_low, value_low, log_total, mixed_low),
    )


def attention_backward(gradient, stored, projection, merger, matching):
    norm_pull, hidden, turn_pull, query_low, key_low, value_low, log_total, mixed_low = stored
    frame_count, head_count = (query_low.shape[0], query_low.shape[1])
    grad_low = gradient.astype(jnp.bfloat16)
    mixed_grad = (
        times_transposed(grad_low, merger)
        .astype(jnp.bfloat16)
        .reshape(frame_count, head_count, HEAD_DIM)
    )
    scores = jnp.where(
        matching,
        jnp.einsum("qhd,khd->hqk", query_low, key_low, preferred_element_type=jnp.float32),
        masked_score,
    )
    probs = jnp.exp(scores - log_total)
    value_grad = jnp.einsum(
        "hqk,qhd->khd", probs.astype(jnp.bfloat16), mixed_grad, preferred_element_type=jnp.float32
    )
    probs_grad = jnp.einsum(
        "qhd,khd->hqk", mixed_grad, value_low, preferred_element_type=jnp.float32
    )
    score_grad = (
        probs * (probs_grad - jnp.sum(probs * probs_grad, axis=-1, keepdims=True))
    ).astype(jnp.bfloat16)
    query_grad = jnp.einsum("hqk,khd->qhd", score_grad, key_low, preferred_element_type=jnp.float32)
    key_grad = jnp.einsum("hqk,qhd->khd", score_grad, query_low, preferred_element_type=jnp.float32)
    query_raw_grad, key_raw_grad = turn_pull((query_grad, key_grad))
    stacked = jnp.stack([query_raw_grad, key_raw_grad, value_grad], axis=1)
    projected_grad = stacked.reshape(frame_count, 3 * head_count * HEAD_DIM).astype(jnp.bfloat16)
    hidden_grad = times_transposed(projected_grad, projection)
    values_grad, gain_grad, shift_grad = norm_pull(hidden_grad)
    return (
        values_grad,
        gain_grad,
        shift_grad,
        (hidden, projected_grad),
        (mixed_low, grad_low),
    )


def conv_forward(values, gain_rows, shift_rows, gating, taps, pointwise, segment):
    normed, norm_pull = jax.vjp(norm_rows, values, gain_rows[2], shift_rows[2])
    hidden = normed.astype(jnp.bfloat16)
    doubled = rows_dot(hidden, gating)

    def mixing(doubled_in, taps_in):
        half_width = doubled_in.shape[1] // 2
        gated = doubled_in[:, :half_width] * jax.nn.sigmoid(doubled_in[:, half_width:])
        return depthwise_time(gated, taps_in, segment)

    filtered, mix_pull = jax.vjp(mixing, doubled, taps)
    renormed, inner_pull = jax.vjp(norm_rows, filtered, gain_rows[3], shift_rows[3])
    activated, silu_pull = jax.vjp(jax.nn.silu, renormed)
    active_low = activated.astype(jnp.bfloat16)
    return (
        rows_dot(active_low, pointwise),
        (norm_pull, hidden, mix_pull, inner_pull, silu_pull, active_low),
    )


def conv_backward(gradient, stored, gating, pointwise):
    norm_pull, hidden, mix_pull, inner_pull, silu_pull, active_low = stored
    grad_low = gradient.astype(jnp.bfloat16)
    active_grad = times_transposed(grad_low, pointwise)
    renormed_grad = silu_pull(active_grad)[0]
    filtered_grad, inner_gain, inner_shift = inner_pull(renormed_grad)
    doubled_grad, taps_grad = mix_pull(filtered_grad)
    doubled_low = doubled_grad.astype(jnp.bfloat16)
    hidden_grad = times_transposed(doubled_low, gating)
    values_grad, outer_gain, outer_shift = norm_pull(hidden_grad)
    return (
        values_grad,
        outer_gain,
        outer_shift,
        inner_gain,
        inner_shift,
        taps_grad,
        (hidden, doubled_low),
        (active_low, grad_low),
    )


def shards(
    sizes,
    frames,
    lengths,
    languages,
    embedding,
    gains,
    shifts,
    firstup,
    firstdown,
    projection,
    merger,
    gating,
    kernel,
    pointwise,
    secondup,
    seconddown,
    cotangent,
):
    frame_count = frames.shape[0]
    segment_all, position_all, language_all = layout(lengths, languages, frame_count)
    segment = segment_all[0]
    language_row = language_all[0]
    cosine, sine = angles(position_all[0])
    matching = (segment[:, None] == segment[None, :])[None, :, :]
    dp_index = lax.axis_index("dp").astype(jnp.int32)
    place = jnp.stack(
        [
            lax.rem(dp_index, jnp.int32(QUARTERS)),
            lax.axis_index("z").astype(jnp.int32),
            lax.axis_index("core").astype(jnp.int32),
        ]
    )
    table_full, gain_full, shift_full, kernel_full = gather_small(
        [embedding, gains, shifts, kernel]
    )
    groups = gather_weights(
        place,
        sizes,
        [[firstup], [firstdown, projection], [merger, gating, pointwise, secondup], [seconddown]],
    )
    (
        firstup_full,
        firstdown_full,
        projection_full,
        merger_full,
        gating_full,
        pointwise_full,
        secondup_full,
        seconddown_full,
    ) = [w for group in groups for w in group]
    gain_rows = gain_full.astype(jnp.float32)
    shift_rows = shift_full.astype(jnp.float32)
    taps = kernel_full.astype(jnp.float32)
    language_hot = (
        language_row[:, None] == jnp.arange(table_full.shape[0], dtype=jnp.int32)[None, :]
    ).astype(jnp.float32)
    start_sum = frames.astype(jnp.float32) + jnp.dot(
        language_hot.astype(jnp.bfloat16), table_full, preferred_element_type=jnp.float32
    )
    first_branch, first_stored = feed_forward(
        start_sum, gain_rows[0], shift_rows[0], firstup_full, firstdown_full
    )
    after_first = start_sum + 0.5 * first_branch
    attend_branch, attend_stored = attention_forward(
        after_first, gain_rows[1], shift_rows[1], projection_full, merger_full, matching, cosine, sine
    )
    after_attention = after_first + attend_branch
    conv_branch, conv_stored = conv_forward(
        after_attention, gain_rows, shift_rows, gating_full, taps, pointwise_full, segment
    )
    after_conv = after_attention + conv_branch
    second_branch, second_stored = feed_forward(
        after_conv, gain_rows[4], shift_rows[4], secondup_full, seconddown_full
    )
    after_second = after_conv + 0.5 * second_branch
    encoded, final_pull = jax.vjp(norm_rows, after_second, gain_rows[5], shift_rows[5])
    grad_second, final_gain, final_shift = final_pull(cotangent.astype(jnp.float32))
    branch_grad, second_gain, second_shift, secondup_grad, seconddown_grad = feed_backward(
        0.5 * grad_second, second_stored, secondup_full, seconddown_full
    )
    grad_conv = grad_second + branch_grad
    (
        branch_grad,
        outer_gain,
        outer_shift,
        inner_gain,
        inner_shift,
        taps_grad,
        gating_grad,
        pointwise_grad,
    ) = conv_backward(grad_conv, conv_stored, gating_full, pointwise_full)
    grad_attention = grad_conv + branch_grad
    branch_grad, attend_gain, attend_shift, projection_grad, merger_grad = attention_backward(
        grad_attention, attend_stored, projection_full, merger_full, matching
    )
    grad_first = grad_attention + branch_grad
    branch_grad, first_gain, first_shift, firstup_grad, firstdown_grad = feed_backward(
        0.5 * grad_first, first_stored, firstup_full, firstdown_full
    )
    frames_grad = grad_first + branch_grad
    table_grad = lax.dot_general(
        language_hot, frames_grad, (((0,), (0,)), ((), ())), precision=lax.Precision.HIGHEST
    )
    gain_stack = jnp.stack(
        [first_gain, attend_gain, outer_gain, inner_gain, second_gain, final_gain]
    )
    shift_stack = jnp.stack(
        [first_shift, attend_shift, outer_shift, inner_shift, second_shift, final_shift]
    )
    table_sum, gain_sum, shift_sum, taps_sum = sum_small(
        place, sizes, [table_grad, gain_stack, shift_stack, taps_grad]
    )
    (seconddown_sum,) = weight_grads(place, sizes, [seconddown_grad], False)
    (secondup_sum,) = weight_grads(place, sizes, [secondup_grad], True)
    pointwise_sum, gating_sum = weight_grads(place, sizes, [pointwise_grad, gating_grad], False)
    merger_sum, projection_sum = weight_grads(place, sizes, [merger_grad, projection_grad], True)
    (firstdown_sum,) = weight_grads(place, sizes, [firstdown_grad], False)
    (firstup_sum,) = weight_grads(place, sizes, [firstup_grad], True)
    return (
        encoded.astype(jnp.bfloat16),
        frames_grad,
        table_sum,
        gain_sum,
        shift_sum,
        firstup_sum,
        firstdown_sum,
        projection_sum,
        merger_sum,
        gating_sum,
        taps_sum,
        pointwise_sum,
        secondup_sum,
        seconddown_sum,
    )


def solution(mesh):
    dp_size, fsdp_size = mesh.shape["dp"], mesh.shape["fsdp"]
    layers = fsdp_size // 2
    split = Mesh(mesh.devices.reshape(dp_size, layers, 2), ("dp", "z", "core"))
    return jax.shard_map(
        functools.partial(shards, (dp_size, layers)),
        mesh=split,
        in_specs=(
            P(("dp", "z", "core"), None),
            P(("dp", "z", "core"), None),
            P(("dp", "z", "core"), None),
            P(None, ("z", "core")),
            P(None, ("z", "core")),
            P(None, ("z", "core")),
            P(("z", "core"), None),
            P(("z", "core"), None),
            P(("z", "core"), None),
            P(("z", "core"), None),
            P(("z", "core"), None),
            P(None, ("z", "core")),
            P(("z", "core"), None),
            P(("z", "core"), None),
            P(("z", "core"), None),
            P(("dp", "z", "core"), None),
        ),
        out_specs=(
            P(("dp", "z", "core"), None),
            P(("dp", "z", "core"), None),
            P(None, ("z", "core")),
            P(None, ("z", "core")),
            P(None, ("z", "core")),
            P(("z", "core"), None),
            P(("z", "core"), None),
            P(("z", "core"), None),
            P(("z", "core"), None),
            P(("z", "core"), None),
            P(None, ("z", "core")),
            P(("z", "core"), None),
            P(("z", "core"), None),
            P(("z", "core"), None),
        ),
        check_vma=False,
    )
```

```python
import functools

import jax
import jax.numpy as jnp
import numpy as np
from jax import lax
from jax.experimental import pallas as pl
from jax.experimental.pallas import tpu as pltpu
from jax.sharding import Mesh
from jax.sharding import PartitionSpec as P

HEAD_DIM = 128


def layout(lengths, languages, frame_count):
    utterances = jnp.arange(lengths.shape[-1], dtype=jnp.int32)
    earlier = utterances[:, None] <= utterances[None, :]
    finish = jnp.sum(jnp.where(earlier[None], lengths[:, :, None], 0), axis=1)
    begins = finish - lengths
    indices = jnp.arange(frame_count, dtype=jnp.int32)
    segment = jnp.sum((indices[None, :, None] >= finish[:, None, :]).astype(jnp.int32), axis=-1)
    owners = segment[:, :, None] == jnp.arange(lengths.shape[-1], dtype=jnp.int32)[None, None, :]
    first_row = jnp.sum(jnp.where(owners, begins[:, None, :], 0), axis=-1)
    language_row = jnp.sum(jnp.where(owners, languages[:, None, :], 0), axis=-1)
    return (segment, indices[None, :] - first_row, language_row)


def angles(position):
    half_dim = HEAD_DIM // 2
    frequency = 10000.0 ** (-jnp.arange(half_dim, dtype=jnp.float32) / half_dim)
    turned = position.astype(jnp.float32)[..., None] * frequency
    return (jnp.cos(turned)[..., None, :], jnp.sin(turned)[..., None, :])


VMEM_SPACE = pl.BlockSpec(memory_space=pltpu.VMEM)
SMEM_SPACE = pl.BlockSpec(memory_space=pltpu.SMEM)
ANY_SPACE = pl.BlockSpec(memory_space=pl.ANY)


class Order:
    def __init__(self, value):
        self.value = value

    def call(self, kernel, out_shape, in_specs, out_specs, scratch_shapes, operands, after=(), micros=8.0):
        count, outs, extra = len(operands), len(out_shape), len(after)
        held_in = [i for i in range(count) if in_specs[i] is VMEM_SPACE]
        held_out = [i for i in range(outs) if out_specs[i] is VMEM_SPACE]
        buffers = [pltpu.VMEM(operands[i].shape, operands[i].dtype) for i in held_in]
        buffers += [pltpu.VMEM(out_shape[i].shape, out_shape[i].dtype) for i in held_out]
        copies = max(1, len(held_in), len(held_out))
        needed = sum(
            int(np.prod(b.shape)) * np.dtype(b.dtype).itemsize
            for b in [*buffers, *scratch_shapes]
            if b.memory_space == pltpu.VMEM
        )

        def body(*refs):
            ins, rest = list(refs[:count]), refs[count + extra + 1 :]
            results, rest = list(rest[:outs]), rest[outs + 1 :]
            held, scratch, sems = rest[: len(buffers)], rest[len(buffers) : -1], rest[-1]
            moves = []
            for at, i in enumerate(held_in):
                moves.append(pltpu.make_async_copy(ins[i], held[at], sems.at[at]))
                moves[-1].start()
                ins[i] = held[at]
            targets = []
            for at, i in enumerate(held_out):
                targets.append(results[i])
                results[i] = held[len(held_in) + at]
            for move in moves:
                move.wait()
            kernel(*ins, *results, *scratch)
            moves = []
            for at, i in enumerate(held_out):
                moves.append(pltpu.make_async_copy(results[i], targets[at], sems.at[at]))
                moves[-1].start()
            for move in moves:
                move.wait()

        result = pl.pallas_call(
            body,
            out_shape=[*out_shape, jax.ShapeDtypeStruct(self.value.shape, self.value.dtype)],
            in_specs=[ANY_SPACE if s is VMEM_SPACE else s for s in in_specs]
            + [ANY_SPACE] * (extra + 1),
            out_specs=[ANY_SPACE] * (outs + 1),
            scratch_shapes=[*buffers, *scratch_shapes, pltpu.SemaphoreType.DMA((copies,))],
            input_output_aliases={count + extra: outs},
            compiler_params=pltpu.CompilerParams(vmem_limit_bytes=min(VMEM_LIMIT, needed + VMEM_SPARE)),
            cost_estimate=pl.CostEstimate(
                flops=1, bytes_accessed=int(micros * COST_SCALE), transcendentals=0
            ),
        )(*operands, *after, self.value)
        self.value = result[-1]
        return result[:-1]


COST_SCALE = 3.0e5
VMEM_LIMIT = 60 * 1024 * 1024
VMEM_SPARE = 16 * 1024 * 1024
QUARTERS = 4
LANES = 128
BITS = (0, 1)


def swap_dp(value, bit, size):
    return lax.ppermute(value, "dp", [(i, i ^ (1 << bit)) for i in range(size)])


def swap_core(value):
    return lax.ppermute(value, "core", [(0, 1), (1, 0)])


def last_bit(index, order):
    return [bit for bit in order if index >> bit & 1][-1]


def pick_kernel(layers, place, gathered, out, sems):
    layer, core = place[1], place[2]
    copies = []
    for k in range(1, layers):
        row = lax.rem(layer + k, layers) * 2 + core
        copies.append(pltpu.make_async_copy(gathered.at[row], out.at[k - 1], sems.at[k - 1]))
        copies[-1].start()
    for copy in copies:
        copy.wait()


def pick(order, place, layers, gathered, after):
    _, rows, width = gathered.shape
    return order.call(
        functools.partial(pick_kernel, layers),
        [jax.ShapeDtypeStruct((layers - 1, rows, width), gathered.dtype)],
        [SMEM_SPACE, ANY_SPACE],
        [VMEM_SPACE],
        [pltpu.SemaphoreType.DMA((layers - 1,))],
        [place, gathered],
        after,
        3.0,
    )[0]


class Factors:
    def __init__(self, left, right):
        self.rights = list(right) if isinstance(right, (list, tuple)) else [right]
        self.split = len(self.rights) > 1
        self.width = sum(r.shape[1] for r in self.rights)
        self.tokens = left.shape[0]
        self.operands = [left, swap_core(left)]
        self.rest = [*self.rights, *[swap_core(r) for r in self.rights]]

    def columns(self, refs, quarter, r, start, tile):
        part = self.width // QUARTERS
        count = len(self.rights)
        if self.split:
            column = pl.ds(start, tile)
            return [refs[r].at[:, column], refs[count + r].at[:, column]]
        column = pl.ds(pl.multiple_of((quarter ^ r) * part + start, tile), tile)
        return [refs[0].at[:, column], refs[1].at[:, column]]


def own_rows(ref, layers, core):
    tokens, features = ref.shape
    rows = features // (2 * layers)
    if rows % LANES == 0:
        blocks = [
            ref[:, pl.ds(pl.multiple_of((2 * k + core) * rows, rows), rows)] for k in range(layers)
        ]
        return jnp.concatenate(blocks, axis=1).T
    turned = ref[...].T.reshape(layers, 2, rows, tokens)
    return jnp.where(core == 0, turned[:, 0], turned[:, 1]).reshape(layers * rows, tokens)


def weight_terms_kernel(layers, factors, tile, wanted, given, place, *refs):
    lefts, at = [], 0
    for f in factors:
        lefts.append(refs[at : at + 2])
        at += 2
    rights = []
    for f in factors:
        rights.append(refs[at : at + len(f.rest)])
        at += len(f.rest)
    sums = []
    for holds in given:
        sums.append(dict(zip(holds, refs[at : at + len(holds)])))
        at += len(holds)
    outs, buffers = refs[at : at + len(wanted)], refs[at + len(wanted) :]
    right_buffer, add_buffer, out_buffer, in_sems, out_sems = buffers
    quarter, core = place[0], place[2]
    jobs, base = [], 0
    for i, f in enumerate(factors):
        part = f.width // QUARTERS
        for number, r in enumerate(wanted):
            for start in range(0, part, tile):
                narrow = pl.ds(base + start, tile)
                jobs.append(
                    (
                        i,
                        f.columns(rights[i], quarter, r, start, tile),
                        [held[r].at[:, narrow] for held in sums if r in held],
                        outs[number].at[:, narrow],
                    )
                )
        base += part
    loads = []
    for number, (i, columns, adds, _) in enumerate(jobs):
        tokens = factors[i].tokens
        moves = [
            (column, right_buffer.at[number, k * tokens : (k + 1) * tokens])
            for k, column in enumerate(columns)
        ]
        moves += [(ref, add_buffer.at[number, k]) for k, ref in enumerate(adds)]
        started = []
        for k, (source, target) in enumerate(moves):
            started.append(pltpu.make_async_copy(source, target, in_sems.at[number, k]))
            started[-1].start()
        loads.append(started)
    stores = []
    for number, (i, _, adds, target) in enumerate(jobs):
        tokens = factors[i].tokens
        if number == 0 or jobs[number - 1][0] != i:
            left = jnp.concatenate([own_rows(ref, layers, core) for ref in lefts[i]], axis=1)
        for copy in loads[number]:
            copy.wait()
        product = jnp.dot(
            left, right_buffer[number, : 2 * tokens], preferred_element_type=jnp.float32
        )
        for k in range(len(adds)):
            product += add_buffer[number, k].astype(jnp.float32)
        out_buffer[number] = product.astype(jnp.bfloat16)
        copy = pltpu.make_async_copy(out_buffer.at[number], target, out_sems.at[number])
        copy.start()
        stores.append(copy)
    for copy in stores:
        copy.wait()


def weight_terms(order, place, layers, factors, wanted, sums, given):
    height = factors[0].operands[0].shape[1] // 2
    tokens = 2 * max(f.tokens for f in factors)
    tile = int(np.gcd.reduce([512] + [f.width // QUARTERS for f in factors]))
    width = sum(f.width for f in factors) // QUARTERS
    count = len(wanted) * width // tile
    depth = max(1, len(sums))
    lefts = [o for f in factors for o in f.operands]
    rest = [o for f in factors for o in f.rest] + [a for each in sums for a in each]
    return order.call(
        functools.partial(weight_terms_kernel, layers, factors, tile, wanted, given),
        [jax.ShapeDtypeStruct((height, width), jnp.bfloat16)] * len(wanted),
        [SMEM_SPACE] + [VMEM_SPACE] * len(lefts) + [ANY_SPACE] * len(rest),
        [ANY_SPACE] * len(wanted),
        [
            pltpu.VMEM((count, tokens, tile), jnp.bfloat16),
            pltpu.VMEM((count if sums else 1, depth, height, tile), jnp.bfloat16),
            pltpu.VMEM((count, height, tile), jnp.bfloat16),
            pltpu.SemaphoreType.DMA((count, depth + 2)),
            pltpu.SemaphoreType.DMA((count,)),
        ],
        [place, *lefts, *rest],
        (),
        5.0,
    )


def spread_kernel(widths, place, *refs):
    pieces, outs = refs[:QUARTERS], refs[QUARTERS:]
    quarter = place[0]
    base = 0
    for i, width in enumerate(widths):
        part = width // QUARTERS
        for r in range(QUARTERS):
            column = pl.ds(pl.multiple_of((quarter ^ r) * part, part), part)
            outs[i][:, column] = pieces[r][:, pl.ds(base, part)].astype(jnp.float32)
        base += part


def spread(order, place, widths, pieces):
    rows = pieces[0].shape[0]
    return order.call(
        functools.partial(spread_kernel, widths),
        [jax.ShapeDtypeStruct((rows, w), jnp.float32) for w in widths],
        [SMEM_SPACE] + [VMEM_SPACE] * QUARTERS,
        [VMEM_SPACE] * len(widths),
        [],
        [place, *pieces],
        (),
        3.0,
    )


class Gather:
    def __init__(self, place, sizes, order, group):
        self.place, self.order, self.group = place, order, group
        self.dp_size, self.layers = sizes
        self.other = [swap_core(w) for w in group]

    def begin(self):
        quarter = self.place[0]
        mine = jnp.concatenate(
            [
                lax.dynamic_slice_in_dim(w, quarter * (w.shape[1] // QUARTERS), w.shape[1] // QUARTERS, 1)
                for w in self.group
            ],
            axis=1,
        )
        self.gathered = lax.all_gather(mine, ("z", "core"), axis=0, tiled=False)

    def exchange(self, flip, after=()):
        held = {0: pick(self.order, self.place, self.layers, self.gathered, after)}
        order = BITS[::-1] if flip else BITS
        for r in range(1, QUARTERS):
            bit = last_bit(r, order)
            held[r] = swap_dp(held[r ^ (1 << bit)], bit, self.dp_size)
        self.pieces = [held[r] for r in range(1, QUARTERS)]
        self.others = [swap_core(piece) for piece in self.pieces]


class Scatter:
    def __init__(self, place, sizes, order, flip):
        self.place, self.order = place, order
        self.dp_size, self.layers = sizes
        self.first, self.second = BITS[::-1] if flip else BITS

    def terms(self, wanted, sums, given):
        return weight_terms(self.order, self.place, self.layers, self.factors, wanted, sums, given)

    def halves(self, *factors):
        self.factors = factors
        self.widths = [f.width for f in factors]
        sent = [r for r in range(QUARTERS) if r >> self.first & 1]
        self.held = [r ^ (1 << self.first) for r in sent]
        away = self.terms(sent, (), ())
        self.sums = [swap_dp(part, self.first, self.dp_size) for part in away]

    def quarters(self):
        (part,) = self.terms([1 << self.second], (self.sums,), (self.held,))
        self.last = swap_dp(part, self.second, self.dp_size)

    def rows(self):
        (own,) = self.terms([0], (self.sums, [self.last]), (self.held, [0]))
        self.mine = lax.psum_scatter(own, "z", scatter_dimension=0, tiled=True)

    def share(self):
        summed = self.mine
        bit = len(BITS)
        while 1 << bit < self.dp_size:
            summed = summed + swap_dp(summed, bit, self.dp_size)
            bit += 1
        held = {0: summed}
        for r in range(1, QUARTERS):
            bit = last_bit(r, (self.first, self.second))
            held[r] = swap_dp(held[r ^ (1 << bit)], bit, self.dp_size)
        self.pieces = [held[r] for r in range(QUARTERS)]

    def spread(self):
        return spread(self.order, self.place, self.widths, self.pieces)


def gather_small(arrays):
    rows = [a.shape[0] for a in arrays]
    packed = jnp.concatenate(arrays, axis=0)
    packed = jnp.pad(packed, ((0, -packed.shape[0] % 16), (0, 0)))
    full = lax.all_gather(packed, ("z", "core"), axis=0, tiled=False)
    full = full.transpose(1, 0, 2).reshape(packed.shape[0], -1)
    pieces, start = [], 0
    for count in rows:
        pieces.append(full[start : start + count])
        start += count
    return pieces


def pack_small(table_hot, frames_grad, vectors):
    count = table_hot.shape[1]
    extra = -(frames_grad.shape[0] + vectors.shape[0]) % 16
    left = jnp.concatenate([frames_grad, vectors, jnp.zeros((extra, vectors.shape[1]), vectors.dtype)])
    used = count + vectors.shape[0]
    share = -(-used // QUARTERS)
    unit = jnp.eye(vectors.shape[0], dtype=table_hot.dtype)
    right = jnp.block(
        [
            [table_hot, jnp.zeros((table_hot.shape[0], vectors.shape[0]), table_hot.dtype)],
            [jnp.zeros((vectors.shape[0], count), table_hot.dtype), unit],
        ]
    )
    right = jnp.pad(right, ((0, extra), (0, share * QUARTERS - used)))
    right = right.reshape(right.shape[0], QUARTERS, share)
    right = jnp.pad(right, ((0, 0), (0, 0), (0, LANES - share)))
    return (
        left.astype(jnp.bfloat16),
        right.reshape(right.shape[0], QUARTERS * LANES).astype(jnp.bfloat16),
    )


def unpack_small(summed, counts):
    used = sum(counts)
    share = -(-used // QUARTERS)
    rows = summed.reshape(summed.shape[0], QUARTERS, LANES)[:, :, :share]
    rows = rows.reshape(summed.shape[0], QUARTERS * share).T
    pieces, start = [], 0
    for count in counts:
        pieces.append(rows[start : start + count])
        start += count
    return pieces

EPSILON = 1e-05
MASKED = -1000000000.0


def dot_rows(left, right):
    return jnp.dot(left, right, preferred_element_type=jnp.float32)


def dot_cols(left, right):
    return lax.dot_general(
        left, right, (((1,), (1,)), ((), ())), preferred_element_type=jnp.float32
    )


def dot_down(left, right):
    return jnp.dot(left.T, right, preferred_element_type=jnp.float32)


def standard(values):
    centred = values - jnp.mean(values, axis=-1, keepdims=True)
    spread = lax.rsqrt(jnp.mean(centred * centred, axis=-1, keepdims=True) + EPSILON)
    return centred * spread, spread


def norm_back(values, gradient, gain):
    shape, spread = standard(values)
    inner = gradient * gain
    back = spread * (
        inner
        - jnp.mean(inner, axis=-1, keepdims=True)
        - shape * jnp.mean(inner * shape, axis=-1, keepdims=True)
    )
    return (
        back,
        jnp.sum(gradient * shape, axis=0, keepdims=True),
        jnp.sum(gradient, axis=0, keepdims=True),
    )


def sigmoid(values):
    return 1.0 / (1.0 + jnp.exp(-values))


def silu_back(values, gradient):
    gate = sigmoid(values)
    return gradient * gate * (1.0 + values * (1.0 - gate))


class Pieces:
    def __init__(self, gather, index):
        group = gather.group
        self.layers = gather.layers
        self.base = sum(w.shape[1] for w in group[:index]) // QUARTERS
        self.rows, self.width = group[index].shape
        self.operands = [
            group[index],
            gather.other[index],
            gather.gathered,
            *gather.pieces,
            *gather.others,
        ]

    @property
    def part(self):
        return self.width // QUARTERS

    def quarters(self, tokens):
        return [jax.ShapeDtypeStruct((tokens, self.part), jnp.bfloat16)] * QUARTERS

    @property
    def scratch(self):
        copies = 1 + (QUARTERS - 1) * 2 * self.layers
        return [
            pltpu.VMEM((QUARTERS, 2 * self.layers, self.rows, self.part), jnp.bfloat16),
            pltpu.SemaphoreType.DMA((copies,)),
        ]

    def load(self, place, refs, buffer, sems):
        own, other, gathered = refs[:3]
        pieces, others = refs[3 : 2 + QUARTERS], refs[2 + QUARTERS :]
        quarter, layer, core = place[0], place[1], place[2]
        span = pl.ds(self.base, self.part)
        number, steps = 0, []
        for r in range(QUARTERS):
            index = quarter ^ r
            column = pl.ds(pl.multiple_of(index * self.part, self.part), self.part)
            moves = []
            if r == 0:
                moves.append((gathered.at[:, :, span], buffer.at[index]))
            else:
                for source, lane in ((own, core), (other, 1 - core)):
                    moves.append((source.at[:, column], buffer.at[index, 2 * layer + lane]))
                for source, lane in ((pieces[r - 1], core), (others[r - 1], 1 - core)):
                    for k in range(1, self.layers):
                        row = lax.rem(layer + k, self.layers) * 2 + lane
                        moves.append((source.at[k - 1, :, span], buffer.at[index, row]))
            copies = []
            for source, target in moves:
                copies.append(pltpu.make_async_copy(source, target, sems.at[number]))
                copies[-1].start()
                number += 1
            steps.append((index, copies))
        return steps

    def block(self, buffer, index):
        return buffer[index].reshape(2 * self.layers * self.rows, self.part)


def wait_all(steps):
    for _, copies in steps:
        for copy in copies:
            copy.wait()


def up_kernel(pieces, row, place, values, gains, shifts, *refs):
    weight, outs, (buffer, sems) = refs[: -4 - QUARTERS], refs[-4 - QUARTERS : -2], refs[-2:]
    hidden_out, expanded_out, active_outs = outs[0], outs[1], outs[2:]
    steps = pieces.load(place, weight, buffer, sems)
    shape, _ = standard(values[...])
    hidden = (shape * gains[row : row + 1] + shifts[row : row + 1]).astype(jnp.bfloat16)
    hidden_out[...] = hidden
    for r, (index, copies) in enumerate(steps):
        for copy in copies:
            copy.wait()
        expanded = dot_rows(hidden, pieces.block(buffer, index))
        expanded_out[r] = expanded
        active_outs[r][...] = (expanded * sigmoid(expanded)).astype(jnp.bfloat16)


def up_step(order, place, gather, index, row, values, gains, shifts):
    pieces = Pieces(gather, index)
    tokens, width = values.shape
    return order.call(
        functools.partial(up_kernel, pieces, row),
        [
            jax.ShapeDtypeStruct((tokens, width), jnp.bfloat16),
            jax.ShapeDtypeStruct((QUARTERS, tokens, pieces.part), jnp.float32),
            *pieces.quarters(tokens),
        ],
        [SMEM_SPACE] + [VMEM_SPACE] * 3 + [ANY_SPACE] * len(pieces.operands),
        [VMEM_SPACE] * (2 + QUARTERS),
        pieces.scratch,
        [place, values, gains, shifts, *pieces.operands],
    )


def down_sum(pieces, place, quarters, weight, buffer, sems):
    total = None
    for r, (index, copies) in enumerate(pieces.load(place, weight, buffer, sems)):
        for copy in copies:
            copy.wait()
        term = dot_cols(quarters[r][...], pieces.block(buffer, index))
        total = term if total is None else total + term
    return total


def down_kernel(pieces, place, values, *refs):
    active, weight, (out, buffer, sems) = refs[:QUARTERS], refs[QUARTERS:-3], refs[-3:]
    out[...] = values[...] + 0.5 * down_sum(pieces, place, active, weight, buffer, sems)


def down_step(order, place, gather, index, values, active):
    pieces = Pieces(gather, index)
    return order.call(
        functools.partial(down_kernel, pieces),
        [jax.ShapeDtypeStruct(values.shape, jnp.float32)],
        [SMEM_SPACE] + [VMEM_SPACE] * (1 + QUARTERS) + [ANY_SPACE] * len(pieces.operands),
        [VMEM_SPACE],
        pieces.scratch,
        [place, values, *active, *pieces.operands],
    )[0]


def last_kernel(pieces, row, place, values, cotangent, gains, shifts, *refs):
    active, weight, outs = refs[:QUARTERS], refs[QUARTERS:-7], refs[-7:]
    encoded, grad_out, low_out, gain_out, shift_out, buffer, sems = outs
    total = values[...] + 0.5 * down_sum(pieces, place, active, weight, buffer, sems)
    gain = gains[row : row + 1]
    shape, _ = standard(total)
    encoded[...] = (shape * gain + shifts[row : row + 1]).astype(jnp.bfloat16)
    back, gain_grad, shift_grad = norm_back(total, cotangent[...].astype(jnp.float32), gain)
    grad_out[...] = back
    low_out[...] = (0.5 * back).astype(jnp.bfloat16)
    gain_out[...] = gain_grad
    shift_out[...] = shift_grad


def vector_shapes(width, count=2):
    return [jax.ShapeDtypeStruct((1, width), jnp.float32)] * count


def last_step(order, place, gather, index, row, values, active, cotangent, gains, shifts):
    pieces = Pieces(gather, index)
    return order.call(
        functools.partial(last_kernel, pieces, row),
        [
            jax.ShapeDtypeStruct(values.shape, jnp.bfloat16),
            jax.ShapeDtypeStruct(values.shape, jnp.float32),
            jax.ShapeDtypeStruct(values.shape, jnp.bfloat16),
            *vector_shapes(values.shape[1]),
        ],
        [SMEM_SPACE] + [VMEM_SPACE] * (4 + QUARTERS) + [ANY_SPACE] * len(pieces.operands),
        [VMEM_SPACE] * 5,
        pieces.scratch,
        [place, values, cotangent, gains, shifts, *active, *pieces.operands],
    )


def down_back_kernel(pieces, place, gradient, expanded, *refs):
    weight, outs, (buffer, sems) = refs[: -2 - QUARTERS], refs[-2 - QUARTERS : -2], refs[-2:]
    for r, (index, copies) in enumerate(pieces.load(place, weight, buffer, sems)):
        for copy in copies:
            copy.wait()
        active_grad = dot_rows(gradient[...], pieces.block(buffer, index))
        outs[r][...] = silu_back(expanded[r], active_grad).astype(jnp.bfloat16)


def down_back_step(order, place, gather, index, gradient, expanded):
    pieces = Pieces(gather, index)
    return order.call(
        functools.partial(down_back_kernel, pieces),
        pieces.quarters(gradient.shape[0]),
        [SMEM_SPACE] + [VMEM_SPACE] * 2 + [ANY_SPACE] * len(pieces.operands),
        [VMEM_SPACE] * QUARTERS,
        pieces.scratch,
        [place, gradient, expanded, *pieces.operands],
    )


def into_norm_kernel(pieces, row, scale, place, values, residual, gains, *refs):
    gradient, refs = refs[:QUARTERS], refs[QUARTERS:]
    weight, (grad_out, low_out, gain_out, shift_out, buffer, sems) = refs[:-6], refs[-6:]
    hidden_grad = down_sum(pieces, place, gradient, weight, buffer, sems)
    back, gain_grad, shift_grad = norm_back(values[...], hidden_grad, gains[row : row + 1])
    total = residual[...] + back
    grad_out[...] = total
    low_out[...] = (scale * total).astype(jnp.bfloat16)
    gain_out[...] = gain_grad
    shift_out[...] = shift_grad


def into_norm_step(order, place, gather, index, row, scale, gradient, values, residual, gains):
    pieces = Pieces(gather, index)
    return order.call(
        functools.partial(into_norm_kernel, pieces, row, scale),
        [
            jax.ShapeDtypeStruct(values.shape, jnp.float32),
            jax.ShapeDtypeStruct(values.shape, jnp.bfloat16),
            *vector_shapes(values.shape[1]),
        ],
        [SMEM_SPACE] + [VMEM_SPACE] * (3 + QUARTERS) + [ANY_SPACE] * len(pieces.operands),
        [VMEM_SPACE] * 4,
        pieces.scratch,
        [place, values, residual, gains, *gradient, *pieces.operands],
    )


def whole_weight(pieces, place, weight, buffer, sems):
    wait_all(pieces.load(place, weight, buffer, sems))


def turn(values, cosine, sine):
    return values * cosine + pltpu.roll(values, HEAD_DIM // 2, 1) * sine


def masked_scores(query, key, matching):
    return jnp.where(matching, dot_cols(query, key), MASKED)


def head(index):
    return slice(index * HEAD_DIM, (index + 1) * HEAD_DIM)


def attend_kernel(pieces, row, place, values, gains, shifts, cosine, sine, down, across, *refs):
    weight, outs = refs[:-7], refs[-7:]
    hidden_out, turned_out, totals_out, mixed_out, projected, buffer, sems = outs
    steps = pieces.load(place, weight, buffer, sems)
    shape, _ = standard(values[...])
    hidden = (shape * gains[row : row + 1] + shifts[row : row + 1]).astype(jnp.bfloat16)
    hidden_out[...] = hidden
    for index, copies in steps:
        for copy in copies:
            copy.wait()
        column = pl.ds(pl.multiple_of(index * pieces.part, pieces.part), pieces.part)
        projected[:, column] = dot_rows(hidden, pieces.block(buffer, index))
    heads = pieces.width // (3 * HEAD_DIM)
    matching = down[...] == across[...]
    for h in range(heads):
        query = turn(projected[:, head(h)], cosine[...], sine[...]) * HEAD_DIM ** (-0.5)
        key = turn(projected[:, head(heads + h)], cosine[...], sine[...])
        query, key = query.astype(jnp.bfloat16), key.astype(jnp.bfloat16)
        value = projected[:, head(2 * heads + h)].astype(jnp.bfloat16)
        turned_out[:, head(h)] = query
        turned_out[:, head(heads + h)] = key
        turned_out[:, head(2 * heads + h)] = value
        scores = masked_scores(query, key, matching)
        highest = jnp.max(scores, axis=-1, keepdims=True)
        powers = jnp.exp(scores - highest)
        total = jnp.sum(powers, axis=-1, keepdims=True)
        totals_out[:, h : h + 1] = highest + jnp.log(total)
        probs = (powers / total).astype(jnp.bfloat16)
        mixed_out[:, head(h)] = dot_rows(probs, value).astype(jnp.bfloat16)


def attend_step(order, place, gather, index, row, values, gains, shifts, cosine, sine, down, across):
    pieces = Pieces(gather, index)
    tokens, width = values.shape
    heads = pieces.width // (3 * HEAD_DIM)
    return order.call(
        functools.partial(attend_kernel, pieces, row),
        [
            jax.ShapeDtypeStruct((tokens, width), jnp.bfloat16),
            jax.ShapeDtypeStruct((tokens, pieces.width), jnp.bfloat16),
            jax.ShapeDtypeStruct((tokens, heads), jnp.float32),
            jax.ShapeDtypeStruct((tokens, heads * HEAD_DIM), jnp.bfloat16),
        ],
        [SMEM_SPACE] + [VMEM_SPACE] * 7 + [ANY_SPACE] * len(pieces.operands),
        [VMEM_SPACE] * 4,
        [pltpu.VMEM((tokens, pieces.width), jnp.float32), *pieces.scratch],
        [place, values, gains, shifts, cosine, sine, down, across, *pieces.operands],
    )


def quarter_shapes(shape):
    return [jax.ShapeDtypeStruct((shape[0], shape[1] // QUARTERS), jnp.bfloat16)] * QUARTERS


def to_quarters(place, values, outs):
    part = values.shape[1] // QUARTERS
    for r, out in enumerate(outs):
        out[...] = values[:, pl.ds(pl.multiple_of((place[0] ^ r) * part, part), part)]


def attend_back_kernel(pieces, place, gradient, turned, totals, cosine, sine, down, across, *refs):
    weight, rest = refs[: -4 - QUARTERS], refs[-4 - QUARTERS :]
    outs, (out, mixed_grad, buffer, sems) = rest[:QUARTERS], rest[QUARTERS:]
    heads = turned.shape[1] // (3 * HEAD_DIM)
    whole_weight(pieces, place, weight, buffer, sems)
    total = None
    for index in range(QUARTERS):
        column = slice(index * pieces.part, (index + 1) * pieces.part)
        term = dot_cols(gradient[:, column], pieces.block(buffer, index))
        total = term if total is None else total + term
    mixed_grad[...] = total.astype(jnp.bfloat16)
    matching = down[...] == across[...]
    for h in range(heads):
        query = turned[:, head(h)]
        key = turned[:, head(heads + h)]
        value = turned[:, head(2 * heads + h)]
        gradient_h = mixed_grad[:, head(h)]
        probs = jnp.exp(masked_scores(query, key, matching) - totals[:, h : h + 1])
        value_grad = dot_down(probs.astype(jnp.bfloat16), gradient_h)
        probs_grad = dot_cols(gradient_h, value)
        inner = jnp.sum(probs * probs_grad, axis=-1, keepdims=True)
        score_grad = (probs * (probs_grad - inner)).astype(jnp.bfloat16)
        query_grad = dot_rows(score_grad, key) * HEAD_DIM ** (-0.5)
        key_grad = dot_down(score_grad, query)
        out[:, head(h)] = turn(query_grad, cosine[...], -sine[...]).astype(jnp.bfloat16)
        out[:, head(heads + h)] = turn(key_grad, cosine[...], -sine[...]).astype(jnp.bfloat16)
        out[:, head(2 * heads + h)] = value_grad.astype(jnp.bfloat16)
    to_quarters(place, out, outs)


def attend_back_step(order, place, gather, index, gradient, turned, totals, cosine, sine, down, across):
    pieces = Pieces(gather, index)
    return order.call(
        functools.partial(attend_back_kernel, pieces),
        quarter_shapes(turned.shape),
        [SMEM_SPACE] + [VMEM_SPACE] * 7 + [ANY_SPACE] * len(pieces.operands),
        [VMEM_SPACE] * QUARTERS,
        [
            pltpu.VMEM(turned.shape, jnp.bfloat16),
            pltpu.VMEM(gradient.shape, jnp.bfloat16),
            *pieces.scratch,
        ],
        [place, gradient, turned, totals, cosine, sine, down, across, *pieces.operands],
    )


def rows_sum(pieces, buffer, left, out):
    for index in range(QUARTERS):
        column = slice(index * pieces.part, (index + 1) * pieces.part)
        out[:, column] = dot_rows(left, pieces.block(buffer, index))


def shifted(values, amount):
    return values if amount == 0 else pltpu.roll(values, amount % values.shape[0], 0)


def merge_kernel(pieces, place, values, mixed, *refs):
    weight, (out, buffer, sems) = refs[:-3], refs[-3:]
    whole_weight(pieces, place, weight, buffer, sems)
    for index in range(QUARTERS):
        column = slice(index * pieces.part, (index + 1) * pieces.part)
        out[:, column] = values[:, column] + dot_rows(mixed[...], pieces.block(buffer, index))


def merge_step(order, place, gather, index, values, mixed):
    pieces = Pieces(gather, index)
    return order.call(
        functools.partial(merge_kernel, pieces),
        [jax.ShapeDtypeStruct(values.shape, jnp.float32)],
        [SMEM_SPACE] + [VMEM_SPACE] * 2 + [ANY_SPACE] * len(pieces.operands),
        [VMEM_SPACE],
        pieces.scratch,
        [place, values, mixed, *pieces.operands],
    )[0]


def conv_kernel(weights, row, place, values, gains, shifts, taps, keep, *refs):
    count = len(weights[0].operands)
    operands = [refs[i * count : (i + 1) * count] for i in range(len(weights))]
    rest = refs[len(weights) * count :]
    done_out, hidden_out, doubled_out, filtered_out, active_out = rest[:5]
    scratch = rest[5:]
    buffers = [scratch[2 * i : 2 * i + 2] for i in range(len(weights))]
    steps = [w.load(place, o, *b) for w, o, b in zip(weights, operands, buffers)]
    gating, pointwise = weights
    shape, _ = standard(values[...])
    hidden = (shape * gains[row : row + 1] + shifts[row : row + 1]).astype(jnp.bfloat16)
    hidden_out[...] = hidden
    wait_all(steps[0])
    rows_sum(gating, buffers[0][0], hidden, doubled_out)
    half = gating.width // 2
    gated = doubled_out[:, :half] * sigmoid(doubled_out[:, half:])
    reach = taps.shape[0] // 2
    filtered = None
    for k in range(taps.shape[0]):
        term = shifted(gated, reach - k) * keep[:, k : k + 1] * taps[k : k + 1]
        filtered = term if filtered is None else filtered + term
    filtered_out[...] = filtered
    shape, _ = standard(filtered)
    renormed = shape * gains[row + 1 : row + 2] + shifts[row + 1 : row + 2]
    active = (renormed * sigmoid(renormed)).astype(jnp.bfloat16)
    active_out[...] = active
    wait_all(steps[1])
    for index in range(QUARTERS):
        column = slice(index * pointwise.part, (index + 1) * pointwise.part)
        term = dot_rows(active, pointwise.block(buffers[1][0], index))
        done_out[:, column] = values[:, column] + term


def conv_step(order, place, gather, row, values, gains, shifts, taps, keep):
    weights = [Pieces(gather, i) for i in range(2)]
    tokens, width = values.shape
    operands = [o for w in weights for o in w.operands]
    return order.call(
        functools.partial(conv_kernel, weights, row),
        [
            jax.ShapeDtypeStruct((tokens, width), jnp.float32),
            jax.ShapeDtypeStruct((tokens, width), jnp.bfloat16),
            jax.ShapeDtypeStruct((tokens, weights[0].width), jnp.float32),
            jax.ShapeDtypeStruct((tokens, weights[0].width // 2), jnp.float32),
            jax.ShapeDtypeStruct((tokens, width), jnp.bfloat16),
        ],
        [SMEM_SPACE] + [VMEM_SPACE] * 5 + [ANY_SPACE] * len(operands),
        [VMEM_SPACE] * 5,
        [s for w in weights for s in w.scratch],
        [place, values, gains, shifts, taps, keep, *operands],
    )


def conv_back_kernel(pieces, row, place, gradient, filtered, doubled, gains, shifts, taps, keep, *refs):
    weight, rest = refs[: -6 - QUARTERS], refs[-6 - QUARTERS :]
    outs = rest[:QUARTERS]
    gain_out, shift_out, taps_out, doubled_grad, buffer, sems = rest[QUARTERS:]
    whole_weight(pieces, place, weight, buffer, sems)
    total = None
    for index in range(QUARTERS):
        column = slice(index * pieces.part, (index + 1) * pieces.part)
        term = dot_cols(gradient[:, column], pieces.block(buffer, index))
        total = term if total is None else total + term
    gain = gains[row : row + 1]
    shape, _ = standard(filtered[...])
    renormed = shape * gain + shifts[row : row + 1]
    back, gain_grad, shift_grad = norm_back(filtered[...], silu_back(renormed, total), gain)
    gain_out[...] = gain_grad
    shift_out[...] = shift_grad
    half = doubled.shape[1] // 2
    gate = sigmoid(doubled[:, half:])
    gated = doubled[:, :half] * gate
    reach = taps.shape[0] // 2
    gated_grad = None
    for k in range(taps.shape[0]):
        kept = back * keep[:, k : k + 1]
        taps_out[k : k + 1] = jnp.sum(kept * shifted(gated, reach - k), axis=0, keepdims=True)
        term = shifted(kept, k - reach) * taps[k : k + 1]
        gated_grad = term if gated_grad is None else gated_grad + term
    doubled_grad[:, :half] = (gated_grad * gate).astype(jnp.bfloat16)
    doubled_grad[:, half:] = (gated_grad * gated * (1.0 - gate)).astype(jnp.bfloat16)
    to_quarters(place, doubled_grad, outs)


def conv_back_step(order, place, gather, index, row, gradient, filtered, doubled, gains, shifts, taps, keep):
    pieces = Pieces(gather, index)
    width = filtered.shape[1]
    return order.call(
        functools.partial(conv_back_kernel, pieces, row),
        [
            *quarter_shapes(doubled.shape),
            *vector_shapes(width),
            jax.ShapeDtypeStruct(taps.shape, jnp.float32),
        ],
        [SMEM_SPACE] + [VMEM_SPACE] * 7 + [ANY_SPACE] * len(pieces.operands),
        [VMEM_SPACE] * (3 + QUARTERS),
        [pltpu.VMEM(doubled.shape, jnp.bfloat16), *pieces.scratch],
        [place, gradient, filtered, doubled, gains, shifts, taps, keep, *pieces.operands],
    )


def shards(
    sizes,
    frames,
    lengths,
    languages,
    embedding,
    gains,
    shifts,
    firstup,
    firstdown,
    projection,
    merger,
    gating,
    kernel,
    pointwise,
    secondup,
    seconddown,
    cotangent,
):
    frame_count = frames.shape[0]
    dp_index = lax.axis_index("dp").astype(jnp.int32)
    place = jnp.stack(
        [
            lax.rem(dp_index, jnp.int32(QUARTERS)),
            lax.axis_index("z").astype(jnp.int32),
            lax.axis_index("core").astype(jnp.int32),
        ]
    )
    order = Order(frames)
    gathers = [
        Gather(place, sizes, order, group)
        for group in (
            [firstup],
            [firstdown],
            [projection, merger],
            [gating, pointwise],
            [secondup],
            [seconddown],
        )
    ]
    for gather in gathers:
        gather.begin()
    table_full, gain_full, shift_full, kernel_full = gather_small(
        [embedding, gains, shifts, kernel]
    )
    segment_all, position_all, language_all = layout(lengths, languages, frame_count)
    segment = segment_all[0]
    language_row = language_all[0]
    cosine, sine = angles(position_all[0])
    cosine = jnp.concatenate([cosine, cosine], axis=-1)[:, 0]
    sine = jnp.concatenate([-sine, sine], axis=-1)[:, 0]
    down, across = segment[:, None], segment[None, :]
    gain_rows = gain_full.astype(jnp.float32)
    shift_rows = shift_full.astype(jnp.float32)
    taps = kernel_full.astype(jnp.float32)
    reach = taps.shape[0] // 2
    segment_pad = jnp.pad(segment, (reach, reach), constant_values=-1)
    keep = jnp.stack(
        [segment_pad[k : k + frame_count] == segment for k in range(taps.shape[0])], axis=1
    ).astype(jnp.float32)
    language_hot = (
        language_row[:, None] == jnp.arange(table_full.shape[0], dtype=jnp.int32)[None, :]
    ).astype(jnp.float32)
    start_sum = frames.astype(jnp.float32) + jnp.dot(
        language_hot.astype(jnp.bfloat16), table_full, preferred_element_type=jnp.float32
    )

    for number, gather in enumerate(gathers[:2]):
        gather.exchange(number % 2 == 1)
    first_hidden, first_expanded, *first_active = up_step(
        order, place, gathers[0], 0, 0, start_sum, gain_rows, shift_rows
    )
    gathers[2].exchange(False)
    after_first = down_step(order, place, gathers[1], 0, start_sum, first_active)
    gathers[3].exchange(True)
    attend_hidden, turned, totals, mixed = attend_step(
        order, place, gathers[2], 0, 1, after_first, gain_rows, shift_rows, cosine, sine, down, across
    )
    after_attention = merge_step(order, place, gathers[2], 1, after_first, mixed)
    gathers[4].exchange(False)
    after_conv, conv_hidden, doubled, filtered, conv_active = conv_step(
        order, place, gathers[3], 2, after_attention, gain_rows, shift_rows, taps, keep
    )
    gathers[5].exchange(True)
    second_hidden, second_expanded, *second_active = up_step(
        order, place, gathers[4], 0, 4, after_conv, gain_rows, shift_rows
    )
    encoded, grad_second, low_second, final_gain, final_shift = last_step(
        order, place, gathers[5], 0, 5, after_conv, second_active, cotangent, gain_rows, shift_rows
    )

    def scatter(flip):
        return Scatter(place, sizes, order, flip)

    down_two, up_two, conv, attend, down_one, up_one = (
        scatter(False),
        scatter(True),
        scatter(False),
        scatter(True),
        scatter(False),
        scatter(True),
    )
    down_factors = Factors(low_second, second_active)
    second_grad = down_back_step(order, place, gathers[5], 0, low_second, second_expanded)
    up_factors = Factors(second_hidden, second_grad)
    down_two.halves(down_factors)
    grad_conv, low_conv, second_gain, second_shift = into_norm_step(
        order, place, gathers[4], 0, 4, 1.0, second_grad, after_conv, grad_second, gain_rows
    )
    up_two.halves(up_factors)
    pointwise_factors = Factors(conv_active, low_conv)
    *doubled_grad, inner_gain, inner_shift, taps_grad = conv_back_step(
        order, place, gathers[3], 1, 3, low_conv, filtered, doubled, gain_rows, shift_rows, taps, keep
    )
    gating_factors = Factors(conv_hidden, doubled_grad)
    grad_attention, low_attention, outer_gain, outer_shift = into_norm_step(
        order, place, gathers[3], 0, 2, 1.0, doubled_grad, after_attention, grad_conv, gain_rows
    )
    down_two.quarters()
    conv.halves(gating_factors, pointwise_factors)
    merger_factors = Factors(mixed, low_attention)
    projected_grad = attend_back_step(
        order, place, gathers[2], 1, low_attention, turned, totals, cosine, sine, down, across
    )
    projection_factors = Factors(attend_hidden, projected_grad)
    up_two.quarters()
    grad_first, low_first, attend_gain, attend_shift = into_norm_step(
        order, place, gathers[2], 0, 1, 0.5, projected_grad, after_first, grad_attention, gain_rows
    )
    attend.halves(projection_factors, merger_factors)
    down_factors = Factors(low_first, first_active)
    down_two.rows()
    first_grad = down_back_step(order, place, gathers[1], 0, low_first, first_expanded)
    up_factors = Factors(first_hidden, first_grad)
    conv.quarters()
    down_one.halves(down_factors)
    frames_grad, low_start, first_gain, first_shift = into_norm_step(
        order, place, gathers[0], 0, 0, 1.0, first_grad, start_sum, grad_first, gain_rows
    )
    up_two.rows()
    attend.quarters()
    vectors = jnp.concatenate(
        [
            first_gain,
            attend_gain,
            outer_gain,
            inner_gain,
            second_gain,
            final_gain,
            first_shift,
            attend_shift,
            outer_shift,
            inner_shift,
            second_shift,
            final_shift,
            taps_grad,
        ]
    )
    small_factors = Factors(*pack_small(language_hot, low_start, vectors))
    up_one.halves(up_factors, small_factors)
    conv.rows()
    down_two.share()
    down_one.quarters()
    attend.rows()
    up_two.share()
    up_one.quarters()
    (seconddown_grad,) = down_two.spread()
    conv.share()
    down_one.rows()
    (secondup_grad,) = up_two.spread()
    attend.share()
    up_one.rows()
    gating_grad, pointwise_grad = conv.spread()
    down_one.share()
    projection_grad, merger_grad = attend.spread()
    (firstdown_grad,) = down_one.spread()
    up_one.share()
    firstup_grad, small = up_one.spread()
    counts = [embedding.shape[0], gains.shape[0], shifts.shape[0], kernel.shape[0]]
    table_sum, gain_sum, shift_sum, taps_sum = unpack_small(small, counts)
    return (
        encoded,
        frames_grad,
        table_sum,
        gain_sum,
        shift_sum,
        firstup_grad,
        firstdown_grad,
        projection_grad,
        merger_grad,
        gating_grad,
        taps_sum,
        pointwise_grad,
        secondup_grad,
        seconddown_grad,
    )


def solution(mesh):
    dp_size, fsdp_size = mesh.shape["dp"], mesh.shape["fsdp"]
    layers = fsdp_size // 2
    split = Mesh(mesh.devices.reshape(dp_size, layers, 2), ("dp", "z", "core"))
    return jax.shard_map(
        functools.partial(shards, (dp_size, layers)),
        mesh=split,
        in_specs=(
            P(("dp", "z", "core"), None),
            P(("dp", "z", "core"), None),
            P(("dp", "z", "core"), None),
            P(None, ("z", "core")),
            P(None, ("z", "core")),
            P(None, ("z", "core")),
            P(("z", "core"), None),
            P(("z", "core"), None),
            P(("z", "core"), None),
            P(("z", "core"), None),
            P(("z", "core"), None),
            P(None, ("z", "core")),
            P(("z", "core"), None),
            P(("z", "core"), None),
            P(("z", "core"), None),
            P(("dp", "z", "core"), None),
        ),
        out_specs=(
            P(("dp", "z", "core"), None),
            P(("dp", "z", "core"), None),
            P(None, ("z", "core")),
            P(None, ("z", "core")),
            P(None, ("z", "core")),
            P(("z", "core"), None),
            P(("z", "core"), None),
            P(("z", "core"), None),
            P(("z", "core"), None),
            P(("z", "core"), None),
            P(None, ("z", "core")),
            P(("z", "core"), None),
            P(("z", "core"), None),
            P(("z", "core"), None),
        ),
        check_vma=False,
    )
```

```python
import functools

import jax
import jax.numpy as jnp
import numpy as np
from jax import lax
from jax.experimental import pallas as pl
from jax.experimental.pallas import tpu as pltpu
from jax.sharding import Mesh
from jax.sharding import PartitionSpec as P

HEAD_DIM = 128


def layout(lengths, languages, frame_count):
    utterances = jnp.arange(lengths.shape[-1], dtype=jnp.int32)
    earlier = utterances[:, None] <= utterances[None, :]
    finish = jnp.sum(jnp.where(earlier[None], lengths[:, :, None], 0), axis=1)
    begins = finish - lengths
    indices = jnp.arange(frame_count, dtype=jnp.int32)
    segment = jnp.sum((indices[None, :, None] >= finish[:, None, :]).astype(jnp.int32), axis=-1)
    owners = segment[:, :, None] == jnp.arange(lengths.shape[-1], dtype=jnp.int32)[None, None, :]
    first_row = jnp.sum(jnp.where(owners, begins[:, None, :], 0), axis=-1)
    language_row = jnp.sum(jnp.where(owners, languages[:, None, :], 0), axis=-1)
    return (segment, indices[None, :] - first_row, language_row)


def angles(position):
    half_dim = HEAD_DIM // 2
    frequency = 10000.0 ** (-jnp.arange(half_dim, dtype=jnp.float32) / half_dim)
    turned = position.astype(jnp.float32)[..., None] * frequency
    return (jnp.cos(turned)[..., None, :], jnp.sin(turned)[..., None, :])


VMEM_SPACE = pl.BlockSpec(memory_space=pltpu.VMEM)
SMEM_SPACE = pl.BlockSpec(memory_space=pltpu.SMEM)
ANY_SPACE = pl.BlockSpec(memory_space=pl.ANY)


class Order:
    def __init__(self, value):
        self.value, self.waits = value, []

    def wait(self, *arrays):
        self.waits += arrays

    def call(self, kernel, out_shape, in_specs, out_specs, scratch_shapes, operands, through=(), lazy=False):
        after, self.waits = self.waits, []
        carried = [*through, self.value]
        count, outs, extra = len(operands), len(out_shape), len(after)
        held_in = [i for i in range(count) if in_specs[i] is VMEM_SPACE]
        held_out = [i for i in range(outs) if out_specs[i] is VMEM_SPACE]
        buffers = [pltpu.VMEM(operands[i].shape, operands[i].dtype) for i in held_in]
        buffers += [pltpu.VMEM(out_shape[i].shape, out_shape[i].dtype) for i in held_out]
        copies = max(1, len(held_in), len(held_out))

        def body(*refs):
            ins, rest = list(refs[:count]), refs[count + extra + len(carried) :]
            results, rest = list(rest[:outs]), rest[outs + len(carried) :]
            held, scratch, sems = rest[: len(buffers)], rest[len(buffers) : -1], rest[-1]
            moves = []
            for at, i in enumerate(held_in):
                moves.append(pltpu.make_async_copy(ins[i], held[at], sems.at[at]))
                moves[-1].start()
                ins[i] = held[at]
            targets = []
            for at, i in enumerate(held_out):
                targets.append(results[i])
                results[i] = held[len(held_in) + at]
            def ready():
                for move in arriving:
                    move.wait()

            arriving = moves
            if lazy:
                kernel(ready, *ins, *results, *scratch)
            else:
                ready()
                kernel(*ins, *results, *scratch)
            moves = []
            for at, i in enumerate(held_out):
                moves.append(pltpu.make_async_copy(results[i], targets[at], sems.at[at]))
                moves[-1].start()
            for move in moves:
                move.wait()

        result = pl.pallas_call(
            body,
            out_shape=[*out_shape, *[jax.ShapeDtypeStruct(x.shape, x.dtype) for x in carried]],
            in_specs=[ANY_SPACE if s is VMEM_SPACE else s for s in in_specs]
            + [ANY_SPACE] * (extra + len(carried)),
            out_specs=[ANY_SPACE] * (outs + len(carried)),
            scratch_shapes=[*buffers, *scratch_shapes, pltpu.SemaphoreType.DMA((copies,))],
            input_output_aliases={count + extra + i: outs + i for i in range(len(carried))},
            compiler_params=pltpu.CompilerParams(vmem_limit_bytes=VMEM_LIMIT),
        )(*operands, *after, *carried)
        self.value = result[-1]
        return result[:-1]


VMEM_LIMIT = 60 * 1024 * 1024
QUARTERS = 4
LANES = 128
BITS = (0, 1)


def swap_dp(value, bit, size):
    return lax.ppermute(value, "dp", [(i, i ^ (1 << bit)) for i in range(size)])


def swap_core(value):
    return lax.ppermute(value, "core", [(0, 1), (1, 0)])


def swap_pairs(value, flip, size):
    pairs = []
    for i in range(size):
        for core in range(2):
            far = i ^ (1 << BITS[core ^ flip])
            pairs.append((2 * i + core, 2 * far + core))
    return lax.ppermute(value, ("dp", "core"), pairs)


def pick_kernel(layers, base, place, gathered, out, sems):
    layer = place[1]
    rows, copies = gathered.shape[1], []
    for k in range(1, layers):
        for lane in range(2):
            at = 2 * (k - 1) + lane
            row = lax.rem(layer + k, layers) * 2 + lane
            source = gathered.at[row, :, pl.ds(base, out.shape[1])]
            target = out.at[pl.ds(at * rows, rows)]
            copies.append(pltpu.make_async_copy(source, target, sems.at[at]))
            copies[-1].start()
    for copy in copies:
        copy.wait()


def pick(order, place, layers, gathered, base, width):
    blocks = 2 * (layers - 1)
    return order.call(
        functools.partial(pick_kernel, layers, base),
        [jax.ShapeDtypeStruct((blocks * gathered.shape[1], width), gathered.dtype)],
        [SMEM_SPACE, ANY_SPACE],
        [VMEM_SPACE],
        [pltpu.SemaphoreType.DMA((blocks,))],
        [place, gathered],
    )[0]


def half_kernel(place, piece, out, sems):
    rows = out.shape[0]
    start = pl.multiple_of(place[2] * rows, rows)
    copy = pltpu.make_async_copy(piece.at[pl.ds(start, rows)], out, sems.at[0])
    copy.start()
    copy.wait()


def half(order, place, piece):
    return order.call(
        half_kernel,
        [jax.ShapeDtypeStruct((piece.shape[0] // 2, piece.shape[1]), piece.dtype)],
        [SMEM_SPACE, ANY_SPACE],
        [VMEM_SPACE],
        [pltpu.SemaphoreType.DMA((1,))],
        [place, piece],
    )[0]


def join_kernel(*refs):
    ins, out, sems = refs[:-2], refs[-2], refs[-1]
    at, copies = 0, []
    for k, ref in enumerate(ins):
        target = out.at[:, pl.ds(at, ref.shape[1])]
        copies.append(pltpu.make_async_copy(ref, target, sems.at[k]))
        copies[-1].start()
        at += ref.shape[1]
    for copy in copies:
        copy.wait()


def join(order, arrays):
    width = sum(a.shape[1] for a in arrays)
    return order.call(
        join_kernel,
        [jax.ShapeDtypeStruct((arrays[0].shape[0], width), arrays[0].dtype)],
        [ANY_SPACE] * len(arrays),
        [VMEM_SPACE],
        [pltpu.SemaphoreType.DMA((len(arrays),))],
        arrays,
    )[0]


class Packed:
    def __init__(self, arrays):
        self.own = list(arrays)
        self.all = [*self.own, *[swap_core(a) for a in self.own]]
        self.tokens = sum(a.shape[1] for a in self.all)

    def part(self, index):
        return [(a, index, a.shape[1]) for a in self.all]


class Factor:
    def __init__(self, left, left_index, right, right_index, base, width, relative=True):
        self.left = left.part(left_index)
        self.right, self.right_index, self.base, self.relative = right, right_index, base, relative
        self.width, self.part, self.tokens = width, width // QUARTERS, left.tokens
        self.arrays = [*left.all, *right.all]

    def columns(self, quarter, r, start, width):
        if self.relative:
            index, column = self.right_index + r, pl.ds(self.base + start, width)
        else:
            index = self.right_index
            column = pl.ds(pl.multiple_of((quarter ^ r) * self.part + start, LANES), width)
        return [(a, index, column, count) for a, _, count in self.right.part(0)]


class Sums:
    def __init__(self, *factors):
        self.factors = factors
        self.width = sum(f.part for f in factors)

    def spans(self):
        base = 0
        for i, f in enumerate(self.factors):
            for start in range(0, f.part, TILE):
                yield i, start, min(TILE, f.part - start), base + start
            base += f.part


TILE = 512


def own_rows(ref, layers, core):
    tokens, features = ref.shape
    rows = features // (2 * layers)
    if rows % LANES == 0:
        blocks = [
            ref[:, pl.ds(pl.multiple_of((2 * k + core) * rows, rows), rows)] for k in range(layers)
        ]
        return jnp.concatenate(blocks, axis=1).T
    turned = ref[...].T.reshape(layers, 2, rows, tokens)
    return jnp.where(core == 0, turned[:, 0], turned[:, 1]).reshape(layers * rows, tokens)


def round_kernel(layers, plan, tables, place, *refs):
    jobs, lefts, count_in, count_out = plan
    ins, outs = refs[:count_in], refs[count_in : count_in + count_out]
    left_buffer, turned, right_buffer, add_buffer, out_buffer, left_sems, in_sems, out_sems = refs[
        count_in + count_out :
    ]
    quarter, core = place[0], place[2]

    quarters = {"both": 3, "near": 1 + core, "far": 2 - core, "own": 0}

    def start(source, target, sem):
        copy = pltpu.make_async_copy(source, target, sem)
        copy.start()
        return copy

    left_copies = []
    for i, factor in enumerate(lefts):
        at, copies = 0, []
        for k, (array, index, rows) in enumerate(factor.left):
            target = left_buffer.at[i, at : at + rows]
            copies.append(start(ins[tables[id(array)]].at[index], target, left_sems.at[i, k]))
            at += rows
        left_copies.append(copies)
    loads = []
    for number, (i, r, first, width, adds, _) in enumerate(jobs):
        at, copies = 0, []
        for array, index, column, rows in lefts[i].columns(quarter, quarters[r], first, width):
            source = ins[tables[id(array)]].at[index, :, column]
            target = right_buffer.at[number, at : at + rows, pl.ds(0, width)]
            copies.append(start(source, target, in_sems.at[number, len(copies)]))
            at += rows
        for k, (array, column) in enumerate(adds):
            height = add_buffer.shape[2]
            source = ins[tables[id(array)]].at[pl.ds(0, height), pl.ds(column, width)]
            target = add_buffer.at[number, k, :, pl.ds(0, width)]
            copies.append(start(source, target, in_sems.at[number, len(copies)]))
        loads.append(copies)
    for i, factor in enumerate(lefts):
        for copy in left_copies[i]:
            copy.wait()
        turned[i, :, : factor.tokens] = own_rows(
            left_buffer.at[i, pl.ds(0, factor.tokens)], layers, core
        )
    stores = []
    for number, (i, _, _, width, adds, (out, column)) in enumerate(jobs):
        tokens = lefts[i].tokens
        for copy in loads[number]:
            copy.wait()
        product = jnp.dot(
            turned[i, :, :tokens],
            right_buffer[number, :tokens, :width],
            preferred_element_type=jnp.float32,
        )
        for k in range(len(adds)):
            product += add_buffer[number, k, :, :width].astype(jnp.float32)
        out_buffer[number, :, :width] = product.astype(jnp.bfloat16)
        source = out_buffer.at[number, :, pl.ds(0, width)]
        target = outs[out].at[pl.ds(0, out_buffer.shape[1]), pl.ds(column, width)]
        stores.append(start(source, target, out_sems.at[number]))
    for copy in stores:
        copy.wait()


class Rounds:
    def __init__(self, place, sizes, order):
        self.place, self.order = place, order
        self.dp_size, self.layers = sizes

    def step(self, halves=(), quarters=(), rows=(), margin=0):
        lefts, jobs, widths = [], [], [0, 0, 0]

        def left(factor):
            if factor not in lefts:
                lefts.append(factor)
            return lefts.index(factor)

        def add(sums, r, out, adds):
            base = widths[out]
            for i, first, width, at in sums.spans():
                mine = [(array, offset + at) for array, offset in adds]
                jobs.append((left(sums.factors[i]), r, first, width, mine, (out, base + at)))
            widths[out] += sums.width
            return base

        sent = []
        for sums in halves:
            sums.near_at = add(sums, "both", 0, [])
            sums.own_at = add(sums, "near", 0, [])
        for sums in quarters:
            sums.far_at = add(sums, "far", 1, [(sums.halves, sums.near_at)])
        for sums in rows:
            add(sums, "own", 2, [(sums.halves, sums.own_at), (sums.quarters, sums.far_at)])
        slots = [k for k in range(3) if widths[k]]
        jobs = [job[:5] + ((slots.index(job[5][0]), job[5][1]),) for job in jobs]
        arrays, tables = [], {}
        used = [a for factor in lefts for a in factor.arrays] + [a for job in jobs for a, _ in job[4]]
        for array in used:
            if id(array) not in tables:
                tables[id(array)] = len(arrays)
                arrays.append(array)
        height = lefts[0].left[0][0].shape[2] // 2
        features = lefts[0].left[0][0].shape[2]
        tokens = max(factor.tokens for factor in lefts)
        widest = max(job[3] for job in jobs)
        depth = max(1, max(len(job[4]) for job in jobs))
        pieces = max(len(factor.left) for factor in lefts)
        rights = max(len(factor.right.all) for factor in lefts)
        outs = self.order.call(
            functools.partial(
                round_kernel, self.layers, (jobs, lefts, len(arrays), len(slots)), tables
            ),
            [
                jax.ShapeDtypeStruct((height + (margin if k == 0 else 0), widths[k]), jnp.bfloat16)
                for k in slots
            ],
            [SMEM_SPACE] + [ANY_SPACE] * len(arrays),
            [ANY_SPACE] * len(slots),
            [
                pltpu.VMEM((len(lefts), tokens, features), jnp.bfloat16),
                pltpu.VMEM((len(lefts), height, tokens), jnp.bfloat16),
                pltpu.VMEM((len(jobs), tokens, widest), jnp.bfloat16),
                pltpu.VMEM((len(jobs), depth, height, widest), jnp.bfloat16),
                pltpu.VMEM((len(jobs), height, widest), jnp.bfloat16),
                pltpu.SemaphoreType.DMA((len(lefts), pieces)),
                pltpu.SemaphoreType.DMA((len(jobs), rights + depth)),
                pltpu.SemaphoreType.DMA((len(jobs),)),
            ],
            [self.place, *arrays],
        )
        moved = {k: swap_pairs(outs[slots.index(k)], k, self.dp_size) for k in slots if k < 2}
        for sums in halves:
            sums.halves = moved[0]
        for sums in quarters:
            sums.quarters = moved[1]
        if 2 in slots:
            return lax.psum_scatter(outs[slots.index(2)], "z", scatter_dimension=0, tiled=True)

    def share(self, mine):
        summed = join(self.order, mine)
        bit = len(BITS)
        while 1 << bit < self.dp_size:
            summed = summed + swap_dp(summed, bit, self.dp_size)
            bit += 1
        near = swap_pairs(summed, 0, self.dp_size)
        far = swap_pairs(summed, 1, self.dp_size)
        return [summed, near, far, swap_pairs(near, 1, self.dp_size)]


def spread_kernel(widths, place, *refs):
    pieces, outs = refs[:QUARTERS], refs[QUARTERS:]
    quarter, core = place[0], place[2]
    base = 0
    for i, width in enumerate(widths):
        part = width // QUARTERS
        for r, place_of in enumerate((0, 1 + core, 2 - core, 3)):
            column = pl.ds(pl.multiple_of((quarter ^ place_of) * part, part), part)
            outs[i][:, column] = pieces[r][:, pl.ds(base, part)].astype(jnp.float32)
        base += part


def spread(order, place, widths, pieces):
    rows = pieces[0].shape[0]
    return order.call(
        functools.partial(spread_kernel, widths),
        [jax.ShapeDtypeStruct((rows, w), jnp.float32) for w in widths],
        [SMEM_SPACE] + [VMEM_SPACE] * QUARTERS,
        [VMEM_SPACE] * len(widths),
        [],
        [place, *pieces],
    )


class GatherSet:
    def __init__(self, place, groups):
        quarter = place[0]
        mine = [
            lax.dynamic_slice_in_dim(w, quarter * (w.shape[1] // QUARTERS), w.shape[1] // QUARTERS, 1)
            for group in groups
            for w in group
        ]
        mine = jnp.concatenate(mine, axis=1) if len(mine) > 1 else mine[0]
        self.gathered = lax.all_gather(mine, ("z", "core"), axis=0, tiled=False)


class Gather:
    def __init__(self, place, sizes, order, group, source, base, other, other_base):
        self.place, self.order, self.group = place, order, group
        self.dp_size, self.layers = sizes
        self.source, self.base, self.other, self.other_base = source, base, other, other_base
        self.width = sum(w.shape[1] for w in group) // QUARTERS

    def near(self):
        piece = pick(
            self.order, self.place, self.layers, self.source.gathered, self.base, self.width
        )
        self.piece = swap_pairs(piece, 0, self.dp_size)
        self.other_piece = swap_core(self.piece)

    def arrived(self):
        return [self.other_piece, self.rest, self.other_rest]

    def far(self):
        self.rest = swap_pairs(half(self.order, self.place, self.piece), 1, self.dp_size)
        self.other_rest = swap_core(self.rest)


def gather_small(arrays):
    rows = [a.shape[0] for a in arrays]
    packed = jnp.concatenate(arrays, axis=0)
    packed = jnp.pad(packed, ((0, -packed.shape[0] % 16), (0, 0)))
    full = lax.all_gather(packed, ("z", "core"), axis=0, tiled=False)
    full = full.transpose(1, 0, 2).reshape(packed.shape[0], -1)
    pieces, start = [], 0
    for count in rows:
        pieces.append(full[start : start + count])
        start += count
    return pieces


def pack_small(table_hot, frames_grad, vectors):
    count = table_hot.shape[1]
    extra = -(frames_grad.shape[0] + vectors.shape[0]) % 16
    left = jnp.concatenate([frames_grad, vectors, jnp.zeros((extra, vectors.shape[1]), vectors.dtype)])
    used = count + vectors.shape[0]
    share = -(-used // QUARTERS)
    unit = jnp.eye(vectors.shape[0], dtype=table_hot.dtype)
    right = jnp.block(
        [
            [table_hot, jnp.zeros((table_hot.shape[0], vectors.shape[0]), table_hot.dtype)],
            [jnp.zeros((vectors.shape[0], count), table_hot.dtype), unit],
        ]
    )
    right = jnp.pad(right, ((0, extra), (0, share * QUARTERS - used)))
    right = right.reshape(right.shape[0], QUARTERS, share)
    right = jnp.pad(right, ((0, 0), (0, 0), (0, LANES - share)))
    right = right.reshape(right.shape[0], QUARTERS * LANES)
    right = jnp.pad(right, ((0, 0), (0, left.shape[1] - right.shape[1])))
    return jnp.stack([left.astype(jnp.bfloat16), right.astype(jnp.bfloat16)])


def unpack_small(summed, counts):
    used = sum(counts)
    share = -(-used // QUARTERS)
    rows = summed.reshape(summed.shape[0], QUARTERS, LANES)[:, :, :share]
    rows = rows.reshape(summed.shape[0], QUARTERS * share).T
    pieces, start = [], 0
    for count in counts:
        pieces.append(rows[start : start + count])
        start += count
    return pieces

EPSILON = 1e-05
MASKED = -1000000000.0


def dot_rows(left, right):
    return jnp.dot(left, right, preferred_element_type=jnp.float32)


def dot_cols(left, right):
    return lax.dot_general(
        left, right, (((1,), (1,)), ((), ())), preferred_element_type=jnp.float32
    )


def dot_down(left, right):
    return jnp.dot(left.T, right, preferred_element_type=jnp.float32)


def standard(values):
    centred = values - jnp.mean(values, axis=-1, keepdims=True)
    spread = lax.rsqrt(jnp.mean(centred * centred, axis=-1, keepdims=True) + EPSILON)
    return centred * spread, spread


def norm_back(values, gradient, gain):
    shape, spread = standard(values)
    inner = gradient * gain
    back = spread * (
        inner
        - jnp.mean(inner, axis=-1, keepdims=True)
        - shape * jnp.mean(inner * shape, axis=-1, keepdims=True)
    )
    return (
        back,
        jnp.sum(gradient * shape, axis=0, keepdims=True),
        jnp.sum(gradient, axis=0, keepdims=True),
    )


def sigmoid(values):
    return 1.0 / (1.0 + jnp.exp(-values))


def silu_back(values, gradient):
    gate = sigmoid(values)
    return gradient * gate * (1.0 + values * (1.0 - gate))


CUTS = 2


def packed_shapes(parts, tokens, width):
    return [jax.ShapeDtypeStruct((parts, tokens // CUTS, width), jnp.bfloat16)] * CUTS


def store_part(outs, index, values, column=slice(None)):
    at = 0
    for out in outs:
        out[index, :, column] = values[at : at + out.shape[1]]
        at += out.shape[1]


def load_part(refs, index, width):
    return jnp.concatenate([ref[index, :, :width] for ref in refs], axis=0)


class Pieces:
    def __init__(self, gather, index):
        group = gather.group
        self.layers = gather.layers
        before = sum(w.shape[1] for w in group[:index])
        self.base = before // QUARTERS
        self.set_base = gather.base + self.base
        self.other_base = gather.other_base + before
        self.rows, self.width = group[index].shape
        self.operands = [
            group[index],
            gather.other,
            gather.source.gathered,
            gather.piece,
            gather.other_piece,
            gather.rest,
            gather.other_rest,
        ]

    @property
    def part(self):
        return self.width // QUARTERS

    @property
    def scratch(self):
        copies = 1 + (QUARTERS - 1) * 2 * self.layers
        return [
            pltpu.VMEM((QUARTERS, 2 * self.layers, self.rows, self.part), jnp.bfloat16),
            pltpu.SemaphoreType.DMA((copies,)),
        ]

    def load(self, place, refs, buffer, sems):
        own, other, gathered, piece, other_piece, rest, other_rest = refs
        quarter, layer, core = place[0], place[1], place[2]
        span = pl.ds(self.base, self.part)
        copies = []

        def move(source, target):
            copies.append(pltpu.make_async_copy(source, target, sems.at[len(copies)]))
            copies[-1].start()

        def blocks(source, index, first, count):
            for number in range(count):
                at = first + number
                row = lax.rem(layer + 1 + at // 2, self.layers) * 2 + lax.rem(at, 2)
                move(source.at[pl.ds(number * self.rows, self.rows), span], buffer.at[index, row])

        move(gathered.at[:, :, pl.ds(self.set_base, self.part)], buffer.at[quarter])
        for r in range(1, QUARTERS):
            index = quarter ^ r
            near = pl.multiple_of(index * self.part, LANES)
            far = pl.multiple_of(self.other_base + index * self.part, LANES)
            move(own.at[:, pl.ds(near, self.part)], buffer.at[index, 2 * layer + core])
            move(other.at[:, pl.ds(far, self.part)], buffer.at[index, 2 * layer + 1 - core])
        count = 2 * (self.layers - 1)
        blocks(piece, quarter ^ (1 + core), jnp.int32(0), count)
        blocks(other_piece, quarter ^ (2 - core), jnp.int32(0), count)
        blocks(rest, quarter ^ 3, core * (count // 2), count // 2)
        blocks(other_rest, quarter ^ 3, (1 - core) * (count // 2), count // 2)
        return [(quarter, copies[:1]), (quarter ^ 1, copies[1:]), (quarter ^ 2, []), (quarter ^ 3, [])]

    def block(self, buffer, index):
        return buffer[index].reshape(2 * self.layers * self.rows, self.part)


def wait_all(steps):
    for _, copies in steps:
        for copy in copies:
            copy.wait()


def up_kernel(pieces, row, ready, place, values, gains, shifts, *refs):
    weight, outs, (buffer, sems) = refs[: -3 - CUTS], refs[-3 - CUTS : -2], refs[-2:]
    expanded_out, packed = outs[0], outs[1:]
    steps = pieces.load(place, weight, buffer, sems)
    ready()
    shape, _ = standard(values[...])
    hidden = (shape * gains[row : row + 1] + shifts[row : row + 1]).astype(jnp.bfloat16)
    store_part(packed, 0, hidden)
    for r, (index, copies) in enumerate(steps):
        for copy in copies:
            copy.wait()
        expanded = dot_rows(hidden, pieces.block(buffer, index))
        expanded_out[r] = expanded.astype(jnp.bfloat16)
        store_part(packed, 1 + r, (expanded * sigmoid(expanded)).astype(jnp.bfloat16))


def up_step(order, place, gather, index, row, values, gains, shifts):
    pieces = Pieces(gather, index)
    tokens, width = values.shape
    expanded, *packed = order.call(
        functools.partial(up_kernel, pieces, row),
        [
            jax.ShapeDtypeStruct((QUARTERS, tokens, pieces.part), jnp.bfloat16),
            *packed_shapes(1 + QUARTERS, tokens, width),
        ],
        [SMEM_SPACE] + [VMEM_SPACE] * 3 + [ANY_SPACE] * len(pieces.operands),
        [VMEM_SPACE] * (1 + CUTS),
        pieces.scratch,
        [place, values, gains, shifts, *pieces.operands],
        lazy=True,
    )
    return expanded, packed


def down_sum(pieces, ready, place, packed, first, weight, buffer, sems):
    total, steps = None, pieces.load(place, weight, buffer, sems)
    ready()
    for r, (index, copies) in enumerate(steps):
        for copy in copies:
            copy.wait()
        term = dot_cols(
            load_part(packed, first + r, pieces.part), pieces.block(buffer, index)
        )
        total = term if total is None else total + term
    return total


def down_kernel(pieces, ready, place, values, *refs):
    active, weight, (out, buffer, sems) = refs[:CUTS], refs[CUTS:-3], refs[-3:]
    branch = down_sum(pieces, ready, place, active, 1, weight, buffer, sems)
    out[...] = values[...] + 0.5 * branch


def down_step(order, place, gather, index, values, active):
    pieces = Pieces(gather, index)
    return order.call(
        functools.partial(down_kernel, pieces),
        [jax.ShapeDtypeStruct(values.shape, jnp.float32)],
        [SMEM_SPACE] + [VMEM_SPACE] * (1 + CUTS) + [ANY_SPACE] * len(pieces.operands),
        [VMEM_SPACE],
        pieces.scratch,
        [place, values, *active, *pieces.operands],
        lazy=True,
    )[0]


def last_kernel(pieces, row, ready, place, values, cotangent, gains, shifts, *refs):
    active, weight, outs = refs[:CUTS], refs[CUTS:-7], refs[-7:]
    encoded, grad_out, low_out, gain_out, shift_out, buffer, sems = outs
    branch = down_sum(pieces, ready, place, active, 1, weight, buffer, sems)
    total = values[...] + 0.5 * branch
    gain = gains[row : row + 1]
    shape, _ = standard(total)
    encoded[...] = (shape * gain + shifts[row : row + 1]).astype(jnp.bfloat16)
    back, gain_grad, shift_grad = norm_back(total, cotangent[...].astype(jnp.float32), gain)
    grad_out[...] = back
    low_out[...] = (0.5 * back).astype(jnp.bfloat16)
    gain_out[...] = gain_grad
    shift_out[...] = shift_grad


def vector_shapes(width, count=2):
    return [jax.ShapeDtypeStruct((1, width), jnp.float32)] * count


def last_step(order, place, gather, index, row, values, active, cotangent, gains, shifts, through):
    pieces = Pieces(gather, index)
    return order.call(
        functools.partial(last_kernel, pieces, row),
        [
            jax.ShapeDtypeStruct(values.shape, jnp.bfloat16),
            jax.ShapeDtypeStruct(values.shape, jnp.float32),
            jax.ShapeDtypeStruct(values.shape, jnp.bfloat16),
            *vector_shapes(values.shape[1]),
        ],
        [SMEM_SPACE] + [VMEM_SPACE] * (4 + CUTS) + [ANY_SPACE] * len(pieces.operands),
        [VMEM_SPACE] * 5,
        pieces.scratch,
        [place, values, cotangent, gains, shifts, *active, *pieces.operands],
        through,
        lazy=True,
    )


def down_back_kernel(pieces, ready, place, gradient, expanded, *refs):
    weight, outs, (buffer, sems) = refs[: -2 - CUTS], refs[-2 - CUTS : -2], refs[-2:]
    steps = pieces.load(place, weight, buffer, sems)
    ready()
    store_part(outs, 0, gradient[...])
    for r, (index, copies) in enumerate(steps):
        for copy in copies:
            copy.wait()
        active_grad = dot_rows(gradient[...], pieces.block(buffer, index))
        store_part(outs, 1 + r, silu_back(expanded[r].astype(jnp.float32), active_grad).astype(jnp.bfloat16))


def down_back_step(order, place, gather, index, gradient, expanded):
    pieces = Pieces(gather, index)
    return order.call(
        functools.partial(down_back_kernel, pieces),
        packed_shapes(1 + QUARTERS, *gradient.shape),
        [SMEM_SPACE] + [VMEM_SPACE] * 2 + [ANY_SPACE] * len(pieces.operands),
        [VMEM_SPACE] * CUTS,
        pieces.scratch,
        [place, gradient, expanded, *pieces.operands],
        lazy=True,
    )


def into_norm_kernel(pieces, first, row, scale, ready, place, values, residual, gains, *refs):
    gradient, refs = refs[:CUTS], refs[CUTS:]
    weight, (grad_out, low_out, gain_out, shift_out, buffer, sems) = refs[:-6], refs[-6:]
    hidden_grad = down_sum(pieces, ready, place, gradient, first, weight, buffer, sems)
    back, gain_grad, shift_grad = norm_back(values[...], hidden_grad, gains[row : row + 1])
    total = residual[...] + back
    grad_out[...] = total
    low_out[...] = (scale * total).astype(jnp.bfloat16)
    gain_out[...] = gain_grad
    shift_out[...] = shift_grad


def into_norm_step(
    order, place, gather, index, first, row, scale, gradient, values, residual, gains, through=()
):
    pieces = Pieces(gather, index)
    return order.call(
        functools.partial(into_norm_kernel, pieces, first, row, scale),
        [
            jax.ShapeDtypeStruct(values.shape, jnp.float32),
            jax.ShapeDtypeStruct(values.shape, jnp.bfloat16),
            *vector_shapes(values.shape[1]),
        ],
        [SMEM_SPACE] + [VMEM_SPACE] * (3 + CUTS) + [ANY_SPACE] * len(pieces.operands),
        [VMEM_SPACE] * 4,
        pieces.scratch,
        [place, values, residual, gains, *gradient, *pieces.operands],
        through,
        lazy=True,
    )


def whole_weight(pieces, ready, place, weight, buffer, sems):
    steps = pieces.load(place, weight, buffer, sems)
    ready()
    wait_all(steps)


def turn(values, cosine, sine):
    return values * cosine + pltpu.roll(values, HEAD_DIM // 2, 1) * sine


def masked_scores(query, key, matching):
    return jnp.where(matching, dot_cols(query, key), MASKED)


def head(index):
    return slice(index * HEAD_DIM, (index + 1) * HEAD_DIM)


def attend_kernel(pieces, row, ready, place, values, gains, shifts, cosine, sine, down, across, *refs):
    weight, outs = refs[:-6], refs[-6:]
    turned_out, totals_out, packed, projected, buffer, sems = outs
    steps = pieces.load(place, weight, buffer, sems)
    ready()
    shape, _ = standard(values[...])
    hidden = (shape * gains[row : row + 1] + shifts[row : row + 1]).astype(jnp.bfloat16)
    packed[0] = hidden
    for index, copies in steps:
        for copy in copies:
            copy.wait()
        column = pl.ds(pl.multiple_of(index * pieces.part, pieces.part), pieces.part)
        projected[:, column] = dot_rows(hidden, pieces.block(buffer, index))
    heads = pieces.width // (3 * HEAD_DIM)
    matching = down[...] == across[...]
    for h in range(heads):
        query = turn(projected[:, head(h)], cosine[...], sine[...]) * HEAD_DIM ** (-0.5)
        key = turn(projected[:, head(heads + h)], cosine[...], sine[...])
        query, key = query.astype(jnp.bfloat16), key.astype(jnp.bfloat16)
        value = projected[:, head(2 * heads + h)].astype(jnp.bfloat16)
        turned_out[:, head(h)] = query
        turned_out[:, head(heads + h)] = key
        turned_out[:, head(2 * heads + h)] = value
        scores = masked_scores(query, key, matching)
        highest = jnp.max(scores, axis=-1, keepdims=True)
        powers = jnp.exp(scores - highest)
        total = jnp.sum(powers, axis=-1, keepdims=True)
        totals_out[:, h : h + 1] = highest + jnp.log(total)
        probs = (powers / total).astype(jnp.bfloat16)
        packed[1, :, head(h)] = dot_rows(probs, value).astype(jnp.bfloat16)


def attend_step(order, place, gather, index, row, values, gains, shifts, cosine, sine, down, across):
    pieces = Pieces(gather, index)
    tokens, width = values.shape
    heads = pieces.width // (3 * HEAD_DIM)
    return order.call(
        functools.partial(attend_kernel, pieces, row),
        [
            jax.ShapeDtypeStruct((tokens, pieces.width), jnp.bfloat16),
            jax.ShapeDtypeStruct((tokens, heads), jnp.float32),
            jax.ShapeDtypeStruct((2, tokens, width), jnp.bfloat16),
        ],
        [SMEM_SPACE] + [VMEM_SPACE] * 7 + [ANY_SPACE] * len(pieces.operands),
        [VMEM_SPACE] * 3,
        [pltpu.VMEM((tokens, pieces.width), jnp.float32), *pieces.scratch],
        [place, values, gains, shifts, cosine, sine, down, across, *pieces.operands],
        lazy=True,
    )


def to_quarters(place, outs, column, values):
    part = values.shape[1] // QUARTERS
    for r in range(QUARTERS):
        block = values[:, pl.ds(pl.multiple_of((place[0] ^ r) * part, part), part)]
        store_part(outs, r, block, slice(column, column + part))


def attend_back_kernel(pieces, ready, place, gradient, turned, totals, cosine, sine, down, across, *refs):
    weight, rest = refs[: -4 - CUTS], refs[-4 - CUTS :]
    outs, (out, mixed_grad, buffer, sems) = rest[:CUTS], rest[CUTS:]
    heads = turned.shape[1] // (3 * HEAD_DIM)
    whole_weight(pieces, ready, place, weight, buffer, sems)
    total = None
    for index in range(QUARTERS):
        column = slice(index * pieces.part, (index + 1) * pieces.part)
        term = dot_cols(gradient[:, column], pieces.block(buffer, index))
        total = term if total is None else total + term
    mixed_grad[...] = total.astype(jnp.bfloat16)
    matching = down[...] == across[...]
    for h in range(heads):
        query = turned[:, head(h)]
        key = turned[:, head(heads + h)]
        value = turned[:, head(2 * heads + h)]
        gradient_h = mixed_grad[:, head(h)]
        probs = jnp.exp(masked_scores(query, key, matching) - totals[:, h : h + 1])
        value_grad = dot_down(probs.astype(jnp.bfloat16), gradient_h)
        probs_grad = dot_cols(gradient_h, value)
        inner = jnp.sum(probs * probs_grad, axis=-1, keepdims=True)
        score_grad = (probs * (probs_grad - inner)).astype(jnp.bfloat16)
        query_grad = dot_rows(score_grad, key) * HEAD_DIM ** (-0.5)
        key_grad = dot_down(score_grad, query)
        out[:, head(h)] = turn(query_grad, cosine[...], -sine[...]).astype(jnp.bfloat16)
        out[:, head(heads + h)] = turn(key_grad, cosine[...], -sine[...]).astype(jnp.bfloat16)
        out[:, head(2 * heads + h)] = value_grad.astype(jnp.bfloat16)
    to_quarters(place, outs, 0, out)
    to_quarters(place, outs, out.shape[1] // QUARTERS, gradient)


def attend_back_step(order, place, gather, index, gradient, turned, totals, cosine, sine, down, across):
    pieces = Pieces(gather, index)
    return order.call(
        functools.partial(attend_back_kernel, pieces),
        packed_shapes(
            QUARTERS, turned.shape[0], (turned.shape[1] + gradient.shape[1]) // QUARTERS
        ),
        [SMEM_SPACE] + [VMEM_SPACE] * 7 + [ANY_SPACE] * len(pieces.operands),
        [VMEM_SPACE] * CUTS,
        [
            pltpu.VMEM(turned.shape, jnp.bfloat16),
            pltpu.VMEM(gradient.shape, jnp.bfloat16),
            *pieces.scratch,
        ],
        [place, gradient, turned, totals, cosine, sine, down, across, *pieces.operands],
        lazy=True,
    )


def rows_sum(pieces, buffer, left):
    return jnp.concatenate(
        [dot_rows(left, pieces.block(buffer, index)) for index in range(QUARTERS)], axis=1
    )


def shifted(values, amount):
    return values if amount == 0 else pltpu.roll(values, amount % values.shape[0], 0)


def merge_kernel(pieces, ready, place, values, mixed, *refs):
    weight, (out, buffer, sems) = refs[:-3], refs[-3:]
    whole_weight(pieces, ready, place, weight, buffer, sems)
    for index in range(QUARTERS):
        column = slice(index * pieces.part, (index + 1) * pieces.part)
        out[:, column] = values[:, column] + dot_rows(mixed[1], pieces.block(buffer, index))


def merge_step(order, place, gather, index, values, mixed):
    pieces = Pieces(gather, index)
    return order.call(
        functools.partial(merge_kernel, pieces),
        [jax.ShapeDtypeStruct(values.shape, jnp.float32)],
        [SMEM_SPACE] + [VMEM_SPACE] * 2 + [ANY_SPACE] * len(pieces.operands),
        [VMEM_SPACE],
        pieces.scratch,
        [place, values, mixed, *pieces.operands],
        lazy=True,
    )[0]


def conv_kernel(weights, row, ready, place, values, gains, shifts, taps, keep, *refs):
    count = len(weights[0].operands)
    operands = [refs[i * count : (i + 1) * count] for i in range(len(weights))]
    rest = refs[len(weights) * count :]
    done_out, doubled_out, filtered_out, packed = rest[:4]
    scratch = rest[4:]
    buffers = [scratch[2 * i : 2 * i + 2] for i in range(len(weights))]
    steps = [w.load(place, o, *b) for w, o, b in zip(weights, operands, buffers)]
    gating, pointwise = weights
    ready()
    shape, _ = standard(values[...])
    hidden = (shape * gains[row : row + 1] + shifts[row : row + 1]).astype(jnp.bfloat16)
    packed[0] = hidden
    wait_all(steps[0])
    doubled = rows_sum(gating, buffers[0][0], hidden)
    doubled_out[...] = doubled.astype(jnp.bfloat16)
    half = gating.width // 2
    gated = doubled[:, :half] * sigmoid(doubled[:, half:])
    reach = taps.shape[0] // 2
    filtered = None
    for k in range(taps.shape[0]):
        term = shifted(gated, reach - k) * keep[:, k : k + 1] * taps[k : k + 1]
        filtered = term if filtered is None else filtered + term
    filtered_out[...] = filtered
    shape, _ = standard(filtered)
    renormed = shape * gains[row + 1 : row + 2] + shifts[row + 1 : row + 2]
    active = (renormed * sigmoid(renormed)).astype(jnp.bfloat16)
    packed[1] = active
    wait_all(steps[1])
    for index in range(QUARTERS):
        column = slice(index * pointwise.part, (index + 1) * pointwise.part)
        term = dot_rows(active, pointwise.block(buffers[1][0], index))
        done_out[:, column] = values[:, column] + term


def conv_step(order, place, gather, row, values, gains, shifts, taps, keep):
    weights = [Pieces(gather, i) for i in range(2)]
    tokens, width = values.shape
    operands = [o for w in weights for o in w.operands]
    return order.call(
        functools.partial(conv_kernel, weights, row),
        [
            jax.ShapeDtypeStruct((tokens, width), jnp.float32),
            jax.ShapeDtypeStruct((tokens, weights[0].width), jnp.bfloat16),
            jax.ShapeDtypeStruct((tokens, weights[0].width // 2), jnp.float32),
            jax.ShapeDtypeStruct((2, tokens, width), jnp.bfloat16),
        ],
        [SMEM_SPACE] + [VMEM_SPACE] * 5 + [ANY_SPACE] * len(operands),
        [VMEM_SPACE] * 4,
        [s for w in weights for s in w.scratch],
        [place, values, gains, shifts, taps, keep, *operands],
        lazy=True,
    )


def conv_back_kernel(pieces, row, ready, place, gradient, filtered, doubled, gains, shifts, taps, keep, *refs):
    weight, rest = refs[: -6 - CUTS], refs[-6 - CUTS :]
    outs = rest[:CUTS]
    gain_out, shift_out, taps_out, doubled_grad, buffer, sems = rest[CUTS:]
    whole_weight(pieces, ready, place, weight, buffer, sems)
    total = None
    for index in range(QUARTERS):
        column = slice(index * pieces.part, (index + 1) * pieces.part)
        term = dot_cols(gradient[:, column], pieces.block(buffer, index))
        total = term if total is None else total + term
    gain = gains[row : row + 1]
    shape, _ = standard(filtered[...])
    renormed = shape * gain + shifts[row : row + 1]
    back, gain_grad, shift_grad = norm_back(filtered[...], silu_back(renormed, total), gain)
    gain_out[...] = gain_grad
    shift_out[...] = shift_grad
    half = doubled.shape[1] // 2
    gate = sigmoid(doubled[:, half:].astype(jnp.float32))
    gated = doubled[:, :half].astype(jnp.float32) * gate
    reach = taps.shape[0] // 2
    gated_grad = None
    for k in range(taps.shape[0]):
        kept = back * keep[:, k : k + 1]
        taps_out[k : k + 1] = jnp.sum(kept * shifted(gated, reach - k), axis=0, keepdims=True)
        term = shifted(kept, k - reach) * taps[k : k + 1]
        gated_grad = term if gated_grad is None else gated_grad + term
    doubled_grad[:, :half] = (gated_grad * gate).astype(jnp.bfloat16)
    doubled_grad[:, half:] = (gated_grad * gated * (1.0 - gate)).astype(jnp.bfloat16)
    to_quarters(place, outs, 0, doubled_grad)
    to_quarters(place, outs, doubled_grad.shape[1] // QUARTERS, gradient)


def conv_back_step(order, place, gather, index, row, gradient, filtered, doubled, gains, shifts, taps, keep):
    pieces = Pieces(gather, index)
    width = filtered.shape[1]
    return order.call(
        functools.partial(conv_back_kernel, pieces, row),
        [
            *packed_shapes(
                QUARTERS, doubled.shape[0], (doubled.shape[1] + gradient.shape[1]) // QUARTERS
            ),
            *vector_shapes(width),
            jax.ShapeDtypeStruct(taps.shape, jnp.float32),
        ],
        [SMEM_SPACE] + [VMEM_SPACE] * 7 + [ANY_SPACE] * len(pieces.operands),
        [VMEM_SPACE] * (3 + CUTS),
        [pltpu.VMEM(doubled.shape, jnp.bfloat16), *pieces.scratch],
        [place, gradient, filtered, doubled, gains, shifts, taps, keep, *pieces.operands],
        lazy=True,
    )


def shards(
    sizes,
    frames,
    lengths,
    languages,
    embedding,
    gains,
    shifts,
    firstup,
    firstdown,
    projection,
    merger,
    gating,
    kernel,
    pointwise,
    secondup,
    seconddown,
    cotangent,
):
    frame_count = frames.shape[0]
    dp_index = lax.axis_index("dp").astype(jnp.int32)
    place = jnp.stack(
        [
            lax.rem(dp_index, jnp.int32(QUARTERS)),
            lax.axis_index("z").astype(jnp.int32),
            lax.axis_index("core").astype(jnp.int32),
        ]
    )
    order = Order(frames)
    order_of_groups = (
        ([firstup], [firstdown]),
        ([projection, merger], [gating, pointwise]),
        ([secondup],),
        ([seconddown],),
    )
    sources = [GatherSet(place, groups) for groups in order_of_groups]
    everything = jnp.concatenate([w for s in order_of_groups for g in s for w in g], axis=1)
    everything_other = swap_core(everything)
    gathers, other_base = [], 0
    for source, groups in zip(sources, order_of_groups):
        base = 0
        for group in groups:
            gathers.append(
                Gather(place, sizes, order, group, source, base, everything_other, other_base)
            )
            base += gathers[-1].width
            other_base += QUARTERS * gathers[-1].width
    table_full, gain_full, shift_full, kernel_full = gather_small(
        [embedding, gains, shifts, kernel]
    )
    segment_all, position_all, language_all = layout(lengths, languages, frame_count)
    segment = segment_all[0]
    language_row = language_all[0]
    cosine, sine = angles(position_all[0])
    cosine = jnp.concatenate([cosine, cosine], axis=-1)[:, 0]
    sine = jnp.concatenate([-sine, sine], axis=-1)[:, 0]
    down, across = segment[:, None], segment[None, :]
    gain_rows = gain_full.astype(jnp.float32)
    shift_rows = shift_full.astype(jnp.float32)
    taps = kernel_full.astype(jnp.float32)
    reach = taps.shape[0] // 2
    segment_pad = jnp.pad(segment, (reach, reach), constant_values=-1)
    keep = jnp.stack(
        [segment_pad[k : k + frame_count] == segment for k in range(taps.shape[0])], axis=1
    ).astype(jnp.float32)
    language_hot = (
        language_row[:, None] == jnp.arange(table_full.shape[0], dtype=jnp.int32)[None, :]
    ).astype(jnp.float32)
    start_sum = frames.astype(jnp.float32) + jnp.dot(
        language_hot.astype(jnp.bfloat16), table_full, preferred_element_type=jnp.float32
    )

    gathers[0].near()
    order.wait(everything_other)
    gathers[0].far()
    gathers[1].near()
    order.wait(*gathers[0].arrived())
    gathers[1].far()
    gathers[2].near()
    first_expanded, first_packed = up_step(
        order, place, gathers[0], 0, 0, start_sum, gain_rows, shift_rows
    )
    order.wait(*gathers[1].arrived())
    gathers[2].far()
    gathers[3].near()
    after_first = down_step(order, place, gathers[1], 0, start_sum, first_packed)
    order.wait(*gathers[2].arrived())
    gathers[3].far()
    gathers[4].near()
    turned, totals, attend_packed = attend_step(
        order, place, gathers[2], 0, 1, after_first, gain_rows, shift_rows, cosine, sine, down, across
    )
    after_attention = merge_step(order, place, gathers[2], 1, after_first, attend_packed)
    order.wait(*gathers[3].arrived())
    gathers[4].far()
    gathers[5].near()
    after_conv, doubled, filtered, conv_packed = conv_step(
        order, place, gathers[3], 2, after_attention, gain_rows, shift_rows, taps, keep
    )
    order.wait(*gathers[4].arrived())
    gathers[5].far()
    second_expanded, second_packed = up_step(
        order, place, gathers[4], 0, 4, after_conv, gain_rows, shift_rows
    )
    encoded, grad_second, low_second, final_gain, final_shift, *held = last_step(
        order,
        place,
        gathers[5],
        0,
        5,
        after_conv,
        second_packed,
        cotangent,
        gain_rows,
        shift_rows,
        [*second_packed, conv_packed, attend_packed],
    )
    *second_packed, conv_packed, attend_packed = held
    forward, conv_forward, attend_forward = (
        Packed(second_packed),
        Packed([conv_packed]),
        Packed([attend_packed]),
    )
    rounds = Rounds(place, sizes, order)
    width = frames.shape[1]

    packed = down_back_step(order, place, gathers[5], 0, low_second, second_expanded)
    backward = Packed(packed)
    grad_conv, low_conv, second_gain, second_shift, *first_packed = into_norm_step(
        order,
        place,
        gathers[4],
        0,
        1,
        4,
        1.0,
        packed,
        after_conv,
        grad_second,
        gain_rows,
        first_packed,
    )
    first_forward = Packed(first_packed)
    down_two = Sums(Factor(backward, 0, forward, 1, 0, seconddown.shape[1]))
    up_two = Sums(Factor(forward, 0, backward, 1, 0, secondup.shape[1]))
    order.wait(*conv_forward.all, *attend_forward.all)
    rounds.step([down_two], margin=80)
    order.wait(*first_forward.all)
    rounds.step([up_two], margin=64)
    *packed, inner_gain, inner_shift, taps_grad = conv_back_step(
        order, place, gathers[3], 1, 3, low_conv, filtered, doubled, gain_rows, shift_rows, taps, keep
    )
    backward = Packed(packed)
    grad_attention, low_attention, outer_gain, outer_shift = into_norm_step(
        order,
        place,
        gathers[3],
        0,
        0,
        2,
        1.0,
        packed,
        after_attention,
        grad_conv,
        gain_rows,
    )
    conv = Sums(
        Factor(conv_forward, 0, backward, 0, 0, gating.shape[1]),
        Factor(conv_forward, 1, backward, 0, gating.shape[1] // QUARTERS, pointwise.shape[1]),
    )
    order.wait(*backward.all)
    packed = attend_back_step(
        order, place, gathers[2], 1, low_attention, turned, totals, cosine, sine, down, across
    )
    backward = Packed(packed)
    rounds.step([conv], [down_two], margin=48)
    grad_first, low_first, attend_gain, attend_shift = into_norm_step(
        order,
        place,
        gathers[2],
        0,
        0,
        1,
        0.5,
        packed,
        after_first,
        grad_attention,
        gain_rows,
    )
    attend = Sums(
        Factor(attend_forward, 0, backward, 0, 0, projection.shape[1]),
        Factor(attend_forward, 1, backward, 0, projection.shape[1] // QUARTERS, merger.shape[1]),
    )
    order.wait(*backward.all)
    packed = down_back_step(order, place, gathers[1], 0, low_first, first_expanded)
    backward = Packed(packed)
    down_two_mine = rounds.step([attend], [up_two], [down_two], margin=32)
    frames_grad, low_start, first_gain, first_shift = into_norm_step(
        order, place, gathers[0], 0, 1, 0, 1.0, packed, start_sum, grad_first, gain_rows
    )
    down_one = Sums(Factor(backward, 0, first_forward, 1, 0, firstdown.shape[1]))
    up_one = Sums(Factor(first_forward, 0, backward, 1, 0, firstup.shape[1]))
    vectors = jnp.concatenate(
        [
            first_gain,
            attend_gain,
            outer_gain,
            inner_gain,
            second_gain,
            final_gain,
            first_shift,
            attend_shift,
            outer_shift,
            inner_shift,
            second_shift,
            final_shift,
            taps_grad,
        ]
    )
    small_packed = Packed([pack_small(language_hot, low_start, vectors)])
    small = Sums(Factor(small_packed, 0, small_packed, 1, 0, QUARTERS * LANES, relative=False))
    up_two_mine = rounds.step([down_one], [conv], [up_two], margin=16)
    conv_mine = rounds.step([up_one], [attend], [conv])
    order.wait(down_two_mine)
    attend_mine = rounds.step([small], [down_one], [attend])
    order.wait(up_two_mine)
    down_one_mine = rounds.step([], [up_one, small], [down_one])
    order.wait(conv_mine)
    last_mine = rounds.step([], [], [up_one, small])
    ffn_pieces = rounds.share([down_two_mine, up_two_mine])
    order.wait(attend_mine)
    middle_pieces = rounds.share([conv_mine, attend_mine])
    seconddown_grad, secondup_grad = spread(
        order, place, [seconddown.shape[1], secondup.shape[1]], ffn_pieces
    )
    middle = [gating, pointwise, projection, merger]
    gating_grad, pointwise_grad, projection_grad, merger_grad = spread(
        order, place, [w.shape[1] for w in middle], middle_pieces
    )
    last_pieces = rounds.share([down_one_mine, last_mine])
    firstdown_grad, firstup_grad, small = spread(
        order, place, [firstdown.shape[1], firstup.shape[1], QUARTERS * LANES], last_pieces
    )
    counts = [embedding.shape[0], gains.shape[0], shifts.shape[0], kernel.shape[0]]
    table_sum, gain_sum, shift_sum, taps_sum = unpack_small(small, counts)
    return (
        encoded,
        frames_grad,
        table_sum,
        gain_sum,
        shift_sum,
        firstup_grad,
        firstdown_grad,
        projection_grad,
        merger_grad,
        gating_grad,
        taps_sum,
        pointwise_grad,
        secondup_grad,
        seconddown_grad,
    )


def solution(mesh):
    dp_size, fsdp_size = mesh.shape["dp"], mesh.shape["fsdp"]
    layers = fsdp_size // 2
    split = Mesh(mesh.devices.reshape(dp_size, layers, 2), ("dp", "z", "core"))
    return jax.shard_map(
        functools.partial(shards, (dp_size, layers)),
        mesh=split,
        in_specs=(
            P(("dp", "z", "core"), None),
            P(("dp", "z", "core"), None),
            P(("dp", "z", "core"), None),
            P(None, ("z", "core")),
            P(None, ("z", "core")),
            P(None, ("z", "core")),
            P(("z", "core"), None),
            P(("z", "core"), None),
            P(("z", "core"), None),
            P(("z", "core"), None),
            P(("z", "core"), None),
            P(None, ("z", "core")),
            P(("z", "core"), None),
            P(("z", "core"), None),
            P(("z", "core"), None),
            P(("dp", "z", "core"), None),
        ),
        out_specs=(
            P(("dp", "z", "core"), None),
            P(("dp", "z", "core"), None),
            P(None, ("z", "core")),
            P(None, ("z", "core")),
            P(None, ("z", "core")),
            P(("z", "core"), None),
            P(("z", "core"), None),
            P(("z", "core"), None),
            P(("z", "core"), None),
            P(("z", "core"), None),
            P(None, ("z", "core")),
            P(("z", "core"), None),
            P(("z", "core"), None),
            P(("z", "core"), None),
        ),
        check_vma=False,
    )
```

```python
import functools

import jax
import jax.numpy as jnp
import numpy as np
from jax import lax
from jax.experimental import pallas as pl
from jax.experimental.pallas import tpu as pltpu
from jax.sharding import Mesh
from jax.sharding import PartitionSpec as P

HEAD_DIM = 128


def layout(lengths, languages, frame_count):
    utterances = jnp.arange(lengths.shape[-1], dtype=jnp.int32)
    earlier = utterances[:, None] <= utterances[None, :]
    finish = jnp.sum(jnp.where(earlier[None], lengths[:, :, None], 0), axis=1)
    begins = finish - lengths
    indices = jnp.arange(frame_count, dtype=jnp.int32)
    segment = jnp.sum((indices[None, :, None] >= finish[:, None, :]).astype(jnp.int32), axis=-1)
    owners = segment[:, :, None] == jnp.arange(lengths.shape[-1], dtype=jnp.int32)[None, None, :]
    first_row = jnp.sum(jnp.where(owners, begins[:, None, :], 0), axis=-1)
    language_row = jnp.sum(jnp.where(owners, languages[:, None, :], 0), axis=-1)
    return (segment, indices[None, :] - first_row, language_row)


def angles(position):
    half_dim = HEAD_DIM // 2
    frequency = 10000.0 ** (-jnp.arange(half_dim, dtype=jnp.float32) / half_dim)
    turned = position.astype(jnp.float32)[..., None] * frequency
    return (jnp.cos(turned)[..., None, :], jnp.sin(turned)[..., None, :])


VMEM_SPACE = pl.BlockSpec(memory_space=pltpu.VMEM)
SMEM_SPACE = pl.BlockSpec(memory_space=pltpu.SMEM)
ANY_SPACE = pl.BlockSpec(memory_space=pl.ANY)


class Order:
    def __init__(self, value):
        self.value, self.waits = value, []

    def wait(self, *arrays):
        self.waits += arrays

    def call(self, kernel, out_shape, in_specs, out_specs, scratch_shapes, operands, through=(), lazy=False):
        after, self.waits = self.waits, []
        carried = [*through, self.value]
        count, outs, extra = len(operands), len(out_shape), len(after)
        held_in = [i for i in range(count) if in_specs[i] is VMEM_SPACE]
        held_out = [i for i in range(outs) if out_specs[i] is VMEM_SPACE]
        buffers = [pltpu.VMEM(operands[i].shape, operands[i].dtype) for i in held_in]
        buffers += [pltpu.VMEM(out_shape[i].shape, out_shape[i].dtype) for i in held_out]
        copies = max(1, len(held_in), len(held_out))

        def body(*refs):
            ins, rest = list(refs[:count]), refs[count + extra + len(carried) :]
            results, rest = list(rest[:outs]), rest[outs + len(carried) :]
            held, scratch, sems = rest[: len(buffers)], rest[len(buffers) : -1], rest[-1]
            moves = []
            for at, i in enumerate(held_in):
                moves.append(pltpu.make_async_copy(ins[i], held[at], sems.at[at]))
                moves[-1].start()
                ins[i] = held[at]
            targets = []
            for at, i in enumerate(held_out):
                targets.append(results[i])
                results[i] = held[len(held_in) + at]
            def ready():
                for move in arriving:
                    move.wait()

            arriving = moves
            if lazy:
                kernel(ready, *ins, *results, *scratch)
            else:
                ready()
                kernel(*ins, *results, *scratch)
            moves = []
            for at, i in enumerate(held_out):
                moves.append(pltpu.make_async_copy(results[i], targets[at], sems.at[at]))
                moves[-1].start()
            for move in moves:
                move.wait()

        result = pl.pallas_call(
            body,
            out_shape=[*out_shape, *[jax.ShapeDtypeStruct(x.shape, x.dtype) for x in carried]],
            in_specs=[ANY_SPACE if s is VMEM_SPACE else s for s in in_specs]
            + [ANY_SPACE] * (extra + len(carried)),
            out_specs=[ANY_SPACE] * (outs + len(carried)),
            scratch_shapes=[*buffers, *scratch_shapes, pltpu.SemaphoreType.DMA((copies,))],
            input_output_aliases={count + extra + i: outs + i for i in range(len(carried))},
            compiler_params=pltpu.CompilerParams(vmem_limit_bytes=VMEM_LIMIT),
        )(*operands, *after, *carried)
        self.value = result[-1]
        return result[:-1]


VMEM_LIMIT = 60 * 1024 * 1024
QUARTERS = 4
LANES = 128
BITS = (0, 1)


def swap_dp(value, bit, size):
    return lax.ppermute(value, "dp", [(i, i ^ (1 << bit)) for i in range(size)])


def swap_core(value):
    return lax.ppermute(value, "core", [(0, 1), (1, 0)])


def swap_pairs(value, flip, size):
    pairs = []
    for i in range(size):
        for core in range(2):
            far = i ^ (1 << BITS[core ^ flip])
            pairs.append((2 * i + core, 2 * far + core))
    return lax.ppermute(value, ("dp", "core"), pairs)


def pick_kernel(layers, base, place, gathered, out, sems):
    layer = place[1]
    rows, copies = gathered.shape[1], []
    for k in range(1, layers):
        for lane in range(2):
            at = 2 * (k - 1) + lane
            row = lax.rem(layer + k, layers) * 2 + lane
            source = gathered.at[row, :, pl.ds(base, out.shape[1])]
            target = out.at[pl.ds(at * rows, rows)]
            copies.append(pltpu.make_async_copy(source, target, sems.at[at]))
            copies[-1].start()
    for copy in copies:
        copy.wait()


def pick(order, place, layers, gathered, base, width, margin):
    blocks = 2 * (layers - 1)
    return order.call(
        functools.partial(pick_kernel, layers, base),
        [jax.ShapeDtypeStruct((blocks * gathered.shape[1] + margin, width), gathered.dtype)],
        [SMEM_SPACE, ANY_SPACE],
        [VMEM_SPACE],
        [pltpu.SemaphoreType.DMA((blocks,))],
        [place, gathered],
    )[0]


def half_kernel(place, piece, out, sems):
    rows = out.shape[0]
    start = pl.multiple_of(place[2] * rows, rows)
    copy = pltpu.make_async_copy(piece.at[pl.ds(start, rows)], out, sems.at[0])
    copy.start()
    copy.wait()


def half(order, place, piece, rows):
    return order.call(
        half_kernel,
        [jax.ShapeDtypeStruct((rows // 2, piece.shape[1]), piece.dtype)],
        [SMEM_SPACE, ANY_SPACE],
        [VMEM_SPACE],
        [pltpu.SemaphoreType.DMA((1,))],
        [place, piece],
    )[0]


def join_kernel(*refs):
    ins, out, sems = refs[:-2], refs[-2], refs[-1]
    at, copies = 0, []
    for k, ref in enumerate(ins):
        target = out.at[:, pl.ds(at, ref.shape[1])]
        copies.append(pltpu.make_async_copy(ref, target, sems.at[k]))
        copies[-1].start()
        at += ref.shape[1]
    for copy in copies:
        copy.wait()


def join(order, arrays):
    width = sum(a.shape[1] for a in arrays)
    return order.call(
        join_kernel,
        [jax.ShapeDtypeStruct((arrays[0].shape[0], width), arrays[0].dtype)],
        [ANY_SPACE] * len(arrays),
        [VMEM_SPACE],
        [pltpu.SemaphoreType.DMA((len(arrays),))],
        arrays,
    )[0]


class Packed:
    def __init__(self, arrays):
        self.own = list(arrays)
        self.all = [*self.own, *[swap_core(a) for a in self.own]]
        self.tokens = sum(a.shape[1] for a in self.all)

    def part(self, index):
        return [(a, index, a.shape[1]) for a in self.all]


class Factor:
    def __init__(self, left, left_index, right, right_index, base, width, relative=True):
        self.left = left.part(left_index)
        self.right, self.right_index, self.base, self.relative = right, right_index, base, relative
        self.width, self.part, self.tokens = width, width // QUARTERS, left.tokens
        self.arrays = [*left.all, *right.all]

    def columns(self, quarter, r, start, width):
        if self.relative:
            index, column = self.right_index + r, pl.ds(self.base + start, width)
        else:
            index = self.right_index
            column = pl.ds(pl.multiple_of((quarter ^ r) * self.part + start, LANES), width)
        return [(a, index, column, count) for a, _, count in self.right.part(0)]


class Sums:
    def __init__(self, *factors):
        self.factors = factors
        self.width = sum(f.part for f in factors)

    def spans(self):
        base = 0
        for i, f in enumerate(self.factors):
            for start in range(0, f.part, TILE):
                yield i, start, min(TILE, f.part - start), base + start
            base += f.part


TILE = 512


def left_width(features, layers):
    return features // 2 if features // (2 * layers) % LANES == 0 else features


def left_spans(features, layers, core):
    rows = features // (2 * layers)
    if rows % LANES:
        return [(pl.ds(0, features), pl.ds(0, features))]
    return [
        (pl.ds(pl.multiple_of((2 * k + core) * rows, rows), rows), pl.ds(k * rows, rows))
        for k in range(layers)
    ]


def own_rows(values, features, layers, core):
    tokens, width = values.shape
    if width < features:
        return values.T
    rows = features // (2 * layers)
    turned = values.T.reshape(layers, 2, rows, tokens)
    return jnp.where(core == 0, turned[:, 0], turned[:, 1]).reshape(layers * rows, tokens)


def round_kernel(layers, plan, tables, place, *refs):
    jobs, lefts, count_in, count_out = plan
    ins, outs = refs[:count_in], refs[count_in : count_in + count_out]
    left_buffer, turned, right_buffer, add_buffer, out_buffer, left_sems, in_sems, out_sems = refs[
        count_in + count_out :
    ]
    quarter, core = place[0], place[2]

    quarters = {"both": 3, "near": 1 + core, "far": 2 - core, "own": 0}

    def start(source, target, sem):
        copy = pltpu.make_async_copy(source, target, sem)
        copy.start()
        return copy

    left_copies = []
    for i, factor in enumerate(lefts):
        at, copies = 0, []
        for k, (array, index, rows) in enumerate(factor.left):
            source = ins[tables[id(array)]].at[index]
            spans = left_spans(source.shape[1], layers, core)
            for number, (columns, there) in enumerate(spans):
                target = left_buffer.at[i, at : at + rows, there]
                sem = left_sems.at[i, k * len(spans) + number]
                copies.append(start(source.at[:, columns], target, sem))
            at += rows
        left_copies.append(copies)
    loads = []
    for number, (i, r, first, width, adds, _) in enumerate(jobs):
        at, copies = 0, []
        for array, index, column, rows in lefts[i].columns(quarter, quarters[r], first, width):
            source = ins[tables[id(array)]].at[index, :, column]
            target = right_buffer.at[number, at : at + rows, pl.ds(0, width)]
            copies.append(start(source, target, in_sems.at[number, len(copies)]))
            at += rows
        for k, (array, column) in enumerate(adds):
            height = add_buffer.shape[2]
            source = ins[tables[id(array)]].at[pl.ds(0, height), pl.ds(column, width)]
            target = add_buffer.at[number, k, :, pl.ds(0, width)]
            copies.append(start(source, target, in_sems.at[number, len(copies)]))
        loads.append(copies)
    for i, factor in enumerate(lefts):
        for copy in left_copies[i]:
            copy.wait()
        turned[i, :, : factor.tokens] = own_rows(
            left_buffer[i, : factor.tokens], factor.left[0][0].shape[2], layers, core
        )
    stores = []
    for number, (i, _, _, width, adds, (out, column)) in enumerate(jobs):
        tokens = lefts[i].tokens
        for copy in loads[number]:
            copy.wait()
        product = jnp.dot(
            turned[i, :, :tokens],
            right_buffer[number, :tokens, :width],
            preferred_element_type=jnp.float32,
        )
        for k in range(len(adds)):
            product += add_buffer[number, k, :, :width].astype(jnp.float32)
        out_buffer[number, :, :width] = product.astype(jnp.bfloat16)
        source = out_buffer.at[number, :, pl.ds(0, width)]
        target = outs[out].at[pl.ds(0, out_buffer.shape[1]), pl.ds(column, width)]
        stores.append(start(source, target, out_sems.at[number]))
    for copy in stores:
        copy.wait()


class Rounds:
    def __init__(self, place, sizes, order):
        self.place, self.order = place, order
        self.dp_size, self.layers = sizes

    def step(self, halves=(), quarters=(), rows=(), margin=0):
        lefts, jobs, widths = [], [], [0] * (2 + len(rows))

        def left(factor):
            if factor not in lefts:
                lefts.append(factor)
            return lefts.index(factor)

        def add(sums, r, out, adds):
            base = widths[out]
            for i, first, width, at in sums.spans():
                mine = [(array, offset + at) for array, offset in adds]
                jobs.append((left(sums.factors[i]), r, first, width, mine, (out, base + at)))
            widths[out] += sums.width
            return base

        sent = []
        for sums in halves:
            sums.near_at = add(sums, "both", 0, [])
            sums.own_at = add(sums, "near", 0, [])
        for sums in quarters:
            sums.far_at = add(sums, "far", 1, [(sums.halves, sums.near_at)])
        for number, sums in enumerate(rows):
            add(sums, "own", 2 + number, [(sums.halves, sums.own_at), (sums.quarters, sums.far_at)])
        slots = [k for k in range(2 + len(rows)) if widths[k]]
        jobs = [job[:5] + ((slots.index(job[5][0]), job[5][1]),) for job in jobs]
        arrays, tables = [], {}
        used = [a for factor in lefts for a in factor.arrays] + [a for job in jobs for a, _ in job[4]]
        for array in used:
            if id(array) not in tables:
                tables[id(array)] = len(arrays)
                arrays.append(array)
        height = lefts[0].left[0][0].shape[2] // 2
        features = lefts[0].left[0][0].shape[2]
        tokens = max(factor.tokens for factor in lefts)
        widest = max(job[3] for job in jobs)
        depth = max(1, max(len(job[4]) for job in jobs))
        pieces = max(len(factor.left) for factor in lefts)
        rights = max(len(factor.right.all) for factor in lefts)
        outs = self.order.call(
            functools.partial(
                round_kernel, self.layers, (jobs, lefts, len(arrays), len(slots)), tables
            ),
            [
                jax.ShapeDtypeStruct((height + (margin if k == 0 else 0), widths[k]), jnp.bfloat16)
                for k in slots
            ],
            [SMEM_SPACE] + [ANY_SPACE] * len(arrays),
            [ANY_SPACE] * len(slots),
            [
                pltpu.VMEM(
                    (len(lefts), tokens, left_width(features, self.layers)), jnp.bfloat16
                ),
                pltpu.VMEM((len(lefts), height, tokens), jnp.bfloat16),
                pltpu.VMEM((len(jobs), tokens, widest), jnp.bfloat16),
                pltpu.VMEM((len(jobs), depth, height, widest), jnp.bfloat16),
                pltpu.VMEM((len(jobs), height, widest), jnp.bfloat16),
                pltpu.SemaphoreType.DMA((len(lefts), pieces * self.layers)),
                pltpu.SemaphoreType.DMA((len(jobs), rights + depth)),
                pltpu.SemaphoreType.DMA((len(jobs),)),
            ],
            [self.place, *arrays],
        )
        moved = {k: swap_pairs(outs[slots.index(k)], k, self.dp_size) for k in slots if k < 2}
        for sums in halves:
            sums.halves = moved[0]
        for sums in quarters:
            sums.quarters = moved[1]
        return [
            lax.psum_scatter(outs[slots.index(k)], "z", scatter_dimension=0, tiled=True)
            for k in slots
            if k >= 2
        ]

    def share(self, mine):
        summed = join(self.order, mine)
        bit = len(BITS)
        while 1 << bit < self.dp_size:
            summed = summed + swap_dp(summed, bit, self.dp_size)
            bit += 1
        near = swap_pairs(summed, 0, self.dp_size)
        far = swap_pairs(summed, 1, self.dp_size)
        return [summed, near, far, swap_pairs(near, 1, self.dp_size)]


def spread_kernel(widths, place, *refs):
    pieces, outs = refs[:QUARTERS], refs[QUARTERS:]
    quarter, core = place[0], place[2]
    base = 0
    for i, width in enumerate(widths):
        part = width // QUARTERS
        for r, place_of in enumerate((0, 1 + core, 2 - core, 3)):
            column = pl.ds(pl.multiple_of((quarter ^ place_of) * part, part), part)
            outs[i][:, column] = pieces[r][:, pl.ds(base, part)].astype(jnp.float32)
        base += part


def spread(order, place, widths, pieces):
    rows = pieces[0].shape[0]
    return order.call(
        functools.partial(spread_kernel, widths),
        [jax.ShapeDtypeStruct((rows, w), jnp.float32) for w in widths],
        [SMEM_SPACE] + [VMEM_SPACE] * QUARTERS,
        [VMEM_SPACE] * len(widths),
        [],
        [place, *pieces],
    )


class GatherSet:
    def __init__(self, place, groups):
        quarter = place[0]
        mine = [
            lax.dynamic_slice_in_dim(w, quarter * (w.shape[1] // QUARTERS), w.shape[1] // QUARTERS, 1)
            for group in groups
            for w in group
        ]
        mine = jnp.concatenate(mine, axis=1) if len(mine) > 1 else mine[0]
        self.gathered = lax.all_gather(mine, ("z", "core"), axis=0, tiled=False)


class Gather:
    def __init__(self, place, sizes, order, group, source, base, other, other_base):
        self.place, self.order, self.group = place, order, group
        self.dp_size, self.layers = sizes
        self.source, self.base, self.other, self.other_base = source, base, other, other_base
        self.width = sum(w.shape[1] for w in group) // QUARTERS
        self.rows = 2 * (self.layers - 1) * group[0].shape[0]

    def near(self, margin):
        piece = pick(
            self.order, self.place, self.layers, self.source.gathered, self.base, self.width, margin
        )
        self.piece = swap_pairs(piece, 0, self.dp_size)
        self.other_piece = swap_core(self.piece)

    def arrived(self):
        return [self.other_piece, self.rest, self.other_rest]

    def far(self):
        self.rest = swap_pairs(half(self.order, self.place, self.piece, self.rows), 1, self.dp_size)
        self.other_rest = swap_core(self.rest)


def gather_small(arrays):
    rows = [a.shape[0] for a in arrays]
    packed = jnp.concatenate(arrays, axis=0)
    packed = jnp.pad(packed, ((0, -packed.shape[0] % 16), (0, 0)))
    full = lax.all_gather(packed, ("z", "core"), axis=0, tiled=False)
    full = full.transpose(1, 0, 2).reshape(packed.shape[0], -1)
    pieces, start = [], 0
    for count in rows:
        pieces.append(full[start : start + count])
        start += count
    return pieces


def pack_small(table_hot, frames_grad, vectors):
    count = table_hot.shape[1]
    extra = -(frames_grad.shape[0] + vectors.shape[0]) % 16
    left = jnp.concatenate([frames_grad, vectors, jnp.zeros((extra, vectors.shape[1]), vectors.dtype)])
    used = count + vectors.shape[0]
    share = -(-used // QUARTERS)
    unit = jnp.eye(vectors.shape[0], dtype=table_hot.dtype)
    right = jnp.block(
        [
            [table_hot, jnp.zeros((table_hot.shape[0], vectors.shape[0]), table_hot.dtype)],
            [jnp.zeros((vectors.shape[0], count), table_hot.dtype), unit],
        ]
    )
    right = jnp.pad(right, ((0, extra), (0, share * QUARTERS - used)))
    right = right.reshape(right.shape[0], QUARTERS, share)
    right = jnp.pad(right, ((0, 0), (0, 0), (0, LANES - share)))
    right = right.reshape(right.shape[0], QUARTERS * LANES)
    right = jnp.pad(right, ((0, 0), (0, left.shape[1] - right.shape[1])))
    return jnp.stack([left.astype(jnp.bfloat16), right.astype(jnp.bfloat16)])


def unpack_small(summed, counts):
    used = sum(counts)
    share = -(-used // QUARTERS)
    rows = summed.reshape(summed.shape[0], QUARTERS, LANES)[:, :, :share]
    rows = rows.reshape(summed.shape[0], QUARTERS * share).T
    pieces, start = [], 0
    for count in counts:
        pieces.append(rows[start : start + count])
        start += count
    return pieces

EPSILON = 1e-05
MASKED = -1000000000.0


def dot_rows(left, right):
    return jnp.dot(left, right, preferred_element_type=jnp.float32)


def dot_cols(left, right):
    return lax.dot_general(
        left, right, (((1,), (1,)), ((), ())), preferred_element_type=jnp.float32
    )


def dot_down(left, right):
    return jnp.dot(left.T, right, preferred_element_type=jnp.float32)


def standard(values):
    centred = values - jnp.mean(values, axis=-1, keepdims=True)
    spread = lax.rsqrt(jnp.mean(centred * centred, axis=-1, keepdims=True) + EPSILON)
    return centred * spread, spread


def norm_back(values, gradient, gain):
    shape, spread = standard(values)
    inner = gradient * gain
    back = spread * (
        inner
        - jnp.mean(inner, axis=-1, keepdims=True)
        - shape * jnp.mean(inner * shape, axis=-1, keepdims=True)
    )
    return (
        back,
        jnp.sum(gradient * shape, axis=0, keepdims=True),
        jnp.sum(gradient, axis=0, keepdims=True),
    )


def sigmoid(values):
    return 1.0 / (1.0 + jnp.exp(-values))


def silu_back(values, gradient):
    gate = sigmoid(values)
    return gradient * gate * (1.0 + values * (1.0 - gate))


CUTS = 2


def packed_shapes(parts, tokens, width):
    return [jax.ShapeDtypeStruct((parts, tokens // CUTS, width), jnp.bfloat16)] * CUTS


def store_part(outs, index, values, column=slice(None)):
    at = 0
    for out in outs:
        out[index, :, column] = values[at : at + out.shape[1]]
        at += out.shape[1]


def load_part(refs, index, width):
    return jnp.concatenate([ref[index, :, :width] for ref in refs], axis=0)


class Pieces:
    def __init__(self, gather, index):
        group = gather.group
        self.layers = gather.layers
        before = sum(w.shape[1] for w in group[:index])
        self.base = before // QUARTERS
        self.set_base = gather.base + self.base
        self.other_base = gather.other_base + before
        self.rows, self.width = group[index].shape
        self.operands = [
            group[index],
            gather.other,
            gather.source.gathered,
            gather.piece,
            gather.other_piece,
            gather.rest,
            gather.other_rest,
        ]

    @property
    def part(self):
        return self.width // QUARTERS

    @property
    def scratch(self):
        copies = 1 + (QUARTERS - 1) * 2 * self.layers
        return [
            pltpu.VMEM((QUARTERS, 2 * self.layers, self.rows, self.part), jnp.bfloat16),
            pltpu.SemaphoreType.DMA((copies,)),
        ]

    def load(self, place, refs, buffer, sems):
        own, other, gathered, piece, other_piece, rest, other_rest = refs
        quarter, layer, core = place[0], place[1], place[2]
        span = pl.ds(self.base, self.part)
        copies = []

        def move(source, target):
            copies.append(pltpu.make_async_copy(source, target, sems.at[len(copies)]))
            copies[-1].start()

        def blocks(source, index, first, count):
            for number in range(count):
                at = first + number
                row = lax.rem(layer + 1 + at // 2, self.layers) * 2 + lax.rem(at, 2)
                move(source.at[pl.ds(number * self.rows, self.rows), span], buffer.at[index, row])

        move(gathered.at[:, :, pl.ds(self.set_base, self.part)], buffer.at[quarter])
        for r in range(1, QUARTERS):
            index = quarter ^ r
            near = pl.multiple_of(index * self.part, LANES)
            far = pl.multiple_of(self.other_base + index * self.part, LANES)
            move(own.at[:, pl.ds(near, self.part)], buffer.at[index, 2 * layer + core])
            move(other.at[:, pl.ds(far, self.part)], buffer.at[index, 2 * layer + 1 - core])
        count = 2 * (self.layers - 1)
        blocks(piece, quarter ^ (1 + core), jnp.int32(0), count)
        blocks(other_piece, quarter ^ (2 - core), jnp.int32(0), count)
        blocks(rest, quarter ^ 3, core * (count // 2), count // 2)
        blocks(other_rest, quarter ^ 3, (1 - core) * (count // 2), count // 2)
        return [(quarter, copies[:1]), (quarter ^ 1, copies[1:]), (quarter ^ 2, []), (quarter ^ 3, [])]

    def block(self, buffer, index):
        return buffer[index].reshape(2 * self.layers * self.rows, self.part)


def wait_all(steps):
    for _, copies in steps:
        for copy in copies:
            copy.wait()


def up_kernel(pieces, row, ready, place, values, gains, shifts, *refs):
    weight, outs, (buffer, sems) = refs[: -3 - CUTS], refs[-3 - CUTS : -2], refs[-2:]
    expanded_out, packed = outs[0], outs[1:]
    steps = pieces.load(place, weight, buffer, sems)
    ready()
    shape, _ = standard(values[...])
    hidden = (shape * gains[row : row + 1] + shifts[row : row + 1]).astype(jnp.bfloat16)
    store_part(packed, 0, hidden)
    for r, (index, copies) in enumerate(steps):
        for copy in copies:
            copy.wait()
        expanded = dot_rows(hidden, pieces.block(buffer, index))
        expanded_out[r] = expanded.astype(jnp.bfloat16)
        store_part(packed, 1 + r, (expanded * sigmoid(expanded)).astype(jnp.bfloat16))


def up_step(order, place, gather, index, row, values, gains, shifts):
    pieces = Pieces(gather, index)
    tokens, width = values.shape
    expanded, *packed = order.call(
        functools.partial(up_kernel, pieces, row),
        [
            jax.ShapeDtypeStruct((QUARTERS, tokens, pieces.part), jnp.bfloat16),
            *packed_shapes(1 + QUARTERS, tokens, width),
        ],
        [SMEM_SPACE] + [VMEM_SPACE] * 3 + [ANY_SPACE] * len(pieces.operands),
        [VMEM_SPACE] * (1 + CUTS),
        pieces.scratch,
        [place, values, gains, shifts, *pieces.operands],
        lazy=True,
    )
    return expanded, packed


def down_sum(pieces, ready, place, packed, first, weight, buffer, sems):
    total, steps = None, pieces.load(place, weight, buffer, sems)
    ready()
    for r, (index, copies) in enumerate(steps):
        for copy in copies:
            copy.wait()
        term = dot_cols(
            load_part(packed, first + r, pieces.part), pieces.block(buffer, index)
        )
        total = term if total is None else total + term
    return total


def down_kernel(pieces, ready, place, values, *refs):
    active, weight, (out, buffer, sems) = refs[:CUTS], refs[CUTS:-3], refs[-3:]
    branch = down_sum(pieces, ready, place, active, 1, weight, buffer, sems)
    out[...] = values[...] + 0.5 * branch


def down_step(order, place, gather, index, values, active):
    pieces = Pieces(gather, index)
    return order.call(
        functools.partial(down_kernel, pieces),
        [jax.ShapeDtypeStruct(values.shape, jnp.float32)],
        [SMEM_SPACE] + [VMEM_SPACE] * (1 + CUTS) + [ANY_SPACE] * len(pieces.operands),
        [VMEM_SPACE],
        pieces.scratch,
        [place, values, *active, *pieces.operands],
        lazy=True,
    )[0]


def last_kernel(pieces, row, ready, place, values, cotangent, gains, shifts, *refs):
    active, weight, outs = refs[:CUTS], refs[CUTS:-7], refs[-7:]
    encoded, grad_out, low_out, gain_out, shift_out, buffer, sems = outs
    branch = down_sum(pieces, ready, place, active, 1, weight, buffer, sems)
    total = values[...] + 0.5 * branch
    gain = gains[row : row + 1]
    shape, _ = standard(total)
    encoded[...] = (shape * gain + shifts[row : row + 1]).astype(jnp.bfloat16)
    back, gain_grad, shift_grad = norm_back(total, cotangent[...].astype(jnp.float32), gain)
    grad_out[...] = back
    low_out[0] = (0.5 * back).astype(jnp.bfloat16)
    gain_out[...] = gain_grad
    shift_out[...] = shift_grad


def vector_shapes(width, count=2):
    return [jax.ShapeDtypeStruct((1, width), jnp.float32)] * count


def last_step(order, place, gather, index, row, values, active, cotangent, gains, shifts):
    pieces = Pieces(gather, index)
    return order.call(
        functools.partial(last_kernel, pieces, row),
        [
            jax.ShapeDtypeStruct(values.shape, jnp.bfloat16),
            jax.ShapeDtypeStruct(values.shape, jnp.float32),
            jax.ShapeDtypeStruct((1, *values.shape), jnp.bfloat16),
            *vector_shapes(values.shape[1]),
        ],
        [SMEM_SPACE] + [VMEM_SPACE] * (4 + CUTS) + [ANY_SPACE] * len(pieces.operands),
        [VMEM_SPACE] * 5,
        pieces.scratch,
        [place, values, cotangent, gains, shifts, *active, *pieces.operands],
        lazy=True,
    )


def down_back_kernel(pieces, ready, place, gradient, expanded, *refs):
    weight, outs, (buffer, sems) = refs[: -2 - CUTS], refs[-2 - CUTS : -2], refs[-2:]
    steps = pieces.load(place, weight, buffer, sems)
    ready()
    for r, (index, copies) in enumerate(steps):
        for copy in copies:
            copy.wait()
        active_grad = dot_rows(gradient[0], pieces.block(buffer, index))
        store_part(outs, r, silu_back(expanded[r].astype(jnp.float32), active_grad).astype(jnp.bfloat16))


def down_back_step(order, place, gather, index, gradient, expanded, through=()):
    pieces = Pieces(gather, index)
    return order.call(
        functools.partial(down_back_kernel, pieces),
        packed_shapes(QUARTERS, gradient.shape[1], pieces.part),
        [SMEM_SPACE] + [VMEM_SPACE] * 2 + [ANY_SPACE] * len(pieces.operands),
        [VMEM_SPACE] * CUTS,
        pieces.scratch,
        [place, gradient, expanded, *pieces.operands],
        through,
        lazy=True,
    )


def into_norm_kernel(pieces, first, row, scale, ready, place, values, residual, gains, *refs):
    gradient, refs = refs[:CUTS], refs[CUTS:]
    weight, (grad_out, low_out, gain_out, shift_out, buffer, sems) = refs[:-6], refs[-6:]
    hidden_grad = down_sum(pieces, ready, place, gradient, first, weight, buffer, sems)
    back, gain_grad, shift_grad = norm_back(values[...], hidden_grad, gains[row : row + 1])
    total = residual[...] + back
    grad_out[...] = total
    low_out[0] = (scale * total).astype(jnp.bfloat16)
    gain_out[...] = gain_grad
    shift_out[...] = shift_grad


def into_norm_step(
    order, place, gather, index, first, row, scale, gradient, values, residual, gains, through=()
):
    pieces = Pieces(gather, index)
    return order.call(
        functools.partial(into_norm_kernel, pieces, first, row, scale),
        [
            jax.ShapeDtypeStruct(values.shape, jnp.float32),
            jax.ShapeDtypeStruct((1, *values.shape), jnp.bfloat16),
            *vector_shapes(values.shape[1]),
        ],
        [SMEM_SPACE] + [VMEM_SPACE] * (3 + CUTS) + [ANY_SPACE] * len(pieces.operands),
        [VMEM_SPACE] * 4,
        pieces.scratch,
        [place, values, residual, gains, *gradient, *pieces.operands],
        through,
        lazy=True,
    )


def whole_weight(pieces, ready, place, weight, buffer, sems):
    steps = pieces.load(place, weight, buffer, sems)
    ready()
    wait_all(steps)


def turn(values, cosine, sine):
    return values * cosine + pltpu.roll(values, HEAD_DIM // 2, 1) * sine


def masked_scores(query, key, matching):
    return jnp.where(matching, dot_cols(query, key), MASKED)


def head(index):
    return slice(index * HEAD_DIM, (index + 1) * HEAD_DIM)


def attend_kernel(pieces, row, ready, place, values, gains, shifts, cosine, sine, down, across, *refs):
    weight, outs = refs[:-6], refs[-6:]
    turned_out, totals_out, packed, projected, buffer, sems = outs
    steps = pieces.load(place, weight, buffer, sems)
    ready()
    shape, _ = standard(values[...])
    hidden = (shape * gains[row : row + 1] + shifts[row : row + 1]).astype(jnp.bfloat16)
    packed[0] = hidden
    for index, copies in steps:
        for copy in copies:
            copy.wait()
        column = pl.ds(pl.multiple_of(index * pieces.part, pieces.part), pieces.part)
        projected[:, column] = dot_rows(hidden, pieces.block(buffer, index))
    heads = pieces.width // (3 * HEAD_DIM)
    matching = down[...] == across[...]
    for h in range(heads):
        query = turn(projected[:, head(h)], cosine[...], sine[...]) * HEAD_DIM ** (-0.5)
        key = turn(projected[:, head(heads + h)], cosine[...], sine[...])
        query, key = query.astype(jnp.bfloat16), key.astype(jnp.bfloat16)
        value = projected[:, head(2 * heads + h)].astype(jnp.bfloat16)
        turned_out[:, head(h)] = query
        turned_out[:, head(heads + h)] = key
        turned_out[:, head(2 * heads + h)] = value
        scores = masked_scores(query, key, matching)
        highest = jnp.max(scores, axis=-1, keepdims=True)
        powers = jnp.exp(scores - highest)
        total = jnp.sum(powers, axis=-1, keepdims=True)
        totals_out[:, h : h + 1] = highest + jnp.log(total)
        probs = (powers / total).astype(jnp.bfloat16)
        packed[1, :, head(h)] = dot_rows(probs, value).astype(jnp.bfloat16)


def attend_step(order, place, gather, index, row, values, gains, shifts, cosine, sine, down, across):
    pieces = Pieces(gather, index)
    tokens, width = values.shape
    heads = pieces.width // (3 * HEAD_DIM)
    return order.call(
        functools.partial(attend_kernel, pieces, row),
        [
            jax.ShapeDtypeStruct((tokens, pieces.width), jnp.bfloat16),
            jax.ShapeDtypeStruct((tokens, heads), jnp.float32),
            jax.ShapeDtypeStruct((2, tokens, width), jnp.bfloat16),
        ],
        [SMEM_SPACE] + [VMEM_SPACE] * 7 + [ANY_SPACE] * len(pieces.operands),
        [VMEM_SPACE] * 3,
        [pltpu.VMEM((tokens, pieces.width), jnp.float32), *pieces.scratch],
        [place, values, gains, shifts, cosine, sine, down, across, *pieces.operands],
        lazy=True,
    )


def to_quarters(place, outs, column, values):
    part = values.shape[1] // QUARTERS
    for r in range(QUARTERS):
        block = values[:, pl.ds(pl.multiple_of((place[0] ^ r) * part, part), part)]
        store_part(outs, r, block, slice(column, column + part))


def attend_back_kernel(pieces, ready, place, gradient, turned, totals, cosine, sine, down, across, *refs):
    weight, rest = refs[: -4 - CUTS], refs[-4 - CUTS :]
    outs, (out, mixed_grad, buffer, sems) = rest[:CUTS], rest[CUTS:]
    heads = turned.shape[1] // (3 * HEAD_DIM)
    whole_weight(pieces, ready, place, weight, buffer, sems)
    total = None
    for index in range(QUARTERS):
        column = slice(index * pieces.part, (index + 1) * pieces.part)
        term = dot_cols(gradient[0, :, column], pieces.block(buffer, index))
        total = term if total is None else total + term
    mixed_grad[...] = total.astype(jnp.bfloat16)
    matching = down[...] == across[...]
    for h in range(heads):
        query = turned[:, head(h)]
        key = turned[:, head(heads + h)]
        value = turned[:, head(2 * heads + h)]
        gradient_h = mixed_grad[:, head(h)]
        probs = jnp.exp(masked_scores(query, key, matching) - totals[:, h : h + 1])
        value_grad = dot_down(probs.astype(jnp.bfloat16), gradient_h)
        probs_grad = dot_cols(gradient_h, value)
        inner = jnp.sum(probs * probs_grad, axis=-1, keepdims=True)
        score_grad = (probs * (probs_grad - inner)).astype(jnp.bfloat16)
        query_grad = dot_rows(score_grad, key) * HEAD_DIM ** (-0.5)
        key_grad = dot_down(score_grad, query)
        out[:, head(h)] = turn(query_grad, cosine[...], -sine[...]).astype(jnp.bfloat16)
        out[:, head(heads + h)] = turn(key_grad, cosine[...], -sine[...]).astype(jnp.bfloat16)
        out[:, head(2 * heads + h)] = value_grad.astype(jnp.bfloat16)
    to_quarters(place, outs, 0, out)


def attend_back_step(order, place, gather, index, gradient, turned, totals, cosine, sine, down, across):
    pieces = Pieces(gather, index)
    return order.call(
        functools.partial(attend_back_kernel, pieces),
        packed_shapes(QUARTERS, turned.shape[0], turned.shape[1] // QUARTERS),
        [SMEM_SPACE] + [VMEM_SPACE] * 7 + [ANY_SPACE] * len(pieces.operands),
        [VMEM_SPACE] * CUTS,
        [
            pltpu.VMEM(turned.shape, jnp.bfloat16),
            pltpu.VMEM(gradient.shape[1:], jnp.bfloat16),
            *pieces.scratch,
        ],
        [place, gradient, turned, totals, cosine, sine, down, across, *pieces.operands],
        lazy=True,
    )


def rows_sum(pieces, buffer, left):
    return jnp.concatenate(
        [dot_rows(left, pieces.block(buffer, index)) for index in range(QUARTERS)], axis=1
    )


def shifted(values, amount):
    return values if amount == 0 else pltpu.roll(values, amount % values.shape[0], 0)


def merge_kernel(pieces, ready, place, values, mixed, *refs):
    weight, (out, buffer, sems) = refs[:-3], refs[-3:]
    whole_weight(pieces, ready, place, weight, buffer, sems)
    for index in range(QUARTERS):
        column = slice(index * pieces.part, (index + 1) * pieces.part)
        out[:, column] = values[:, column] + dot_rows(mixed[1], pieces.block(buffer, index))


def merge_step(order, place, gather, index, values, mixed):
    pieces = Pieces(gather, index)
    return order.call(
        functools.partial(merge_kernel, pieces),
        [jax.ShapeDtypeStruct(values.shape, jnp.float32)],
        [SMEM_SPACE] + [VMEM_SPACE] * 2 + [ANY_SPACE] * len(pieces.operands),
        [VMEM_SPACE],
        pieces.scratch,
        [place, values, mixed, *pieces.operands],
        lazy=True,
    )[0]


def conv_kernel(weights, row, ready, place, values, gains, shifts, taps, keep, *refs):
    count = len(weights[0].operands)
    operands = [refs[i * count : (i + 1) * count] for i in range(len(weights))]
    rest = refs[len(weights) * count :]
    done_out, doubled_out, filtered_out, packed = rest[:4]
    scratch = rest[4:]
    buffers = [scratch[2 * i : 2 * i + 2] for i in range(len(weights))]
    steps = [w.load(place, o, *b) for w, o, b in zip(weights, operands, buffers)]
    gating, pointwise = weights
    ready()
    shape, _ = standard(values[...])
    hidden = (shape * gains[row : row + 1] + shifts[row : row + 1]).astype(jnp.bfloat16)
    packed[0] = hidden
    wait_all(steps[0])
    doubled = rows_sum(gating, buffers[0][0], hidden)
    doubled_out[...] = doubled.astype(jnp.bfloat16)
    half = gating.width // 2
    gated = doubled[:, :half] * sigmoid(doubled[:, half:])
    reach = taps.shape[0] // 2
    filtered = None
    for k in range(taps.shape[0]):
        term = shifted(gated, reach - k) * keep[:, k : k + 1] * taps[k : k + 1]
        filtered = term if filtered is None else filtered + term
    filtered_out[...] = filtered
    shape, _ = standard(filtered)
    renormed = shape * gains[row + 1 : row + 2] + shifts[row + 1 : row + 2]
    active = (renormed * sigmoid(renormed)).astype(jnp.bfloat16)
    packed[1] = active
    wait_all(steps[1])
    for index in range(QUARTERS):
        column = slice(index * pointwise.part, (index + 1) * pointwise.part)
        term = dot_rows(active, pointwise.block(buffers[1][0], index))
        done_out[:, column] = values[:, column] + term


def conv_step(order, place, gather, row, values, gains, shifts, taps, keep):
    weights = [Pieces(gather, i) for i in range(2)]
    tokens, width = values.shape
    operands = [o for w in weights for o in w.operands]
    return order.call(
        functools.partial(conv_kernel, weights, row),
        [
            jax.ShapeDtypeStruct((tokens, width), jnp.float32),
            jax.ShapeDtypeStruct((tokens, weights[0].width), jnp.bfloat16),
            jax.ShapeDtypeStruct((tokens, weights[0].width // 2), jnp.float32),
            jax.ShapeDtypeStruct((2, tokens, width), jnp.bfloat16),
        ],
        [SMEM_SPACE] + [VMEM_SPACE] * 5 + [ANY_SPACE] * len(operands),
        [VMEM_SPACE] * 4,
        [s for w in weights for s in w.scratch],
        [place, values, gains, shifts, taps, keep, *operands],
        lazy=True,
    )


def conv_back_kernel(pieces, row, ready, place, gradient, filtered, doubled, gains, shifts, taps, keep, *refs):
    weight, rest = refs[: -6 - CUTS], refs[-6 - CUTS :]
    outs = rest[:CUTS]
    gain_out, shift_out, taps_out, doubled_grad, buffer, sems = rest[CUTS:]
    whole_weight(pieces, ready, place, weight, buffer, sems)
    total = None
    for index in range(QUARTERS):
        column = slice(index * pieces.part, (index + 1) * pieces.part)
        term = dot_cols(gradient[0, :, column], pieces.block(buffer, index))
        total = term if total is None else total + term
    gain = gains[row : row + 1]
    shape, _ = standard(filtered[...])
    renormed = shape * gain + shifts[row : row + 1]
    back, gain_grad, shift_grad = norm_back(filtered[...], silu_back(renormed, total), gain)
    gain_out[...] = gain_grad
    shift_out[...] = shift_grad
    half = doubled.shape[1] // 2
    gate = sigmoid(doubled[:, half:].astype(jnp.float32))
    gated = doubled[:, :half].astype(jnp.float32) * gate
    reach = taps.shape[0] // 2
    gated_grad = None
    for k in range(taps.shape[0]):
        kept = back * keep[:, k : k + 1]
        taps_out[k : k + 1] = jnp.sum(kept * shifted(gated, reach - k), axis=0, keepdims=True)
        term = shifted(kept, k - reach) * taps[k : k + 1]
        gated_grad = term if gated_grad is None else gated_grad + term
    doubled_grad[:, :half] = (gated_grad * gate).astype(jnp.bfloat16)
    doubled_grad[:, half:] = (gated_grad * gated * (1.0 - gate)).astype(jnp.bfloat16)
    to_quarters(place, outs, 0, doubled_grad)


def conv_back_step(order, place, gather, index, row, gradient, filtered, doubled, gains, shifts, taps, keep):
    pieces = Pieces(gather, index)
    width = filtered.shape[1]
    return order.call(
        functools.partial(conv_back_kernel, pieces, row),
        [
            *packed_shapes(QUARTERS, doubled.shape[0], doubled.shape[1] // QUARTERS),
            *vector_shapes(width),
            jax.ShapeDtypeStruct(taps.shape, jnp.float32),
        ],
        [SMEM_SPACE] + [VMEM_SPACE] * 7 + [ANY_SPACE] * len(pieces.operands),
        [VMEM_SPACE] * (3 + CUTS),
        [pltpu.VMEM(doubled.shape, jnp.bfloat16), *pieces.scratch],
        [place, gradient, filtered, doubled, gains, shifts, taps, keep, *pieces.operands],
        lazy=True,
    )


def shards(
    sizes,
    frames,
    lengths,
    languages,
    embedding,
    gains,
    shifts,
    firstup,
    firstdown,
    projection,
    merger,
    gating,
    kernel,
    pointwise,
    secondup,
    seconddown,
    cotangent,
):
    frame_count = frames.shape[0]
    dp_index = lax.axis_index("dp").astype(jnp.int32)
    place = jnp.stack(
        [
            lax.rem(dp_index, jnp.int32(QUARTERS)),
            lax.axis_index("z").astype(jnp.int32),
            lax.axis_index("core").astype(jnp.int32),
        ]
    )
    order = Order(frames)
    order_of_groups = (
        ([firstup], [firstdown]),
        ([projection, merger], [gating, pointwise]),
        ([secondup],),
        ([seconddown],),
    )
    sources = [GatherSet(place, groups) for groups in order_of_groups]
    everything = jnp.concatenate([w for s in order_of_groups for g in s for w in g], axis=1)
    everything_other = swap_core(everything)
    gathers, other_base = [], 0
    for source, groups in zip(sources, order_of_groups):
        base = 0
        for group in groups:
            gathers.append(
                Gather(place, sizes, order, group, source, base, everything_other, other_base)
            )
            base += gathers[-1].width
            other_base += QUARTERS * gathers[-1].width
    table_full, gain_full, shift_full, kernel_full = gather_small(
        [embedding, gains, shifts, kernel]
    )
    segment_all, position_all, language_all = layout(lengths, languages, frame_count)
    segment = segment_all[0]
    language_row = language_all[0]
    cosine, sine = angles(position_all[0])
    cosine = jnp.concatenate([cosine, cosine], axis=-1)[:, 0]
    sine = jnp.concatenate([-sine, sine], axis=-1)[:, 0]
    down, across = segment[:, None], segment[None, :]
    gain_rows = gain_full.astype(jnp.float32)
    shift_rows = shift_full.astype(jnp.float32)
    taps = kernel_full.astype(jnp.float32)
    reach = taps.shape[0] // 2
    segment_pad = jnp.pad(segment, (reach, reach), constant_values=-1)
    keep = jnp.stack(
        [segment_pad[k : k + frame_count] == segment for k in range(taps.shape[0])], axis=1
    ).astype(jnp.float32)
    language_hot = (
        language_row[:, None] == jnp.arange(table_full.shape[0], dtype=jnp.int32)[None, :]
    ).astype(jnp.float32)
    start_sum = frames.astype(jnp.float32) + jnp.dot(
        language_hot.astype(jnp.bfloat16), table_full, preferred_element_type=jnp.float32
    )

    gathers[0].near(80)
    gathers[1].near(64)
    order.wait(everything_other)
    gathers[0].far()
    order.wait(gathers[0].rest)
    gathers[2].near(48)
    gathers[1].far()
    gathers[3].near(32)
    first_expanded, first_packed = up_step(
        order, place, gathers[0], 0, 0, start_sum, gain_rows, shift_rows
    )
    gathers[2].far()
    gathers[4].near(16)
    after_first = down_step(order, place, gathers[1], 0, start_sum, first_packed)
    gathers[3].far()
    gathers[5].near(0)
    turned, totals, attend_packed = attend_step(
        order, place, gathers[2], 0, 1, after_first, gain_rows, shift_rows, cosine, sine, down, across
    )
    after_attention = merge_step(order, place, gathers[2], 1, after_first, attend_packed)
    gathers[4].far()
    after_conv, doubled, filtered, conv_packed = conv_step(
        order, place, gathers[3], 2, after_attention, gain_rows, shift_rows, taps, keep
    )
    gathers[5].far()
    second_expanded, second_packed = up_step(
        order, place, gathers[4], 0, 4, after_conv, gain_rows, shift_rows
    )
    second_forward = Packed(second_packed)
    encoded, grad_second, low_second, final_gain, final_shift = last_step(
        order,
        place,
        gathers[5],
        0,
        5,
        after_conv,
        second_packed,
        cotangent,
        gain_rows,
        shift_rows,
    )
    rounds = Rounds(place, sizes, order)

    low = Packed([low_second])
    down_two = Sums(Factor(low, 0, second_forward, 1, 0, seconddown.shape[1]))
    rounds.step([down_two], margin=80)
    *packed, first_packed_a, first_packed_b = down_back_step(
        order, place, gathers[5], 0, low_second, second_expanded, first_packed
    )
    backward, first_forward = Packed(packed), Packed([first_packed_a, first_packed_b])
    grad_conv, low_conv, second_gain, second_shift, *held = into_norm_step(
        order,
        place,
        gathers[4],
        0,
        0,
        4,
        1.0,
        packed,
        after_conv,
        grad_second,
        gain_rows,
        [conv_packed, attend_packed],
    )
    conv_forward, attend_forward = Packed(held[:1]), Packed(held[1:])
    up_two = Sums(Factor(second_forward, 0, backward, 0, 0, secondup.shape[1]))
    order.wait(*first_forward.all)
    rounds.step([up_two], margin=64)
    low = Packed([low_conv])
    order.wait(*conv_forward.all, *attend_forward.all)
    *packed, inner_gain, inner_shift, taps_grad = conv_back_step(
        order, place, gathers[3], 1, 3, low_conv, filtered, doubled, gain_rows, shift_rows, taps, keep
    )
    backward = Packed(packed)
    grad_attention, low_attention, outer_gain, outer_shift = into_norm_step(
        order,
        place,
        gathers[3],
        0,
        0,
        2,
        1.0,
        packed,
        after_attention,
        grad_conv,
        gain_rows,
    )
    conv = Sums(
        Factor(conv_forward, 0, backward, 0, 0, gating.shape[1]),
        Factor(conv_forward, 1, low, 0, 0, pointwise.shape[1], relative=False),
        Factor(attend_forward, 1, Packed([low_attention]), 0, 0, merger.shape[1], relative=False),
    )
    rounds.step([conv], [down_two], margin=48)
    packed = attend_back_step(
        order, place, gathers[2], 1, low_attention, turned, totals, cosine, sine, down, across
    )
    backward = Packed(packed)
    grad_first, low_first, attend_gain, attend_shift = into_norm_step(
        order,
        place,
        gathers[2],
        0,
        0,
        1,
        0.5,
        packed,
        after_first,
        grad_attention,
        gain_rows,
    )
    projection_factor = Factor(attend_forward, 0, backward, 0, 0, projection.shape[1])
    order.wait(*backward.all)
    low = Packed([low_first])
    packed = down_back_step(order, place, gathers[1], 0, low_first, first_expanded)
    backward = Packed(packed)
    down_one = Sums(Factor(low, 0, first_forward, 1, 0, firstdown.shape[1]))
    (down_two_mine,) = rounds.step([down_one], [up_two], [down_two], margin=32)
    frames_grad, low_start, first_gain, first_shift = into_norm_step(
        order, place, gathers[0], 0, 0, 0, 1.0, packed, start_sum, grad_first, gain_rows
    )
    up_one = Sums(Factor(first_forward, 0, backward, 0, 0, firstup.shape[1]))
    (up_two_mine,) = rounds.step([up_one], [conv], [up_two], margin=16)
    vectors = jnp.concatenate(
        [
            first_gain,
            attend_gain,
            outer_gain,
            inner_gain,
            second_gain,
            final_gain,
            first_shift,
            attend_shift,
            outer_shift,
            inner_shift,
            second_shift,
            final_shift,
            taps_grad,
        ]
    )
    small_packed = Packed([pack_small(language_hot, low_start[0], vectors)])
    last = Sums(
        projection_factor,
        Factor(small_packed, 0, small_packed, 1, 0, QUARTERS * LANES, relative=False),
    )
    order.wait(down_two_mine)
    (conv_mine,) = rounds.step([last], [down_one], [conv], margin=80)
    order.wait(up_two_mine)
    (down_one_mine,) = rounds.step([], [up_one], [down_one])
    order.wait(conv_mine)
    (up_one_mine,) = rounds.step([], [last], [up_one])
    pieces = rounds.share([down_two_mine, up_two_mine])
    order.wait(down_one_mine)
    (last_mine,) = rounds.step([], [], [last])
    middle_pieces = rounds.share([conv_mine, down_one_mine])
    seconddown_grad, secondup_grad = spread(
        order, place, [seconddown.shape[1], secondup.shape[1]], pieces
    )
    middle = [gating, pointwise, merger, firstdown]
    gating_grad, pointwise_grad, merger_grad, firstdown_grad = spread(
        order, place, [w.shape[1] for w in middle], middle_pieces
    )
    pieces = rounds.share([up_one_mine, last_mine])
    firstup_grad, projection_grad, small = spread(
        order, place, [firstup.shape[1], projection.shape[1], QUARTERS * LANES], pieces
    )
    counts = [embedding.shape[0], gains.shape[0], shifts.shape[0], kernel.shape[0]]
    table_sum, gain_sum, shift_sum, taps_sum = unpack_small(small, counts)
    return (
        encoded,
        frames_grad,
        table_sum,
        gain_sum,
        shift_sum,
        firstup_grad,
        firstdown_grad,
        projection_grad,
        merger_grad,
        gating_grad,
        taps_sum,
        pointwise_grad,
        secondup_grad,
        seconddown_grad,
    )


def solution(mesh):
    dp_size, fsdp_size = mesh.shape["dp"], mesh.shape["fsdp"]
    layers = fsdp_size // 2
    split = Mesh(mesh.devices.reshape(dp_size, layers, 2), ("dp", "z", "core"))
    return jax.shard_map(
        functools.partial(shards, (dp_size, layers)),
        mesh=split,
        in_specs=(
            P(("dp", "z", "core"), None),
            P(("dp", "z", "core"), None),
            P(("dp", "z", "core"), None),
            P(None, ("z", "core")),
            P(None, ("z", "core")),
            P(None, ("z", "core")),
            P(("z", "core"), None),
            P(("z", "core"), None),
            P(("z", "core"), None),
            P(("z", "core"), None),
            P(("z", "core"), None),
            P(None, ("z", "core")),
            P(("z", "core"), None),
            P(("z", "core"), None),
            P(("z", "core"), None),
            P(("dp", "z", "core"), None),
        ),
        out_specs=(
            P(("dp", "z", "core"), None),
            P(("dp", "z", "core"), None),
            P(None, ("z", "core")),
            P(None, ("z", "core")),
            P(None, ("z", "core")),
            P(("z", "core"), None),
            P(("z", "core"), None),
            P(("z", "core"), None),
            P(("z", "core"), None),
            P(("z", "core"), None),
            P(None, ("z", "core")),
            P(("z", "core"), None),
            P(("z", "core"), None),
            P(("z", "core"), None),
        ),
        check_vma=False,
    )
```

```python
import functools

import jax
import jax.numpy as jnp
import numpy as np
from jax import lax
from jax.experimental import pallas as pl
from jax.experimental.pallas import tpu as pltpu
from jax.sharding import Mesh
from jax.sharding import PartitionSpec as P

HEAD_DIM = 128


def layout(lengths, languages, frame_count):
    utterances = jnp.arange(lengths.shape[-1], dtype=jnp.int32)
    earlier = utterances[:, None] <= utterances[None, :]
    finish = jnp.sum(jnp.where(earlier[None], lengths[:, :, None], 0), axis=1)
    begins = finish - lengths
    indices = jnp.arange(frame_count, dtype=jnp.int32)
    segment = jnp.sum((indices[None, :, None] >= finish[:, None, :]).astype(jnp.int32), axis=-1)
    owners = segment[:, :, None] == jnp.arange(lengths.shape[-1], dtype=jnp.int32)[None, None, :]
    first_row = jnp.sum(jnp.where(owners, begins[:, None, :], 0), axis=-1)
    language_row = jnp.sum(jnp.where(owners, languages[:, None, :], 0), axis=-1)
    return (segment, indices[None, :] - first_row, language_row)


def angles(position):
    half_dim = HEAD_DIM // 2
    frequency = 10000.0 ** (-jnp.arange(half_dim, dtype=jnp.float32) / half_dim)
    turned = position.astype(jnp.float32)[..., None] * frequency
    return (jnp.cos(turned)[..., None, :], jnp.sin(turned)[..., None, :])


VMEM_SPACE = pl.BlockSpec(memory_space=pltpu.VMEM)
SMEM_SPACE = pl.BlockSpec(memory_space=pltpu.SMEM)
ANY_SPACE = pl.BlockSpec(memory_space=pl.ANY)


class Order:
    def __init__(self, value):
        self.value, self.waits = value, []

    def wait(self, *arrays):
        self.waits += arrays

    def call(self, kernel, out_shape, in_specs, out_specs, scratch_shapes, operands, through=(), lazy=False):
        after, self.waits = self.waits, []
        carried = [*through, self.value]
        count, outs, extra = len(operands), len(out_shape), len(after)
        held_in = [i for i in range(count) if in_specs[i] is VMEM_SPACE]
        held_out = [i for i in range(outs) if out_specs[i] is VMEM_SPACE]
        buffers = [pltpu.VMEM(operands[i].shape, operands[i].dtype) for i in held_in]
        buffers += [pltpu.VMEM(out_shape[i].shape, out_shape[i].dtype) for i in held_out]
        copies = max(1, len(held_in), len(held_out))

        def body(*refs):
            ins, rest = list(refs[:count]), refs[count + extra + len(carried) :]
            results, rest = list(rest[:outs]), rest[outs + len(carried) :]
            held, scratch, sems = rest[: len(buffers)], rest[len(buffers) : -1], rest[-1]
            moves = []
            for at, i in enumerate(held_in):
                moves.append(pltpu.make_async_copy(ins[i], held[at], sems.at[at]))
                moves[-1].start()
                ins[i] = held[at]
            targets = []
            for at, i in enumerate(held_out):
                targets.append(results[i])
                results[i] = held[len(held_in) + at]
            def ready():
                for move in arriving:
                    move.wait()

            arriving = moves
            if lazy:
                kernel(ready, *ins, *results, *scratch)
            else:
                ready()
                kernel(*ins, *results, *scratch)
            moves = []
            for at, i in enumerate(held_out):
                moves.append(pltpu.make_async_copy(results[i], targets[at], sems.at[at]))
                moves[-1].start()
            for move in moves:
                move.wait()

        result = pl.pallas_call(
            body,
            out_shape=[*out_shape, *[jax.ShapeDtypeStruct(x.shape, x.dtype) for x in carried]],
            in_specs=[ANY_SPACE if s is VMEM_SPACE else s for s in in_specs]
            + [ANY_SPACE] * (extra + len(carried)),
            out_specs=[ANY_SPACE] * (outs + len(carried)),
            scratch_shapes=[*buffers, *scratch_shapes, pltpu.SemaphoreType.DMA((copies,))],
            input_output_aliases={count + extra + i: outs + i for i in range(len(carried))},
            compiler_params=pltpu.CompilerParams(vmem_limit_bytes=VMEM_LIMIT),
        )(*operands, *after, *carried)
        self.value = result[-1]
        return result[:-1]


VMEM_LIMIT = 60 * 1024 * 1024
QUARTERS = 4
LANES = 128
BITS = (0, 1)


def swap_dp(value, bit, size):
    return lax.ppermute(value, "dp", [(i, i ^ (1 << bit)) for i in range(size)])


def swap_core(value):
    return lax.ppermute(value, "core", [(0, 1), (1, 0)])


def swap_pairs(value, flip, size):
    pairs = []
    for i in range(size):
        for core in range(2):
            far = i ^ (1 << BITS[core ^ flip])
            pairs.append((2 * i + core, 2 * far + core))
    return lax.ppermute(value, ("dp", "core"), pairs)


def pick_kernel(layers, base, place, gathered, out, sems):
    layer = place[1]
    rows, copies = gathered.shape[1], []
    for k in range(1, layers):
        for lane in range(2):
            at = 2 * (k - 1) + lane
            row = lax.rem(layer + k, layers) * 2 + lane
            source = gathered.at[row, :, pl.ds(base, out.shape[1])]
            target = out.at[pl.ds(at * rows, rows)]
            copies.append(pltpu.make_async_copy(source, target, sems.at[at]))
            copies[-1].start()
    for copy in copies:
        copy.wait()


def pick(order, place, layers, gathered, base, width, margin):
    blocks = 2 * (layers - 1)
    return order.call(
        functools.partial(pick_kernel, layers, base),
        [jax.ShapeDtypeStruct((blocks * gathered.shape[1] + margin, width), gathered.dtype)],
        [SMEM_SPACE, ANY_SPACE],
        [VMEM_SPACE],
        [pltpu.SemaphoreType.DMA((blocks,))],
        [place, gathered],
    )[0]


def half_kernel(place, piece, out, sems):
    rows = out.shape[0]
    start = pl.multiple_of(place[2] * rows, rows)
    copy = pltpu.make_async_copy(piece.at[pl.ds(start, rows)], out, sems.at[0])
    copy.start()
    copy.wait()


def half(order, place, piece, rows):
    return order.call(
        half_kernel,
        [jax.ShapeDtypeStruct((rows // 2, piece.shape[1]), piece.dtype)],
        [SMEM_SPACE, ANY_SPACE],
        [VMEM_SPACE],
        [pltpu.SemaphoreType.DMA((1,))],
        [place, piece],
    )[0]


def join_kernel(*refs):
    ins, out, sems = refs[:-2], refs[-2], refs[-1]
    at, copies = 0, []
    for k, ref in enumerate(ins):
        target = out.at[:, pl.ds(at, ref.shape[1])]
        copies.append(pltpu.make_async_copy(ref, target, sems.at[k]))
        copies[-1].start()
        at += ref.shape[1]
    for copy in copies:
        copy.wait()


def join(order, arrays):
    width = sum(a.shape[1] for a in arrays)
    return order.call(
        join_kernel,
        [jax.ShapeDtypeStruct((arrays[0].shape[0], width), arrays[0].dtype)],
        [ANY_SPACE] * len(arrays),
        [VMEM_SPACE],
        [pltpu.SemaphoreType.DMA((len(arrays),))],
        arrays,
    )[0]


class Packed:
    def __init__(self, arrays):
        self.own = list(arrays)
        self.all = [*self.own, *[swap_core(a) for a in self.own]]
        self.tokens = sum(a.shape[1] for a in self.all)

    def part(self, index):
        return [(a, index, a.shape[1]) for a in self.all]


class Factor:
    def __init__(self, left, left_index, right, right_index, base, width, relative=True):
        self.left = left.part(left_index)
        self.right, self.right_index, self.base, self.relative = right, right_index, base, relative
        self.width, self.part, self.tokens = width, width // QUARTERS, left.tokens
        self.arrays = [*left.all, *right.all]

    def columns(self, quarter, r, start, width):
        if self.relative:
            index, column = self.right_index + r, pl.ds(self.base + start, width)
        else:
            index = self.right_index
            column = pl.ds(pl.multiple_of((quarter ^ r) * self.part + start, LANES), width)
        return [(a, index, column, count) for a, _, count in self.right.part(0)]


class Sums:
    def __init__(self, *factors):
        self.factors = factors
        self.width = sum(f.part for f in factors)

    def spans(self):
        base = 0
        for i, f in enumerate(self.factors):
            for start in range(0, f.part, TILE):
                yield i, start, min(TILE, f.part - start), base + start
            base += f.part


TILE = 512


def left_width(features, layers):
    return features // 2 if features // (2 * layers) % LANES == 0 else features


def left_spans(features, layers, core):
    rows = features // (2 * layers)
    if rows % LANES:
        return [(pl.ds(0, features), pl.ds(0, features))]
    return [
        (pl.ds(pl.multiple_of((2 * k + core) * rows, rows), rows), pl.ds(k * rows, rows))
        for k in range(layers)
    ]


def own_rows(values, features, layers, core):
    tokens, width = values.shape
    if width < features:
        return values.T
    rows = features // (2 * layers)
    turned = values.T.reshape(layers, 2, rows, tokens)
    return jnp.where(core == 0, turned[:, 0], turned[:, 1]).reshape(layers * rows, tokens)


def round_kernel(layers, plan, tables, place, *refs):
    jobs, lefts, count_in, count_out = plan
    ins, outs = refs[:count_in], refs[count_in : count_in + count_out]
    left_buffer, turned, right_buffer, add_buffer, out_buffer, left_sems, in_sems, out_sems = refs[
        count_in + count_out :
    ]
    quarter, core = place[0], place[2]

    quarters = {"both": 3, "near": 1 + core, "far": 2 - core, "own": 0}

    def start(source, target, sem):
        copy = pltpu.make_async_copy(source, target, sem)
        copy.start()
        return copy

    left_copies = []
    for i, factor in enumerate(lefts):
        at, copies = 0, []
        for k, (array, index, rows) in enumerate(factor.left):
            source = ins[tables[id(array)]].at[index]
            spans = left_spans(source.shape[1], layers, core)
            for number, (columns, there) in enumerate(spans):
                target = left_buffer.at[i, at : at + rows, there]
                sem = left_sems.at[i, k * len(spans) + number]
                copies.append(start(source.at[:, columns], target, sem))
            at += rows
        left_copies.append(copies)
    loads = []
    for number, (i, r, first, width, adds, _) in enumerate(jobs):
        at, copies = 0, []
        for array, index, column, rows in lefts[i].columns(quarter, quarters[r], first, width):
            source = ins[tables[id(array)]].at[index, :, column]
            target = right_buffer.at[number, at : at + rows, pl.ds(0, width)]
            copies.append(start(source, target, in_sems.at[number, len(copies)]))
            at += rows
        for k, (array, column) in enumerate(adds):
            height = add_buffer.shape[2]
            source = ins[tables[id(array)]].at[pl.ds(0, height), pl.ds(column, width)]
            target = add_buffer.at[number, k, :, pl.ds(0, width)]
            copies.append(start(source, target, in_sems.at[number, len(copies)]))
        loads.append(copies)
    for i, factor in enumerate(lefts):
        for copy in left_copies[i]:
            copy.wait()
        turned[i, :, : factor.tokens] = own_rows(
            left_buffer[i, : factor.tokens], factor.left[0][0].shape[2], layers, core
        )
    stores = []
    for number, (i, _, _, width, adds, (out, column)) in enumerate(jobs):
        tokens = lefts[i].tokens
        for copy in loads[number]:
            copy.wait()
        product = jnp.dot(
            turned[i, :, :tokens],
            right_buffer[number, :tokens, :width],
            preferred_element_type=jnp.float32,
        )
        for k in range(len(adds)):
            product += add_buffer[number, k, :, :width].astype(jnp.float32)
        out_buffer[number, :, :width] = product.astype(jnp.bfloat16)
        source = out_buffer.at[number, :, pl.ds(0, width)]
        target = outs[out].at[pl.ds(0, out_buffer.shape[1]), pl.ds(column, width)]
        stores.append(start(source, target, out_sems.at[number]))
    for copy in stores:
        copy.wait()


class Rounds:
    def __init__(self, place, sizes, order):
        self.place, self.order = place, order
        self.dp_size, self.layers = sizes

    def step(self, halves=(), quarters=(), rows=(), margin=0):
        lefts, jobs, widths = [], [], [0] * (2 + len(rows))

        def left(factor):
            if factor not in lefts:
                lefts.append(factor)
            return lefts.index(factor)

        def add(sums, r, out, adds):
            base = widths[out]
            for i, first, width, at in sums.spans():
                mine = [(array, offset + at) for array, offset in adds]
                jobs.append((left(sums.factors[i]), r, first, width, mine, (out, base + at)))
            widths[out] += sums.width
            return base

        sent = []
        for sums in halves:
            sums.near_at = add(sums, "both", 0, [])
            sums.own_at = add(sums, "near", 0, [])
        for sums in quarters:
            sums.far_at = add(sums, "far", 1, [(sums.halves, sums.near_at)])
        for number, sums in enumerate(rows):
            add(sums, "own", 2 + number, [(sums.halves, sums.own_at), (sums.quarters, sums.far_at)])
        slots = [k for k in range(2 + len(rows)) if widths[k]]
        jobs = [job[:5] + ((slots.index(job[5][0]), job[5][1]),) for job in jobs]
        arrays, tables = [], {}
        used = [a for factor in lefts for a in factor.arrays] + [a for job in jobs for a, _ in job[4]]
        for array in used:
            if id(array) not in tables:
                tables[id(array)] = len(arrays)
                arrays.append(array)
        height = lefts[0].left[0][0].shape[2] // 2
        features = lefts[0].left[0][0].shape[2]
        tokens = max(factor.tokens for factor in lefts)
        widest = max(job[3] for job in jobs)
        depth = max(1, max(len(job[4]) for job in jobs))
        pieces = max(len(factor.left) for factor in lefts)
        rights = max(len(factor.right.all) for factor in lefts)
        outs = self.order.call(
            functools.partial(
                round_kernel, self.layers, (jobs, lefts, len(arrays), len(slots)), tables
            ),
            [
                jax.ShapeDtypeStruct((height + (margin if k == 0 else 0), widths[k]), jnp.bfloat16)
                for k in slots
            ],
            [SMEM_SPACE] + [ANY_SPACE] * len(arrays),
            [ANY_SPACE] * len(slots),
            [
                pltpu.VMEM(
                    (len(lefts), tokens, left_width(features, self.layers)), jnp.bfloat16
                ),
                pltpu.VMEM((len(lefts), height, tokens), jnp.bfloat16),
                pltpu.VMEM((len(jobs), tokens, widest), jnp.bfloat16),
                pltpu.VMEM((len(jobs), depth, height, widest), jnp.bfloat16),
                pltpu.VMEM((len(jobs), height, widest), jnp.bfloat16),
                pltpu.SemaphoreType.DMA((len(lefts), pieces * self.layers)),
                pltpu.SemaphoreType.DMA((len(jobs), rights + depth)),
                pltpu.SemaphoreType.DMA((len(jobs),)),
            ],
            [self.place, *arrays],
        )
        moved = {k: swap_pairs(outs[slots.index(k)], k, self.dp_size) for k in slots if k < 2}
        for sums in halves:
            sums.halves = moved[0]
        for sums in quarters:
            sums.quarters = moved[1]
        return [
            lax.psum_scatter(outs[slots.index(k)], "z", scatter_dimension=0, tiled=True)
            for k in slots
            if k >= 2
        ]

    def share(self, mine):
        summed = join(self.order, mine)
        bit = len(BITS)
        while 1 << bit < self.dp_size:
            summed = summed + swap_dp(summed, bit, self.dp_size)
            bit += 1
        near = swap_pairs(summed, 0, self.dp_size)
        far = swap_pairs(summed, 1, self.dp_size)
        return [summed, near, far, swap_pairs(near, 1, self.dp_size)]


def spread_kernel(widths, place, *refs):
    pieces, outs = refs[:QUARTERS], refs[QUARTERS:]
    quarter, core = place[0], place[2]
    base = 0
    for i, width in enumerate(widths):
        part = width // QUARTERS
        for r, place_of in enumerate((0, 1 + core, 2 - core, 3)):
            column = pl.ds(pl.multiple_of((quarter ^ place_of) * part, part), part)
            outs[i][:, column] = pieces[r][:, pl.ds(base, part)].astype(jnp.float32)
        base += part


def spread(order, place, widths, pieces):
    rows = pieces[0].shape[0]
    return order.call(
        functools.partial(spread_kernel, widths),
        [jax.ShapeDtypeStruct((rows, w), jnp.float32) for w in widths],
        [SMEM_SPACE] + [VMEM_SPACE] * QUARTERS,
        [VMEM_SPACE] * len(widths),
        [],
        [place, *pieces],
    )


class GatherSet:
    def __init__(self, place, groups):
        quarter = place[0]
        mine = [
            lax.dynamic_slice_in_dim(w, quarter * (w.shape[1] // QUARTERS), w.shape[1] // QUARTERS, 1)
            for group in groups
            for w in group
        ]
        mine = jnp.concatenate(mine, axis=1) if len(mine) > 1 else mine[0]
        self.gathered = lax.all_gather(mine, ("z", "core"), axis=0, tiled=False)


class Gather:
    def __init__(self, place, sizes, order, group, source, base, other, other_base):
        self.place, self.order, self.group = place, order, group
        self.dp_size, self.layers = sizes
        self.source, self.base, self.other, self.other_base = source, base, other, other_base
        self.width = sum(w.shape[1] for w in group) // QUARTERS
        self.rows = 2 * (self.layers - 1) * group[0].shape[0]

    def near(self, margin):
        piece = pick(
            self.order, self.place, self.layers, self.source.gathered, self.base, self.width, margin
        )
        self.piece = swap_pairs(piece, 0, self.dp_size)
        self.other_piece = swap_core(self.piece)

    def arrived(self):
        return [self.other_piece, self.rest, self.other_rest]

    def far(self):
        self.rest = swap_pairs(half(self.order, self.place, self.piece, self.rows), 1, self.dp_size)
        self.other_rest = swap_core(self.rest)


def gather_small(arrays):
    rows = [a.shape[0] for a in arrays]
    packed = jnp.concatenate(arrays, axis=0)
    packed = jnp.pad(packed, ((0, -packed.shape[0] % 16), (0, 0)))
    full = lax.all_gather(packed, ("z", "core"), axis=0, tiled=False)
    full = full.transpose(1, 0, 2).reshape(packed.shape[0], -1)
    pieces, start = [], 0
    for count in rows:
        pieces.append(full[start : start + count])
        start += count
    return pieces


def pack_small(table_hot, frames_grad, vectors):
    count = table_hot.shape[1]
    extra = -(frames_grad.shape[0] + vectors.shape[0]) % 16
    left = jnp.concatenate([frames_grad, vectors, jnp.zeros((extra, vectors.shape[1]), vectors.dtype)])
    used = count + vectors.shape[0]
    share = -(-used // QUARTERS)
    unit = jnp.eye(vectors.shape[0], dtype=table_hot.dtype)
    right = jnp.block(
        [
            [table_hot, jnp.zeros((table_hot.shape[0], vectors.shape[0]), table_hot.dtype)],
            [jnp.zeros((vectors.shape[0], count), table_hot.dtype), unit],
        ]
    )
    right = jnp.pad(right, ((0, extra), (0, share * QUARTERS - used)))
    right = right.reshape(right.shape[0], QUARTERS, share)
    right = jnp.pad(right, ((0, 0), (0, 0), (0, LANES - share)))
    right = right.reshape(right.shape[0], QUARTERS * LANES)
    right = jnp.pad(right, ((0, 0), (0, left.shape[1] - right.shape[1])))
    return jnp.stack([left.astype(jnp.bfloat16), right.astype(jnp.bfloat16)])


def unpack_small(summed, counts):
    used = sum(counts)
    share = -(-used // QUARTERS)
    rows = summed.reshape(summed.shape[0], QUARTERS, LANES)[:, :, :share]
    rows = rows.reshape(summed.shape[0], QUARTERS * share).T
    pieces, start = [], 0
    for count in counts:
        pieces.append(rows[start : start + count])
        start += count
    return pieces

EPSILON = 1e-05
MASKED = -1000000000.0


def dot_rows(left, right):
    return jnp.dot(left, right, preferred_element_type=jnp.float32)


def dot_cols(left, right):
    return lax.dot_general(
        left, right, (((1,), (1,)), ((), ())), preferred_element_type=jnp.float32
    )


def dot_down(left, right):
    return jnp.dot(left.T, right, preferred_element_type=jnp.float32)


def standard(values):
    centred = values - jnp.mean(values, axis=-1, keepdims=True)
    spread = lax.rsqrt(jnp.mean(centred * centred, axis=-1, keepdims=True) + EPSILON)
    return centred * spread, spread


def norm_back(values, gradient, gain):
    shape, spread = standard(values)
    inner = gradient * gain
    back = spread * (
        inner
        - jnp.mean(inner, axis=-1, keepdims=True)
        - shape * jnp.mean(inner * shape, axis=-1, keepdims=True)
    )
    return (
        back,
        jnp.sum(gradient * shape, axis=0, keepdims=True),
        jnp.sum(gradient, axis=0, keepdims=True),
    )


def sigmoid(values):
    return 1.0 / (1.0 + jnp.exp(-values))


def silu_back(values, gradient):
    gate = sigmoid(values)
    return gradient * gate * (1.0 + values * (1.0 - gate))


CUTS = 2


def packed_shapes(parts, tokens, width):
    return [jax.ShapeDtypeStruct((parts, tokens // CUTS, width), jnp.bfloat16)] * CUTS


def store_part(outs, index, values, column=slice(None)):
    at = 0
    for out in outs:
        out[index, :, column] = values[at : at + out.shape[1]]
        at += out.shape[1]


def load_part(refs, index, width):
    return jnp.concatenate([ref[index, :, :width] for ref in refs], axis=0)


class Pieces:
    def __init__(self, gather, index):
        group = gather.group
        self.layers = gather.layers
        before = sum(w.shape[1] for w in group[:index])
        self.base = before // QUARTERS
        self.set_base = gather.base + self.base
        self.other_base = gather.other_base + before
        self.rows, self.width = group[index].shape
        self.operands = [
            group[index],
            gather.other,
            gather.source.gathered,
            gather.piece,
            gather.other_piece,
            gather.rest,
            gather.other_rest,
        ]

    @property
    def part(self):
        return self.width // QUARTERS

    @property
    def scratch(self):
        copies = 1 + (QUARTERS - 1) * 2 * self.layers
        return [
            pltpu.VMEM((QUARTERS, 2 * self.layers, self.rows, self.part), jnp.bfloat16),
            pltpu.SemaphoreType.DMA((copies,)),
        ]

    def load(self, place, refs, buffer, sems):
        own, other, gathered, piece, other_piece, rest, other_rest = refs
        quarter, layer, core = place[0], place[1], place[2]
        span = pl.ds(self.base, self.part)
        copies = []

        def move(source, target):
            copies.append(pltpu.make_async_copy(source, target, sems.at[len(copies)]))
            copies[-1].start()

        def blocks(source, index, first, count):
            for number in range(count):
                at = first + number
                row = lax.rem(layer + 1 + at // 2, self.layers) * 2 + lax.rem(at, 2)
                move(source.at[pl.ds(number * self.rows, self.rows), span], buffer.at[index, row])

        move(gathered.at[:, :, pl.ds(self.set_base, self.part)], buffer.at[quarter])
        for r in range(1, QUARTERS):
            index = quarter ^ r
            near = pl.multiple_of(index * self.part, LANES)
            far = pl.multiple_of(self.other_base + index * self.part, LANES)
            move(own.at[:, pl.ds(near, self.part)], buffer.at[index, 2 * layer + core])
            move(other.at[:, pl.ds(far, self.part)], buffer.at[index, 2 * layer + 1 - core])
        count = 2 * (self.layers - 1)
        blocks(piece, quarter ^ (1 + core), jnp.int32(0), count)
        blocks(other_piece, quarter ^ (2 - core), jnp.int32(0), count)
        blocks(rest, quarter ^ 3, core * (count // 2), count // 2)
        blocks(other_rest, quarter ^ 3, (1 - core) * (count // 2), count // 2)
        return [(quarter, copies[:1]), (quarter ^ 1, copies[1:]), (quarter ^ 2, []), (quarter ^ 3, [])]

    def block(self, buffer, index):
        return buffer[index].reshape(2 * self.layers * self.rows, self.part)


def wait_all(steps):
    for _, copies in steps:
        for copy in copies:
            copy.wait()


def up_kernel(pieces, row, ready, place, values, gains, shifts, *refs):
    weight, outs, (buffer, sems) = refs[: -3 - CUTS], refs[-3 - CUTS : -2], refs[-2:]
    expanded_out, packed = outs[0], outs[1:]
    steps = pieces.load(place, weight, buffer, sems)
    ready()
    shape, _ = standard(values[...])
    hidden = (shape * gains[row : row + 1] + shifts[row : row + 1]).astype(jnp.bfloat16)
    store_part(packed, 0, hidden)
    for r, (index, copies) in enumerate(steps):
        for copy in copies:
            copy.wait()
        expanded = dot_rows(hidden, pieces.block(buffer, index))
        expanded_out[r] = expanded.astype(jnp.bfloat16)
        store_part(packed, 1 + r, (expanded * sigmoid(expanded)).astype(jnp.bfloat16))


def up_step(order, place, gather, index, row, values, gains, shifts):
    pieces = Pieces(gather, index)
    tokens, width = values.shape
    expanded, *packed = order.call(
        functools.partial(up_kernel, pieces, row),
        [
            jax.ShapeDtypeStruct((QUARTERS, tokens, pieces.part), jnp.bfloat16),
            *packed_shapes(1 + QUARTERS, tokens, width),
        ],
        [SMEM_SPACE] + [VMEM_SPACE] * 3 + [ANY_SPACE] * len(pieces.operands),
        [VMEM_SPACE] * (1 + CUTS),
        pieces.scratch,
        [place, values, gains, shifts, *pieces.operands],
        lazy=True,
    )
    return expanded, packed


def down_sum(pieces, ready, place, packed, first, weight, buffer, sems):
    total, steps = None, pieces.load(place, weight, buffer, sems)
    ready()
    for r, (index, copies) in enumerate(steps):
        for copy in copies:
            copy.wait()
        term = dot_cols(
            load_part(packed, first + r, pieces.part), pieces.block(buffer, index)
        )
        total = term if total is None else total + term
    return total


def down_kernel(pieces, ready, place, values, *refs):
    active, weight, (out, buffer, sems) = refs[:CUTS], refs[CUTS:-3], refs[-3:]
    branch = down_sum(pieces, ready, place, active, 1, weight, buffer, sems)
    out[...] = values[...] + 0.5 * branch


def down_step(order, place, gather, index, values, active):
    pieces = Pieces(gather, index)
    return order.call(
        functools.partial(down_kernel, pieces),
        [jax.ShapeDtypeStruct(values.shape, jnp.float32)],
        [SMEM_SPACE] + [VMEM_SPACE] * (1 + CUTS) + [ANY_SPACE] * len(pieces.operands),
        [VMEM_SPACE],
        pieces.scratch,
        [place, values, *active, *pieces.operands],
        lazy=True,
    )[0]


def last_kernel(pieces, row, ready, place, values, cotangent, gains, shifts, *refs):
    active, weight, outs = refs[:CUTS], refs[CUTS:-7], refs[-7:]
    encoded, grad_out, low_out, gain_out, shift_out, buffer, sems = outs
    branch = down_sum(pieces, ready, place, active, 1, weight, buffer, sems)
    total = values[...] + 0.5 * branch
    gain = gains[row : row + 1]
    shape, _ = standard(total)
    encoded[...] = (shape * gain + shifts[row : row + 1]).astype(jnp.bfloat16)
    back, gain_grad, shift_grad = norm_back(total, cotangent[...].astype(jnp.float32), gain)
    grad_out[...] = back
    low_out[0] = (0.5 * back).astype(jnp.bfloat16)
    gain_out[...] = gain_grad
    shift_out[...] = shift_grad


def vector_shapes(width, count=2):
    return [jax.ShapeDtypeStruct((1, width), jnp.float32)] * count


def last_step(order, place, gather, index, row, values, active, cotangent, gains, shifts):
    pieces = Pieces(gather, index)
    return order.call(
        functools.partial(last_kernel, pieces, row),
        [
            jax.ShapeDtypeStruct(values.shape, jnp.bfloat16),
            jax.ShapeDtypeStruct(values.shape, jnp.float32),
            jax.ShapeDtypeStruct((1, *values.shape), jnp.bfloat16),
            *vector_shapes(values.shape[1]),
        ],
        [SMEM_SPACE] + [VMEM_SPACE] * (4 + CUTS) + [ANY_SPACE] * len(pieces.operands),
        [VMEM_SPACE] * 5,
        pieces.scratch,
        [place, values, cotangent, gains, shifts, *active, *pieces.operands],
        lazy=True,
    )


def down_back_kernel(pieces, ready, place, gradient, expanded, *refs):
    weight, outs, (buffer, sems) = refs[: -2 - CUTS], refs[-2 - CUTS : -2], refs[-2:]
    steps = pieces.load(place, weight, buffer, sems)
    ready()
    for r, (index, copies) in enumerate(steps):
        for copy in copies:
            copy.wait()
        active_grad = dot_rows(gradient[0], pieces.block(buffer, index))
        store_part(outs, r, silu_back(expanded[r].astype(jnp.float32), active_grad).astype(jnp.bfloat16))


def down_back_step(order, place, gather, index, gradient, expanded, through=()):
    pieces = Pieces(gather, index)
    return order.call(
        functools.partial(down_back_kernel, pieces),
        packed_shapes(QUARTERS, gradient.shape[1], pieces.part),
        [SMEM_SPACE] + [VMEM_SPACE] * 2 + [ANY_SPACE] * len(pieces.operands),
        [VMEM_SPACE] * CUTS,
        pieces.scratch,
        [place, gradient, expanded, *pieces.operands],
        through,
        lazy=True,
    )


def into_norm_kernel(pieces, first, row, scale, ready, place, values, residual, gains, *refs):
    gradient, refs = refs[:CUTS], refs[CUTS:]
    weight, (grad_out, low_out, gain_out, shift_out, buffer, sems) = refs[:-6], refs[-6:]
    hidden_grad = down_sum(pieces, ready, place, gradient, first, weight, buffer, sems)
    back, gain_grad, shift_grad = norm_back(values[...], hidden_grad, gains[row : row + 1])
    total = residual[...] + back
    grad_out[...] = total
    low_out[0] = (scale * total).astype(jnp.bfloat16)
    gain_out[...] = gain_grad
    shift_out[...] = shift_grad


def into_norm_step(
    order, place, gather, index, first, row, scale, gradient, values, residual, gains, through=()
):
    pieces = Pieces(gather, index)
    return order.call(
        functools.partial(into_norm_kernel, pieces, first, row, scale),
        [
            jax.ShapeDtypeStruct(values.shape, jnp.float32),
            jax.ShapeDtypeStruct((1, *values.shape), jnp.bfloat16),
            *vector_shapes(values.shape[1]),
        ],
        [SMEM_SPACE] + [VMEM_SPACE] * (3 + CUTS) + [ANY_SPACE] * len(pieces.operands),
        [VMEM_SPACE] * 4,
        pieces.scratch,
        [place, values, residual, gains, *gradient, *pieces.operands],
        through,
        lazy=True,
    )


def whole_weight(pieces, ready, place, weight, buffer, sems):
    steps = pieces.load(place, weight, buffer, sems)
    ready()
    wait_all(steps)


def turn(values, cosine, sine):
    return values * cosine + pltpu.roll(values, HEAD_DIM // 2, 1) * sine


def masked_scores(query, key, matching):
    return jnp.where(matching, dot_cols(query, key), MASKED)


def head(index):
    return slice(index * HEAD_DIM, (index + 1) * HEAD_DIM)


def attend_kernel(pieces, row, ready, place, values, gains, shifts, cosine, sine, down, across, *refs):
    weight, outs = refs[:-6], refs[-6:]
    turned_out, totals_out, packed, projected, buffer, sems = outs
    steps = pieces.load(place, weight, buffer, sems)
    ready()
    shape, _ = standard(values[...])
    hidden = (shape * gains[row : row + 1] + shifts[row : row + 1]).astype(jnp.bfloat16)
    packed[0] = hidden
    for index, copies in steps:
        for copy in copies:
            copy.wait()
        column = pl.ds(pl.multiple_of(index * pieces.part, pieces.part), pieces.part)
        projected[:, column] = dot_rows(hidden, pieces.block(buffer, index))
    heads = pieces.width // (3 * HEAD_DIM)
    matching = down[...] == across[...]
    for h in range(heads):
        query = turn(projected[:, head(h)], cosine[...], sine[...]) * HEAD_DIM ** (-0.5)
        key = turn(projected[:, head(heads + h)], cosine[...], sine[...])
        query, key = query.astype(jnp.bfloat16), key.astype(jnp.bfloat16)
        value = projected[:, head(2 * heads + h)].astype(jnp.bfloat16)
        turned_out[:, head(h)] = query
        turned_out[:, head(heads + h)] = key
        turned_out[:, head(2 * heads + h)] = value
        scores = masked_scores(query, key, matching)
        highest = jnp.max(scores, axis=-1, keepdims=True)
        powers = jnp.exp(scores - highest)
        total = jnp.sum(powers, axis=-1, keepdims=True)
        totals_out[:, h : h + 1] = highest + jnp.log(total)
        probs = (powers / total).astype(jnp.bfloat16)
        packed[1, :, head(h)] = dot_rows(probs, value).astype(jnp.bfloat16)


def attend_step(order, place, gather, index, row, values, gains, shifts, cosine, sine, down, across):
    pieces = Pieces(gather, index)
    tokens, width = values.shape
    heads = pieces.width // (3 * HEAD_DIM)
    return order.call(
        functools.partial(attend_kernel, pieces, row),
        [
            jax.ShapeDtypeStruct((tokens, pieces.width), jnp.bfloat16),
            jax.ShapeDtypeStruct((tokens, heads), jnp.float32),
            jax.ShapeDtypeStruct((2, tokens, width), jnp.bfloat16),
        ],
        [SMEM_SPACE] + [VMEM_SPACE] * 7 + [ANY_SPACE] * len(pieces.operands),
        [VMEM_SPACE] * 3,
        [pltpu.VMEM((tokens, pieces.width), jnp.float32), *pieces.scratch],
        [place, values, gains, shifts, cosine, sine, down, across, *pieces.operands],
        lazy=True,
    )


def to_quarters(place, outs, column, values):
    part = values.shape[1] // QUARTERS
    for r in range(QUARTERS):
        block = values[:, pl.ds(pl.multiple_of((place[0] ^ r) * part, part), part)]
        store_part(outs, r, block, slice(column, column + part))


def attend_back_kernel(pieces, ready, place, gradient, turned, totals, cosine, sine, down, across, *refs):
    weight, rest = refs[: -4 - CUTS], refs[-4 - CUTS :]
    outs, (out, mixed_grad, buffer, sems) = rest[:CUTS], rest[CUTS:]
    heads = turned.shape[1] // (3 * HEAD_DIM)
    whole_weight(pieces, ready, place, weight, buffer, sems)
    total = None
    for index in range(QUARTERS):
        column = slice(index * pieces.part, (index + 1) * pieces.part)
        term = dot_cols(gradient[0, :, column], pieces.block(buffer, index))
        total = term if total is None else total + term
    mixed_grad[...] = total.astype(jnp.bfloat16)
    matching = down[...] == across[...]
    for h in range(heads):
        query = turned[:, head(h)]
        key = turned[:, head(heads + h)]
        value = turned[:, head(2 * heads + h)]
        gradient_h = mixed_grad[:, head(h)]
        probs = jnp.exp(masked_scores(query, key, matching) - totals[:, h : h + 1])
        value_grad = dot_down(probs.astype(jnp.bfloat16), gradient_h)
        probs_grad = dot_cols(gradient_h, value)
        inner = jnp.sum(probs * probs_grad, axis=-1, keepdims=True)
        score_grad = (probs * (probs_grad - inner)).astype(jnp.bfloat16)
        query_grad = dot_rows(score_grad, key) * HEAD_DIM ** (-0.5)
        key_grad = dot_down(score_grad, query)
        out[:, head(h)] = turn(query_grad, cosine[...], -sine[...]).astype(jnp.bfloat16)
        out[:, head(heads + h)] = turn(key_grad, cosine[...], -sine[...]).astype(jnp.bfloat16)
        out[:, head(2 * heads + h)] = value_grad.astype(jnp.bfloat16)
    to_quarters(place, outs, 0, out)


def attend_back_step(order, place, gather, index, gradient, turned, totals, cosine, sine, down, across):
    pieces = Pieces(gather, index)
    return order.call(
        functools.partial(attend_back_kernel, pieces),
        packed_shapes(QUARTERS, turned.shape[0], turned.shape[1] // QUARTERS),
        [SMEM_SPACE] + [VMEM_SPACE] * 7 + [ANY_SPACE] * len(pieces.operands),
        [VMEM_SPACE] * CUTS,
        [
            pltpu.VMEM(turned.shape, jnp.bfloat16),
            pltpu.VMEM(gradient.shape[1:], jnp.bfloat16),
            *pieces.scratch,
        ],
        [place, gradient, turned, totals, cosine, sine, down, across, *pieces.operands],
        lazy=True,
    )


def rows_sum(pieces, buffer, left):
    return jnp.concatenate(
        [dot_rows(left, pieces.block(buffer, index)) for index in range(QUARTERS)], axis=1
    )


def shifted(values, amount):
    return values if amount == 0 else pltpu.roll(values, amount % values.shape[0], 0)


def merge_kernel(pieces, ready, place, values, mixed, *refs):
    weight, (out, buffer, sems) = refs[:-3], refs[-3:]
    whole_weight(pieces, ready, place, weight, buffer, sems)
    for index in range(QUARTERS):
        column = slice(index * pieces.part, (index + 1) * pieces.part)
        out[:, column] = values[:, column] + dot_rows(mixed[1], pieces.block(buffer, index))


def merge_step(order, place, gather, index, values, mixed):
    pieces = Pieces(gather, index)
    return order.call(
        functools.partial(merge_kernel, pieces),
        [jax.ShapeDtypeStruct(values.shape, jnp.float32)],
        [SMEM_SPACE] + [VMEM_SPACE] * 2 + [ANY_SPACE] * len(pieces.operands),
        [VMEM_SPACE],
        pieces.scratch,
        [place, values, mixed, *pieces.operands],
        lazy=True,
    )[0]


def conv_kernel(weights, row, ready, place, values, gains, shifts, taps, keep, *refs):
    count = len(weights[0].operands)
    operands = [refs[i * count : (i + 1) * count] for i in range(len(weights))]
    rest = refs[len(weights) * count :]
    done_out, doubled_out, filtered_out, packed = rest[:4]
    scratch = rest[4:]
    buffers = [scratch[2 * i : 2 * i + 2] for i in range(len(weights))]
    steps = [w.load(place, o, *b) for w, o, b in zip(weights, operands, buffers)]
    gating, pointwise = weights
    ready()
    shape, _ = standard(values[...])
    hidden = (shape * gains[row : row + 1] + shifts[row : row + 1]).astype(jnp.bfloat16)
    packed[0] = hidden
    wait_all(steps[0])
    doubled = rows_sum(gating, buffers[0][0], hidden)
    doubled_out[...] = doubled.astype(jnp.bfloat16)
    half = gating.width // 2
    gated = doubled[:, :half] * sigmoid(doubled[:, half:])
    reach = taps.shape[0] // 2
    filtered = None
    for k in range(taps.shape[0]):
        term = shifted(gated, reach - k) * keep[:, k : k + 1] * taps[k : k + 1]
        filtered = term if filtered is None else filtered + term
    filtered_out[...] = filtered
    shape, _ = standard(filtered)
    renormed = shape * gains[row + 1 : row + 2] + shifts[row + 1 : row + 2]
    active = (renormed * sigmoid(renormed)).astype(jnp.bfloat16)
    packed[1] = active
    wait_all(steps[1])
    for index in range(QUARTERS):
        column = slice(index * pointwise.part, (index + 1) * pointwise.part)
        term = dot_rows(active, pointwise.block(buffers[1][0], index))
        done_out[:, column] = values[:, column] + term


def conv_step(order, place, gather, row, values, gains, shifts, taps, keep):
    weights = [Pieces(gather, i) for i in range(2)]
    tokens, width = values.shape
    operands = [o for w in weights for o in w.operands]
    return order.call(
        functools.partial(conv_kernel, weights, row),
        [
            jax.ShapeDtypeStruct((tokens, width), jnp.float32),
            jax.ShapeDtypeStruct((tokens, weights[0].width), jnp.bfloat16),
            jax.ShapeDtypeStruct((tokens, weights[0].width // 2), jnp.float32),
            jax.ShapeDtypeStruct((2, tokens, width), jnp.bfloat16),
        ],
        [SMEM_SPACE] + [VMEM_SPACE] * 5 + [ANY_SPACE] * len(operands),
        [VMEM_SPACE] * 4,
        [s for w in weights for s in w.scratch],
        [place, values, gains, shifts, taps, keep, *operands],
        lazy=True,
    )


def conv_back_kernel(pieces, row, ready, place, gradient, filtered, doubled, gains, shifts, taps, keep, *refs):
    weight, rest = refs[: -6 - CUTS], refs[-6 - CUTS :]
    outs = rest[:CUTS]
    gain_out, shift_out, taps_out, doubled_grad, buffer, sems = rest[CUTS:]
    whole_weight(pieces, ready, place, weight, buffer, sems)
    total = None
    for index in range(QUARTERS):
        column = slice(index * pieces.part, (index + 1) * pieces.part)
        term = dot_cols(gradient[0, :, column], pieces.block(buffer, index))
        total = term if total is None else total + term
    gain = gains[row : row + 1]
    shape, _ = standard(filtered[...])
    renormed = shape * gain + shifts[row : row + 1]
    back, gain_grad, shift_grad = norm_back(filtered[...], silu_back(renormed, total), gain)
    gain_out[...] = gain_grad
    shift_out[...] = shift_grad
    half = doubled.shape[1] // 2
    gate = sigmoid(doubled[:, half:].astype(jnp.float32))
    gated = doubled[:, :half].astype(jnp.float32) * gate
    reach = taps.shape[0] // 2
    gated_grad = None
    for k in range(taps.shape[0]):
        kept = back * keep[:, k : k + 1]
        taps_out[k : k + 1] = jnp.sum(kept * shifted(gated, reach - k), axis=0, keepdims=True)
        term = shifted(kept, k - reach) * taps[k : k + 1]
        gated_grad = term if gated_grad is None else gated_grad + term
    doubled_grad[:, :half] = (gated_grad * gate).astype(jnp.bfloat16)
    doubled_grad[:, half:] = (gated_grad * gated * (1.0 - gate)).astype(jnp.bfloat16)
    to_quarters(place, outs, 0, doubled_grad)


def conv_back_step(order, place, gather, index, row, gradient, filtered, doubled, gains, shifts, taps, keep):
    pieces = Pieces(gather, index)
    width = filtered.shape[1]
    return order.call(
        functools.partial(conv_back_kernel, pieces, row),
        [
            *packed_shapes(QUARTERS, doubled.shape[0], doubled.shape[1] // QUARTERS),
            *vector_shapes(width),
            jax.ShapeDtypeStruct(taps.shape, jnp.float32),
        ],
        [SMEM_SPACE] + [VMEM_SPACE] * 7 + [ANY_SPACE] * len(pieces.operands),
        [VMEM_SPACE] * (3 + CUTS),
        [pltpu.VMEM(doubled.shape, jnp.bfloat16), *pieces.scratch],
        [place, gradient, filtered, doubled, gains, shifts, taps, keep, *pieces.operands],
        lazy=True,
    )


def shards(
    sizes,
    frames,
    lengths,
    languages,
    embedding,
    gains,
    shifts,
    firstup,
    firstdown,
    projection,
    merger,
    gating,
    kernel,
    pointwise,
    secondup,
    seconddown,
    cotangent,
):
    frame_count = frames.shape[0]
    dp_index = lax.axis_index("dp").astype(jnp.int32)
    place = jnp.stack(
        [
            lax.rem(dp_index, jnp.int32(QUARTERS)),
            lax.axis_index("z").astype(jnp.int32),
            lax.axis_index("core").astype(jnp.int32),
        ]
    )
    order = Order(frames)
    order_of_groups = (
        ([firstup], [firstdown]),
        ([projection, merger], [gating, pointwise]),
        ([secondup],),
        ([seconddown],),
    )
    sources = [GatherSet(place, groups) for groups in order_of_groups]
    everything = jnp.concatenate([w for s in order_of_groups for g in s for w in g], axis=1)
    everything_other = swap_core(everything)
    gathers, other_base = [], 0
    for source, groups in zip(sources, order_of_groups):
        base = 0
        for group in groups:
            gathers.append(
                Gather(place, sizes, order, group, source, base, everything_other, other_base)
            )
            base += gathers[-1].width
            other_base += QUARTERS * gathers[-1].width
    table_full, gain_full, shift_full, kernel_full = gather_small(
        [embedding, gains, shifts, kernel]
    )
    segment_all, position_all, language_all = layout(lengths, languages, frame_count)
    segment = segment_all[0]
    language_row = language_all[0]
    cosine, sine = angles(position_all[0])
    cosine = jnp.concatenate([cosine, cosine], axis=-1)[:, 0]
    sine = jnp.concatenate([-sine, sine], axis=-1)[:, 0]
    down, across = segment[:, None], segment[None, :]
    gain_rows = gain_full.astype(jnp.float32)
    shift_rows = shift_full.astype(jnp.float32)
    taps = kernel_full.astype(jnp.float32)
    reach = taps.shape[0] // 2
    segment_pad = jnp.pad(segment, (reach, reach), constant_values=-1)
    keep = jnp.stack(
        [segment_pad[k : k + frame_count] == segment for k in range(taps.shape[0])], axis=1
    ).astype(jnp.float32)
    language_hot = (
        language_row[:, None] == jnp.arange(table_full.shape[0], dtype=jnp.int32)[None, :]
    ).astype(jnp.float32)
    start_sum = frames.astype(jnp.float32) + jnp.dot(
        language_hot.astype(jnp.bfloat16), table_full, preferred_element_type=jnp.float32
    )

    gathers[0].near(40)
    gathers[1].near(32)
    order.wait(everything_other)
    gathers[0].far()
    order.wait(gathers[0].rest)
    gathers[2].near(24)
    gathers[1].far()
    gathers[3].near(16)
    first_expanded, first_packed = up_step(
        order, place, gathers[0], 0, 0, start_sum, gain_rows, shift_rows
    )
    gathers[2].far()
    gathers[4].near(8)
    after_first = down_step(order, place, gathers[1], 0, start_sum, first_packed)
    gathers[3].far()
    gathers[5].near(0)
    turned, totals, attend_packed = attend_step(
        order, place, gathers[2], 0, 1, after_first, gain_rows, shift_rows, cosine, sine, down, across
    )
    after_attention = merge_step(order, place, gathers[2], 1, after_first, attend_packed)
    gathers[4].far()
    after_conv, doubled, filtered, conv_packed = conv_step(
        order, place, gathers[3], 2, after_attention, gain_rows, shift_rows, taps, keep
    )
    gathers[5].far()
    second_expanded, second_packed = up_step(
        order, place, gathers[4], 0, 4, after_conv, gain_rows, shift_rows
    )
    second_forward = Packed(second_packed)
    encoded, grad_second, low_second, final_gain, final_shift = last_step(
        order,
        place,
        gathers[5],
        0,
        5,
        after_conv,
        second_packed,
        cotangent,
        gain_rows,
        shift_rows,
    )
    rounds = Rounds(place, sizes, order)

    low = Packed([low_second])
    down_two = Sums(Factor(low, 0, second_forward, 1, 0, seconddown.shape[1]))
    rounds.step([down_two], margin=80)
    *packed, first_packed_a, first_packed_b = down_back_step(
        order, place, gathers[5], 0, low_second, second_expanded, first_packed
    )
    backward, first_forward = Packed(packed), Packed([first_packed_a, first_packed_b])
    grad_conv, low_conv, second_gain, second_shift, *held = into_norm_step(
        order,
        place,
        gathers[4],
        0,
        0,
        4,
        1.0,
        packed,
        after_conv,
        grad_second,
        gain_rows,
        [conv_packed, attend_packed],
    )
    conv_forward, attend_forward = Packed(held[:1]), Packed(held[1:])
    up_two = Sums(Factor(second_forward, 0, backward, 0, 0, secondup.shape[1]))
    order.wait(*first_forward.all)
    rounds.step([up_two], margin=64)
    low = Packed([low_conv])
    order.wait(*conv_forward.all, *attend_forward.all)
    *packed, inner_gain, inner_shift, taps_grad = conv_back_step(
        order, place, gathers[3], 1, 3, low_conv, filtered, doubled, gain_rows, shift_rows, taps, keep
    )
    backward = Packed(packed)
    grad_attention, low_attention, outer_gain, outer_shift = into_norm_step(
        order,
        place,
        gathers[3],
        0,
        0,
        2,
        1.0,
        packed,
        after_attention,
        grad_conv,
        gain_rows,
    )
    conv = Sums(
        Factor(conv_forward, 0, backward, 0, 0, gating.shape[1]),
        Factor(conv_forward, 1, low, 0, 0, pointwise.shape[1], relative=False),
        Factor(attend_forward, 1, Packed([low_attention]), 0, 0, merger.shape[1], relative=False),
    )
    rounds.step([conv], [down_two], margin=48)
    packed = attend_back_step(
        order, place, gathers[2], 1, low_attention, turned, totals, cosine, sine, down, across
    )
    backward = Packed(packed)
    grad_first, low_first, attend_gain, attend_shift = into_norm_step(
        order,
        place,
        gathers[2],
        0,
        0,
        1,
        0.5,
        packed,
        after_first,
        grad_attention,
        gain_rows,
    )
    projection_factor = Factor(attend_forward, 0, backward, 0, 0, projection.shape[1])
    order.wait(*backward.all)
    low = Packed([low_first])
    packed = down_back_step(order, place, gathers[1], 0, low_first, first_expanded)
    backward = Packed(packed)
    down_one = Sums(Factor(low, 0, first_forward, 1, 0, firstdown.shape[1]))
    (down_two_mine,) = rounds.step([down_one], [up_two], [down_two], margin=32)
    frames_grad, low_start, first_gain, first_shift = into_norm_step(
        order, place, gathers[0], 0, 0, 0, 1.0, packed, start_sum, grad_first, gain_rows
    )
    up_one = Sums(Factor(first_forward, 0, backward, 0, 0, firstup.shape[1]))
    (up_two_mine,) = rounds.step([up_one], [conv], [up_two], margin=16)
    vectors = jnp.concatenate(
        [
            first_gain,
            attend_gain,
            outer_gain,
            inner_gain,
            second_gain,
            final_gain,
            first_shift,
            attend_shift,
            outer_shift,
            inner_shift,
            second_shift,
            final_shift,
            taps_grad,
        ]
    )
    small_packed = Packed([pack_small(language_hot, low_start[0], vectors)])
    last = Sums(
        projection_factor,
        Factor(small_packed, 0, small_packed, 1, 0, QUARTERS * LANES, relative=False),
    )
    order.wait(down_two_mine)
    (conv_mine,) = rounds.step([last], [down_one], [conv], margin=80)
    order.wait(up_two_mine)
    (down_one_mine,) = rounds.step([], [up_one], [down_one])
    order.wait(conv_mine)
    (up_one_mine,) = rounds.step([], [last], [up_one])
    pieces = rounds.share([down_two_mine, up_two_mine])
    order.wait(down_one_mine)
    (last_mine,) = rounds.step([], [], [last])
    middle_pieces = rounds.share([conv_mine, down_one_mine])
    seconddown_grad, secondup_grad = spread(
        order, place, [seconddown.shape[1], secondup.shape[1]], pieces
    )
    up_pieces = rounds.share([up_one_mine])
    middle = [gating, pointwise, merger, firstdown]
    gating_grad, pointwise_grad, merger_grad, firstdown_grad = spread(
        order, place, [w.shape[1] for w in middle], middle_pieces
    )
    pieces = rounds.share([last_mine])
    (firstup_grad,) = spread(order, place, [firstup.shape[1]], up_pieces)
    projection_grad, small = spread(
        order, place, [projection.shape[1], QUARTERS * LANES], pieces
    )
    counts = [embedding.shape[0], gains.shape[0], shifts.shape[0], kernel.shape[0]]
    table_sum, gain_sum, shift_sum, taps_sum = unpack_small(small, counts)
    return (
        encoded,
        frames_grad,
        table_sum,
        gain_sum,
        shift_sum,
        firstup_grad,
        firstdown_grad,
        projection_grad,
        merger_grad,
        gating_grad,
        taps_sum,
        pointwise_grad,
        secondup_grad,
        seconddown_grad,
    )


def solution(mesh):
    dp_size, fsdp_size = mesh.shape["dp"], mesh.shape["fsdp"]
    layers = fsdp_size // 2
    split = Mesh(mesh.devices.reshape(dp_size, layers, 2), ("dp", "z", "core"))
    return jax.shard_map(
        functools.partial(shards, (dp_size, layers)),
        mesh=split,
        in_specs=(
            P(("dp", "z", "core"), None),
            P(("dp", "z", "core"), None),
            P(("dp", "z", "core"), None),
            P(None, ("z", "core")),
            P(None, ("z", "core")),
            P(None, ("z", "core")),
            P(("z", "core"), None),
            P(("z", "core"), None),
            P(("z", "core"), None),
            P(("z", "core"), None),
            P(("z", "core"), None),
            P(None, ("z", "core")),
            P(("z", "core"), None),
            P(("z", "core"), None),
            P(("z", "core"), None),
            P(("dp", "z", "core"), None),
        ),
        out_specs=(
            P(("dp", "z", "core"), None),
            P(("dp", "z", "core"), None),
            P(None, ("z", "core")),
            P(None, ("z", "core")),
            P(None, ("z", "core")),
            P(("z", "core"), None),
            P(("z", "core"), None),
            P(("z", "core"), None),
            P(("z", "core"), None),
            P(("z", "core"), None),
            P(None, ("z", "core")),
            P(("z", "core"), None),
            P(("z", "core"), None),
            P(("z", "core"), None),
        ),
        check_vma=False,
    )
```

```python
import functools

import jax
import jax.numpy as jnp
import numpy as np
from jax import lax
from jax.experimental import pallas as pl
from jax.experimental.pallas import tpu as pltpu
from jax.sharding import Mesh
from jax.sharding import PartitionSpec as P

HEAD_DIM = 128


def layout(lengths, languages, frame_count):
    utterances = jnp.arange(lengths.shape[-1], dtype=jnp.int32)
    earlier = utterances[:, None] <= utterances[None, :]
    finish = jnp.sum(jnp.where(earlier[None], lengths[:, :, None], 0), axis=1)
    begins = finish - lengths
    indices = jnp.arange(frame_count, dtype=jnp.int32)
    segment = jnp.sum((indices[None, :, None] >= finish[:, None, :]).astype(jnp.int32), axis=-1)
    owners = segment[:, :, None] == jnp.arange(lengths.shape[-1], dtype=jnp.int32)[None, None, :]
    first_row = jnp.sum(jnp.where(owners, begins[:, None, :], 0), axis=-1)
    language_row = jnp.sum(jnp.where(owners, languages[:, None, :], 0), axis=-1)
    return (segment, indices[None, :] - first_row, language_row)


def angles(position):
    half_dim = HEAD_DIM // 2
    frequency = 10000.0 ** (-jnp.arange(half_dim, dtype=jnp.float32) / half_dim)
    turned = position.astype(jnp.float32)[..., None] * frequency
    return (jnp.cos(turned)[..., None, :], jnp.sin(turned)[..., None, :])


VMEM_SPACE = pl.BlockSpec(memory_space=pltpu.VMEM)
SMEM_SPACE = pl.BlockSpec(memory_space=pltpu.SMEM)
ANY_SPACE = pl.BlockSpec(memory_space=pl.ANY)


class Order:
    def __init__(self, value):
        self.value, self.waits = value, []

    def wait(self, *arrays):
        self.waits += arrays

    def call(self, kernel, out_shape, in_specs, out_specs, scratch_shapes, operands, through=(), lazy=False):
        after, self.waits = self.waits, []
        carried = [*through, self.value]
        count, outs, extra = len(operands), len(out_shape), len(after)
        held_in = [i for i in range(count) if in_specs[i] is VMEM_SPACE]
        held_out = [i for i in range(outs) if out_specs[i] is VMEM_SPACE]
        buffers = [pltpu.VMEM(operands[i].shape, operands[i].dtype) for i in held_in]
        buffers += [pltpu.VMEM(out_shape[i].shape, out_shape[i].dtype) for i in held_out]
        copies = max(1, len(held_in), len(held_out))

        def body(*refs):
            ins, rest = list(refs[:count]), refs[count + extra + len(carried) :]
            results, rest = list(rest[:outs]), rest[outs + len(carried) :]
            held, scratch, sems = rest[: len(buffers)], rest[len(buffers) : -1], rest[-1]
            moves = []
            for at, i in enumerate(held_in):
                moves.append(pltpu.make_async_copy(ins[i], held[at], sems.at[at]))
                moves[-1].start()
                ins[i] = held[at]
            targets = []
            for at, i in enumerate(held_out):
                targets.append(results[i])
                results[i] = held[len(held_in) + at]
            def ready():
                for move in arriving:
                    move.wait()

            arriving = moves
            if lazy:
                kernel(ready, *ins, *results, *scratch)
            else:
                ready()
                kernel(*ins, *results, *scratch)
            moves = []
            for at, i in enumerate(held_out):
                moves.append(pltpu.make_async_copy(results[i], targets[at], sems.at[at]))
                moves[-1].start()
            for move in moves:
                move.wait()

        result = pl.pallas_call(
            body,
            out_shape=[*out_shape, *[jax.ShapeDtypeStruct(x.shape, x.dtype) for x in carried]],
            in_specs=[ANY_SPACE if s is VMEM_SPACE else s for s in in_specs]
            + [ANY_SPACE] * (extra + len(carried)),
            out_specs=[ANY_SPACE] * (outs + len(carried)),
            scratch_shapes=[*buffers, *scratch_shapes, pltpu.SemaphoreType.DMA((copies,))],
            input_output_aliases={count + extra + i: outs + i for i in range(len(carried))},
            compiler_params=pltpu.CompilerParams(vmem_limit_bytes=VMEM_LIMIT),
        )(*operands, *after, *carried)
        self.value = result[-1]
        return result[:-1]


VMEM_LIMIT = 52 * 1024 * 1024
QUARTERS = 4
LANES = 128
BITS = (0, 1)


def swap_dp(value, bit, size):
    return lax.ppermute(value, "dp", [(i, i ^ (1 << bit)) for i in range(size)])


def swap_core(value):
    return lax.ppermute(value, "core", [(0, 1), (1, 0)])


def swap_pairs(value, flip, size):
    pairs = []
    for i in range(size):
        for core in range(2):
            far = i ^ (1 << BITS[core ^ flip])
            pairs.append((2 * i + core, 2 * far + core))
    return lax.ppermute(value, ("dp", "core"), pairs)


def pick_kernel(layers, base, place, gathered, out, sems):
    layer = place[1]
    rows, copies = gathered.shape[1], []
    for k in range(1, layers):
        for lane in range(2):
            at = 2 * (k - 1) + lane
            row = lax.rem(layer + k, layers) * 2 + lane
            source = gathered.at[row, :, pl.ds(base, out.shape[1])]
            target = out.at[pl.ds(at * rows, rows)]
            copies.append(pltpu.make_async_copy(source, target, sems.at[at]))
            copies[-1].start()
    for copy in copies:
        copy.wait()


def pick(order, place, layers, gathered, base, width, margin):
    blocks = 2 * (layers - 1)
    return order.call(
        functools.partial(pick_kernel, layers, base),
        [jax.ShapeDtypeStruct((blocks * gathered.shape[1] + margin, width), gathered.dtype)],
        [SMEM_SPACE, ANY_SPACE],
        [VMEM_SPACE],
        [pltpu.SemaphoreType.DMA((blocks,))],
        [place, gathered],
    )[0]


def half_kernel(place, piece, out, sems):
    rows = out.shape[0]
    start = pl.multiple_of(place[2] * rows, rows)
    copy = pltpu.make_async_copy(piece.at[pl.ds(start, rows)], out, sems.at[0])
    copy.start()
    copy.wait()


def half(order, place, piece, rows):
    return order.call(
        half_kernel,
        [jax.ShapeDtypeStruct((rows // 2, piece.shape[1]), piece.dtype)],
        [SMEM_SPACE, ANY_SPACE],
        [VMEM_SPACE],
        [pltpu.SemaphoreType.DMA((1,))],
        [place, piece],
    )[0]


def join_kernel(*refs):
    ins, out, sems = refs[:-2], refs[-2], refs[-1]
    at, copies = 0, []
    for k, ref in enumerate(ins):
        target = out.at[:, pl.ds(at, ref.shape[1])]
        copies.append(pltpu.make_async_copy(ref, target, sems.at[k]))
        copies[-1].start()
        at += ref.shape[1]
    for copy in copies:
        copy.wait()


def join(order, arrays):
    width = sum(a.shape[1] for a in arrays)
    return order.call(
        join_kernel,
        [jax.ShapeDtypeStruct((arrays[0].shape[0], width), arrays[0].dtype)],
        [ANY_SPACE] * len(arrays),
        [VMEM_SPACE],
        [pltpu.SemaphoreType.DMA((len(arrays),))],
        arrays,
    )[0]


class Packed:
    def __init__(self, arrays):
        self.own = list(arrays)
        self.all = [*self.own, *[swap_core(a) for a in self.own]]
        self.tokens = sum(a.shape[1] for a in self.all)

    def part(self, index):
        return [(a, index, a.shape[1]) for a in self.all]


class Factor:
    def __init__(self, left, left_index, right, right_index, base, width, relative=True):
        self.left = left.part(left_index)
        self.right, self.right_index, self.base, self.relative = right, right_index, base, relative
        self.width, self.part, self.tokens = width, width // QUARTERS, left.tokens
        self.arrays = [*left.all, *right.all]

    def columns(self, quarter, r, start, width):
        if self.relative:
            index, column = self.right_index + r, pl.ds(self.base + start, width)
        else:
            index = self.right_index
            column = pl.ds(pl.multiple_of((quarter ^ r) * self.part + start, LANES), width)
        return [(a, index, column, count) for a, _, count in self.right.part(0)]


class Sums:
    def __init__(self, *factors):
        self.factors = factors
        self.width = sum(f.part for f in factors)

    def spans(self):
        base = 0
        for i, f in enumerate(self.factors):
            for start in range(0, f.part, TILE):
                yield i, start, min(TILE, f.part - start), base + start
            base += f.part


TILE = 512


def left_width(features, layers):
    return features // 2 if features // (2 * layers) % LANES == 0 else features


def left_spans(features, layers, core):
    rows = features // (2 * layers)
    if rows % LANES:
        return [(pl.ds(0, features), pl.ds(0, features))]
    return [
        (pl.ds(pl.multiple_of((2 * k + core) * rows, rows), rows), pl.ds(k * rows, rows))
        for k in range(layers)
    ]


def own_rows(values, features, layers, core):
    tokens, width = values.shape
    if width < features:
        return values.T
    rows = features // (2 * layers)
    turned = values.T.reshape(layers, 2, rows, tokens)
    return jnp.where(core == 0, turned[:, 0], turned[:, 1]).reshape(layers * rows, tokens)


def round_kernel(layers, plan, tables, place, *refs):
    jobs, lefts, count_in, count_out = plan
    ins, outs = refs[:count_in], refs[count_in : count_in + count_out]
    left_buffer, turned, right_buffer, add_buffer, out_buffer, left_sems, in_sems, out_sems = refs[
        count_in + count_out :
    ]
    quarter, core = place[0], place[2]

    quarters = {"both": 3, "near": 1 + core, "far": 2 - core, "own": 0}

    def start(source, target, sem):
        copy = pltpu.make_async_copy(source, target, sem)
        copy.start()
        return copy

    left_copies = []
    for i, factor in enumerate(lefts):
        at, copies = 0, []
        for k, (array, index, rows) in enumerate(factor.left):
            source = ins[tables[id(array)]].at[index]
            spans = left_spans(source.shape[1], layers, core)
            for number, (columns, there) in enumerate(spans):
                target = left_buffer.at[i, at : at + rows, there]
                sem = left_sems.at[i, k * len(spans) + number]
                copies.append(start(source.at[:, columns], target, sem))
            at += rows
        left_copies.append(copies)
    loads = []
    for number, (i, r, first, width, adds, _) in enumerate(jobs):
        at, copies = 0, []
        for array, index, column, rows in lefts[i].columns(quarter, quarters[r], first, width):
            source = ins[tables[id(array)]].at[index, :, column]
            target = right_buffer.at[number, at : at + rows, pl.ds(0, width)]
            copies.append(start(source, target, in_sems.at[number, len(copies)]))
            at += rows
        for k, (array, column) in enumerate(adds):
            height = add_buffer.shape[2]
            source = ins[tables[id(array)]].at[pl.ds(0, height), pl.ds(column, width)]
            target = add_buffer.at[number, k, :, pl.ds(0, width)]
            copies.append(start(source, target, in_sems.at[number, len(copies)]))
        loads.append(copies)
    for i, factor in enumerate(lefts):
        for copy in left_copies[i]:
            copy.wait()
        turned[i, :, : factor.tokens] = own_rows(
            left_buffer[i, : factor.tokens], factor.left[0][0].shape[2], layers, core
        )
    stores = []
    for number, (i, _, _, width, adds, (out, column)) in enumerate(jobs):
        tokens = lefts[i].tokens
        for copy in loads[number]:
            copy.wait()
        product = jnp.dot(
            turned[i, :, :tokens],
            right_buffer[number, :tokens, :width],
            preferred_element_type=jnp.float32,
        )
        for k in range(len(adds)):
            product += add_buffer[number, k, :, :width].astype(jnp.float32)
        out_buffer[number, :, :width] = product.astype(jnp.bfloat16)
        source = out_buffer.at[number, :, pl.ds(0, width)]
        target = outs[out].at[pl.ds(0, out_buffer.shape[1]), pl.ds(column, width)]
        stores.append(start(source, target, out_sems.at[number]))
    for copy in stores:
        copy.wait()


class Rounds:
    def __init__(self, place, sizes, order):
        self.place, self.order = place, order
        self.dp_size, self.layers = sizes

    def step(self, halves=(), quarters=(), rows=(), margin=0):
        lefts, jobs, widths = [], [], [0] * (2 + len(rows))

        def left(factor):
            if factor not in lefts:
                lefts.append(factor)
            return lefts.index(factor)

        def add(sums, r, out, adds):
            base = widths[out]
            for i, first, width, at in sums.spans():
                mine = [(array, offset + at) for array, offset in adds]
                jobs.append((left(sums.factors[i]), r, first, width, mine, (out, base + at)))
            widths[out] += sums.width
            return base

        sent = []
        for sums in halves:
            sums.near_at = add(sums, "both", 0, [])
            sums.own_at = add(sums, "near", 0, [])
        for sums in quarters:
            sums.far_at = add(sums, "far", 1, [(sums.halves, sums.near_at)])
        for number, sums in enumerate(rows):
            add(sums, "own", 2 + number, [(sums.halves, sums.own_at), (sums.quarters, sums.far_at)])
        slots = [k for k in range(2 + len(rows)) if widths[k]]
        jobs = [job[:5] + ((slots.index(job[5][0]), job[5][1]),) for job in jobs]
        arrays, tables = [], {}
        used = [a for factor in lefts for a in factor.arrays] + [a for job in jobs for a, _ in job[4]]
        for array in used:
            if id(array) not in tables:
                tables[id(array)] = len(arrays)
                arrays.append(array)
        height = lefts[0].left[0][0].shape[2] // 2
        features = lefts[0].left[0][0].shape[2]
        tokens = max(factor.tokens for factor in lefts)
        widest = max(job[3] for job in jobs)
        depth = max(1, max(len(job[4]) for job in jobs))
        pieces = max(len(factor.left) for factor in lefts)
        rights = max(len(factor.right.all) for factor in lefts)
        outs = self.order.call(
            functools.partial(
                round_kernel, self.layers, (jobs, lefts, len(arrays), len(slots)), tables
            ),
            [
                jax.ShapeDtypeStruct((height + (margin if k == 0 else 0), widths[k]), jnp.bfloat16)
                for k in slots
            ],
            [SMEM_SPACE] + [ANY_SPACE] * len(arrays),
            [ANY_SPACE] * len(slots),
            [
                pltpu.VMEM(
                    (len(lefts), tokens, left_width(features, self.layers)), jnp.bfloat16
                ),
                pltpu.VMEM((len(lefts), height, tokens), jnp.bfloat16),
                pltpu.VMEM((len(jobs), tokens, widest), jnp.bfloat16),
                pltpu.VMEM((len(jobs), depth, height, widest), jnp.bfloat16),
                pltpu.VMEM((len(jobs), height, widest), jnp.bfloat16),
                pltpu.SemaphoreType.DMA((len(lefts), pieces * self.layers)),
                pltpu.SemaphoreType.DMA((len(jobs), rights + depth)),
                pltpu.SemaphoreType.DMA((len(jobs),)),
            ],
            [self.place, *arrays],
        )
        moved = {k: swap_pairs(outs[slots.index(k)], k, self.dp_size) for k in slots if k < 2}
        for sums in halves:
            sums.halves = moved[0]
        for sums in quarters:
            sums.quarters = moved[1]
        return [
            lax.psum_scatter(outs[slots.index(k)], "z", scatter_dimension=0, tiled=True)
            for k in slots
            if k >= 2
        ]

    def share(self, mine):
        summed = join(self.order, mine)
        bit = len(BITS)
        while 1 << bit < self.dp_size:
            summed = summed + swap_dp(summed, bit, self.dp_size)
            bit += 1
        near = swap_pairs(summed, 0, self.dp_size)
        far = swap_pairs(summed, 1, self.dp_size)
        return [summed, near, far, swap_pairs(near, 1, self.dp_size)]


def spread_kernel(widths, place, *refs):
    pieces, outs = refs[:QUARTERS], refs[QUARTERS:]
    quarter, core = place[0], place[2]
    base = 0
    for i, width in enumerate(widths):
        part = width // QUARTERS
        for r, place_of in enumerate((0, 1 + core, 2 - core, 3)):
            column = pl.ds(pl.multiple_of((quarter ^ place_of) * part, part), part)
            outs[i][:, column] = pieces[r][:, pl.ds(base, part)].astype(jnp.float32)
        base += part


def spread(order, place, widths, pieces):
    rows = pieces[0].shape[0]
    return order.call(
        functools.partial(spread_kernel, widths),
        [jax.ShapeDtypeStruct((rows, w), jnp.float32) for w in widths],
        [SMEM_SPACE] + [VMEM_SPACE] * QUARTERS,
        [VMEM_SPACE] * len(widths),
        [],
        [place, *pieces],
    )


class GatherSet:
    def __init__(self, place, groups):
        quarter = place[0]
        mine = [
            lax.dynamic_slice_in_dim(w, quarter * (w.shape[1] // QUARTERS), w.shape[1] // QUARTERS, 1)
            for group in groups
            for w in group
        ]
        mine = jnp.concatenate(mine, axis=1) if len(mine) > 1 else mine[0]
        self.gathered = lax.all_gather(mine, ("z", "core"), axis=0, tiled=False)


class Gather:
    def __init__(self, place, sizes, order, group, source, base, other, other_base):
        self.place, self.order, self.group = place, order, group
        self.dp_size, self.layers = sizes
        self.source, self.base, self.other, self.other_base = source, base, other, other_base
        self.width = sum(w.shape[1] for w in group) // QUARTERS
        self.rows = 2 * (self.layers - 1) * group[0].shape[0]

    def near(self, margin):
        piece = pick(
            self.order, self.place, self.layers, self.source.gathered, self.base, self.width, margin
        )
        self.piece = swap_pairs(piece, 0, self.dp_size)
        self.other_piece = swap_core(self.piece)

    def arrived(self):
        return [self.other_piece, self.rest, self.other_rest]

    def far(self):
        self.rest = swap_pairs(half(self.order, self.place, self.piece, self.rows), 1, self.dp_size)
        self.other_rest = swap_core(self.rest)


def gather_small(arrays):
    rows = [a.shape[0] for a in arrays]
    packed = jnp.concatenate(arrays, axis=0)
    packed = jnp.pad(packed, ((0, -packed.shape[0] % 16), (0, 0)))
    full = lax.all_gather(packed, ("z", "core"), axis=0, tiled=False)
    full = full.transpose(1, 0, 2).reshape(packed.shape[0], -1)
    pieces, start = [], 0
    for count in rows:
        pieces.append(full[start : start + count])
        start += count
    return pieces


def pack_small(table_hot, frames_grad, vectors):
    count = table_hot.shape[1]
    extra = -(frames_grad.shape[0] + vectors.shape[0]) % 16
    left = jnp.concatenate([frames_grad, vectors, jnp.zeros((extra, vectors.shape[1]), vectors.dtype)])
    used = count + vectors.shape[0]
    share = -(-used // QUARTERS)
    unit = jnp.eye(vectors.shape[0], dtype=table_hot.dtype)
    right = jnp.block(
        [
            [table_hot, jnp.zeros((table_hot.shape[0], vectors.shape[0]), table_hot.dtype)],
            [jnp.zeros((vectors.shape[0], count), table_hot.dtype), unit],
        ]
    )
    right = jnp.pad(right, ((0, extra), (0, share * QUARTERS - used)))
    right = right.reshape(right.shape[0], QUARTERS, share)
    right = jnp.pad(right, ((0, 0), (0, 0), (0, LANES - share)))
    right = right.reshape(right.shape[0], QUARTERS * LANES)
    right = jnp.pad(right, ((0, 0), (0, left.shape[1] - right.shape[1])))
    return jnp.stack([left.astype(jnp.bfloat16), right.astype(jnp.bfloat16)])


def unpack_small(summed, counts):
    used = sum(counts)
    share = -(-used // QUARTERS)
    rows = summed.reshape(summed.shape[0], QUARTERS, LANES)[:, :, :share]
    rows = rows.reshape(summed.shape[0], QUARTERS * share).T
    pieces, start = [], 0
    for count in counts:
        pieces.append(rows[start : start + count])
        start += count
    return pieces

EPSILON = 1e-05
MASKED = -1000000000.0


def dot_rows(left, right):
    return jnp.dot(left, right, preferred_element_type=jnp.float32)


def dot_cols(left, right):
    return lax.dot_general(
        left, right, (((1,), (1,)), ((), ())), preferred_element_type=jnp.float32
    )


def dot_down(left, right):
    return jnp.dot(left.T, right, preferred_element_type=jnp.float32)


def standard(values):
    centred = values - jnp.mean(values, axis=-1, keepdims=True)
    spread = lax.rsqrt(jnp.mean(centred * centred, axis=-1, keepdims=True) + EPSILON)
    return centred * spread, spread


def norm_back(values, gradient, gain):
    shape, spread = standard(values)
    inner = gradient * gain
    back = spread * (
        inner
        - jnp.mean(inner, axis=-1, keepdims=True)
        - shape * jnp.mean(inner * shape, axis=-1, keepdims=True)
    )
    return (
        back,
        jnp.sum(gradient * shape, axis=0, keepdims=True),
        jnp.sum(gradient, axis=0, keepdims=True),
    )


def sigmoid(values):
    return 1.0 / (1.0 + jnp.exp(-values))


def silu_back(values, gradient):
    gate = sigmoid(values)
    return gradient * gate * (1.0 + values * (1.0 - gate))


CUTS = 2


def packed_shapes(parts, tokens, width):
    return [jax.ShapeDtypeStruct((parts, tokens // CUTS, width), jnp.bfloat16)] * CUTS


def store_part(outs, index, values, column=slice(None)):
    at = 0
    for out in outs:
        out[index, :, column] = values[at : at + out.shape[1]]
        at += out.shape[1]


def load_part(refs, index, width):
    return jnp.concatenate([ref[index, :, :width] for ref in refs], axis=0)


class Pieces:
    def __init__(self, gather, index):
        group = gather.group
        self.layers = gather.layers
        before = sum(w.shape[1] for w in group[:index])
        self.base = before // QUARTERS
        self.set_base = gather.base + self.base
        self.other_base = gather.other_base + before
        self.rows, self.width = group[index].shape
        self.operands = [
            group[index],
            gather.other,
            gather.source.gathered,
            gather.piece,
            gather.other_piece,
            gather.rest,
            gather.other_rest,
        ]

    @property
    def part(self):
        return self.width // QUARTERS

    @property
    def scratch(self):
        copies = 1 + (QUARTERS - 1) * 2 * self.layers
        return [
            pltpu.VMEM((QUARTERS, 2 * self.layers, self.rows, self.part), jnp.bfloat16),
            pltpu.SemaphoreType.DMA((copies,)),
        ]

    def load(self, place, refs, buffer, sems):
        own, other, gathered, piece, other_piece, rest, other_rest = refs
        quarter, layer, core = place[0], place[1], place[2]
        span = pl.ds(self.base, self.part)
        copies = []

        def move(source, target):
            copies.append(pltpu.make_async_copy(source, target, sems.at[len(copies)]))
            copies[-1].start()

        def blocks(source, index, first, count):
            for number in range(count):
                at = first + number
                row = lax.rem(layer + 1 + at // 2, self.layers) * 2 + lax.rem(at, 2)
                move(source.at[pl.ds(number * self.rows, self.rows), span], buffer.at[index, row])

        move(gathered.at[:, :, pl.ds(self.set_base, self.part)], buffer.at[quarter])
        for r in range(1, QUARTERS):
            index = quarter ^ r
            near = pl.multiple_of(index * self.part, LANES)
            far = pl.multiple_of(self.other_base + index * self.part, LANES)
            move(own.at[:, pl.ds(near, self.part)], buffer.at[index, 2 * layer + core])
            move(other.at[:, pl.ds(far, self.part)], buffer.at[index, 2 * layer + 1 - core])
        count = 2 * (self.layers - 1)
        blocks(piece, quarter ^ (1 + core), jnp.int32(0), count)
        blocks(other_piece, quarter ^ (2 - core), jnp.int32(0), count)
        blocks(rest, quarter ^ 3, core * (count // 2), count // 2)
        blocks(other_rest, quarter ^ 3, (1 - core) * (count // 2), count // 2)
        return [(quarter, copies[:1]), (quarter ^ 1, copies[1:]), (quarter ^ 2, []), (quarter ^ 3, [])]

    def block(self, buffer, index):
        return buffer[index].reshape(2 * self.layers * self.rows, self.part)


def wait_all(steps):
    for _, copies in steps:
        for copy in copies:
            copy.wait()


def up_kernel(pieces, row, ready, place, values, gains, shifts, *refs):
    weight, outs, (buffer, sems) = refs[: -3 - CUTS], refs[-3 - CUTS : -2], refs[-2:]
    expanded_out, packed = outs[0], outs[1:]
    steps = pieces.load(place, weight, buffer, sems)
    ready()
    shape, _ = standard(values[...])
    hidden = (shape * gains[row : row + 1] + shifts[row : row + 1]).astype(jnp.bfloat16)
    store_part(packed, 0, hidden)
    for r, (index, copies) in enumerate(steps):
        for copy in copies:
            copy.wait()
        expanded = dot_rows(hidden, pieces.block(buffer, index))
        expanded_out[r] = expanded.astype(jnp.bfloat16)
        store_part(packed, 1 + r, (expanded * sigmoid(expanded)).astype(jnp.bfloat16))


def up_step(order, place, gather, index, row, values, gains, shifts):
    pieces = Pieces(gather, index)
    tokens, width = values.shape
    expanded, *packed = order.call(
        functools.partial(up_kernel, pieces, row),
        [
            jax.ShapeDtypeStruct((QUARTERS, tokens, pieces.part), jnp.bfloat16),
            *packed_shapes(1 + QUARTERS, tokens, width),
        ],
        [SMEM_SPACE] + [VMEM_SPACE] * 3 + [ANY_SPACE] * len(pieces.operands),
        [VMEM_SPACE] * (1 + CUTS),
        pieces.scratch,
        [place, values, gains, shifts, *pieces.operands],
        lazy=True,
    )
    return expanded, packed


def down_sum(pieces, ready, place, packed, first, weight, buffer, sems):
    total, steps = None, pieces.load(place, weight, buffer, sems)
    ready()
    for r, (index, copies) in enumerate(steps):
        for copy in copies:
            copy.wait()
        term = dot_cols(
            load_part(packed, first + r, pieces.part), pieces.block(buffer, index)
        )
        total = term if total is None else total + term
    return total


def down_kernel(pieces, ready, place, values, *refs):
    active, weight, (out, buffer, sems) = refs[:CUTS], refs[CUTS:-3], refs[-3:]
    branch = down_sum(pieces, ready, place, active, 1, weight, buffer, sems)
    out[...] = values[...] + 0.5 * branch


def down_step(order, place, gather, index, values, active):
    pieces = Pieces(gather, index)
    return order.call(
        functools.partial(down_kernel, pieces),
        [jax.ShapeDtypeStruct(values.shape, jnp.float32)],
        [SMEM_SPACE] + [VMEM_SPACE] * (1 + CUTS) + [ANY_SPACE] * len(pieces.operands),
        [VMEM_SPACE],
        pieces.scratch,
        [place, values, *active, *pieces.operands],
        lazy=True,
    )[0]


def last_kernel(pieces, row, ready, place, values, cotangent, gains, shifts, *refs):
    active, weight, outs = refs[:CUTS], refs[CUTS:-7], refs[-7:]
    encoded, grad_out, low_out, gain_out, shift_out, buffer, sems = outs
    branch = down_sum(pieces, ready, place, active, 1, weight, buffer, sems)
    total = values[...] + 0.5 * branch
    gain = gains[row : row + 1]
    shape, _ = standard(total)
    encoded[...] = (shape * gain + shifts[row : row + 1]).astype(jnp.bfloat16)
    back, gain_grad, shift_grad = norm_back(total, cotangent[...].astype(jnp.float32), gain)
    grad_out[...] = back
    low_out[0] = (0.5 * back).astype(jnp.bfloat16)
    gain_out[...] = gain_grad
    shift_out[...] = shift_grad


def vector_shapes(width, count=2):
    return [jax.ShapeDtypeStruct((1, width), jnp.float32)] * count


def last_step(order, place, gather, index, row, values, active, cotangent, gains, shifts):
    pieces = Pieces(gather, index)
    return order.call(
        functools.partial(last_kernel, pieces, row),
        [
            jax.ShapeDtypeStruct(values.shape, jnp.bfloat16),
            jax.ShapeDtypeStruct(values.shape, jnp.float32),
            jax.ShapeDtypeStruct((1, *values.shape), jnp.bfloat16),
            *vector_shapes(values.shape[1]),
        ],
        [SMEM_SPACE] + [VMEM_SPACE] * (4 + CUTS) + [ANY_SPACE] * len(pieces.operands),
        [VMEM_SPACE] * 5,
        pieces.scratch,
        [place, values, cotangent, gains, shifts, *active, *pieces.operands],
        lazy=True,
    )


def down_back_kernel(pieces, ready, place, gradient, expanded, *refs):
    weight, outs, (buffer, sems) = refs[: -2 - CUTS], refs[-2 - CUTS : -2], refs[-2:]
    steps = pieces.load(place, weight, buffer, sems)
    ready()
    for r, (index, copies) in enumerate(steps):
        for copy in copies:
            copy.wait()
        active_grad = dot_rows(gradient[0], pieces.block(buffer, index))
        store_part(outs, r, silu_back(expanded[r].astype(jnp.float32), active_grad).astype(jnp.bfloat16))


def down_back_step(order, place, gather, index, gradient, expanded, through=()):
    pieces = Pieces(gather, index)
    return order.call(
        functools.partial(down_back_kernel, pieces),
        packed_shapes(QUARTERS, gradient.shape[1], pieces.part),
        [SMEM_SPACE] + [VMEM_SPACE] * 2 + [ANY_SPACE] * len(pieces.operands),
        [VMEM_SPACE] * CUTS,
        pieces.scratch,
        [place, gradient, expanded, *pieces.operands],
        through,
        lazy=True,
    )


def into_norm_kernel(pieces, first, row, scale, ready, place, values, residual, gains, *refs):
    gradient, refs = refs[:CUTS], refs[CUTS:]
    weight, (grad_out, low_out, gain_out, shift_out, buffer, sems) = refs[:-6], refs[-6:]
    hidden_grad = down_sum(pieces, ready, place, gradient, first, weight, buffer, sems)
    back, gain_grad, shift_grad = norm_back(values[...], hidden_grad, gains[row : row + 1])
    total = residual[...] + back
    grad_out[...] = total
    low_out[0] = (scale * total).astype(jnp.bfloat16)
    gain_out[...] = gain_grad
    shift_out[...] = shift_grad


def into_norm_step(
    order, place, gather, index, first, row, scale, gradient, values, residual, gains, through=()
):
    pieces = Pieces(gather, index)
    return order.call(
        functools.partial(into_norm_kernel, pieces, first, row, scale),
        [
            jax.ShapeDtypeStruct(values.shape, jnp.float32),
            jax.ShapeDtypeStruct((1, *values.shape), jnp.bfloat16),
            *vector_shapes(values.shape[1]),
        ],
        [SMEM_SPACE] + [VMEM_SPACE] * (3 + CUTS) + [ANY_SPACE] * len(pieces.operands),
        [VMEM_SPACE] * 4,
        pieces.scratch,
        [place, values, residual, gains, *gradient, *pieces.operands],
        through,
        lazy=True,
    )


def whole_weight(pieces, ready, place, weight, buffer, sems):
    steps = pieces.load(place, weight, buffer, sems)
    ready()
    wait_all(steps)


def turn(values, cosine, sine):
    return values * cosine + pltpu.roll(values, HEAD_DIM // 2, 1) * sine


def masked_scores(query, key, matching):
    return jnp.where(matching, dot_cols(query, key), MASKED)


def head(index):
    return slice(index * HEAD_DIM, (index + 1) * HEAD_DIM)


def attend_kernel(pieces, row, ready, place, values, gains, shifts, cosine, sine, down, across, *refs):
    weight, outs = refs[:-6], refs[-6:]
    turned_out, totals_out, packed, projected, buffer, sems = outs
    steps = pieces.load(place, weight, buffer, sems)
    ready()
    shape, _ = standard(values[...])
    hidden = (shape * gains[row : row + 1] + shifts[row : row + 1]).astype(jnp.bfloat16)
    packed[0] = hidden
    for index, copies in steps:
        for copy in copies:
            copy.wait()
        column = pl.ds(pl.multiple_of(index * pieces.part, pieces.part), pieces.part)
        projected[:, column] = dot_rows(hidden, pieces.block(buffer, index))
    heads = pieces.width // (3 * HEAD_DIM)
    matching = down[...] == across[...]
    for h in range(heads):
        query = turn(projected[:, head(h)], cosine[...], sine[...]) * HEAD_DIM ** (-0.5)
        key = turn(projected[:, head(heads + h)], cosine[...], sine[...])
        query, key = query.astype(jnp.bfloat16), key.astype(jnp.bfloat16)
        value = projected[:, head(2 * heads + h)].astype(jnp.bfloat16)
        turned_out[:, head(h)] = query
        turned_out[:, head(heads + h)] = key
        turned_out[:, head(2 * heads + h)] = value
        scores = masked_scores(query, key, matching)
        highest = jnp.max(scores, axis=-1, keepdims=True)
        powers = jnp.exp(scores - highest)
        total = jnp.sum(powers, axis=-1, keepdims=True)
        totals_out[:, h : h + 1] = highest + jnp.log(total)
        probs = (powers / total).astype(jnp.bfloat16)
        packed[1, :, head(h)] = dot_rows(probs, value).astype(jnp.bfloat16)


def attend_step(order, place, gather, index, row, values, gains, shifts, cosine, sine, down, across):
    pieces = Pieces(gather, index)
    tokens, width = values.shape
    heads = pieces.width // (3 * HEAD_DIM)
    return order.call(
        functools.partial(attend_kernel, pieces, row),
        [
            jax.ShapeDtypeStruct((tokens, pieces.width), jnp.bfloat16),
            jax.ShapeDtypeStruct((tokens, heads), jnp.float32),
            jax.ShapeDtypeStruct((2, tokens, width), jnp.bfloat16),
        ],
        [SMEM_SPACE] + [VMEM_SPACE] * 7 + [ANY_SPACE] * len(pieces.operands),
        [VMEM_SPACE] * 3,
        [pltpu.VMEM((tokens, pieces.width), jnp.float32), *pieces.scratch],
        [place, values, gains, shifts, cosine, sine, down, across, *pieces.operands],
        lazy=True,
    )


def to_quarters(place, outs, column, values):
    part = values.shape[1] // QUARTERS
    for r in range(QUARTERS):
        block = values[:, pl.ds(pl.multiple_of((place[0] ^ r) * part, part), part)]
        store_part(outs, r, block, slice(column, column + part))


def attend_back_kernel(pieces, ready, place, gradient, turned, totals, cosine, sine, down, across, *refs):
    weight, rest = refs[: -4 - CUTS], refs[-4 - CUTS :]
    outs, (out, mixed_grad, buffer, sems) = rest[:CUTS], rest[CUTS:]
    heads = turned.shape[1] // (3 * HEAD_DIM)
    whole_weight(pieces, ready, place, weight, buffer, sems)
    total = None
    for index in range(QUARTERS):
        column = slice(index * pieces.part, (index + 1) * pieces.part)
        term = dot_cols(gradient[0, :, column], pieces.block(buffer, index))
        total = term if total is None else total + term
    mixed_grad[...] = total.astype(jnp.bfloat16)
    matching = down[...] == across[...]
    for h in range(heads):
        query = turned[:, head(h)]
        key = turned[:, head(heads + h)]
        value = turned[:, head(2 * heads + h)]
        gradient_h = mixed_grad[:, head(h)]
        probs = jnp.exp(masked_scores(query, key, matching) - totals[:, h : h + 1])
        value_grad = dot_down(probs.astype(jnp.bfloat16), gradient_h)
        probs_grad = dot_cols(gradient_h, value)
        inner = jnp.sum(probs * probs_grad, axis=-1, keepdims=True)
        score_grad = (probs * (probs_grad - inner)).astype(jnp.bfloat16)
        query_grad = dot_rows(score_grad, key) * HEAD_DIM ** (-0.5)
        key_grad = dot_down(score_grad, query)
        out[:, head(h)] = turn(query_grad, cosine[...], -sine[...]).astype(jnp.bfloat16)
        out[:, head(heads + h)] = turn(key_grad, cosine[...], -sine[...]).astype(jnp.bfloat16)
        out[:, head(2 * heads + h)] = value_grad.astype(jnp.bfloat16)
    to_quarters(place, outs, 0, out)


def attend_back_step(order, place, gather, index, gradient, turned, totals, cosine, sine, down, across):
    pieces = Pieces(gather, index)
    return order.call(
        functools.partial(attend_back_kernel, pieces),
        packed_shapes(QUARTERS, turned.shape[0], turned.shape[1] // QUARTERS),
        [SMEM_SPACE] + [VMEM_SPACE] * 7 + [ANY_SPACE] * len(pieces.operands),
        [VMEM_SPACE] * CUTS,
        [
            pltpu.VMEM(turned.shape, jnp.bfloat16),
            pltpu.VMEM(gradient.shape[1:], jnp.bfloat16),
            *pieces.scratch,
        ],
        [place, gradient, turned, totals, cosine, sine, down, across, *pieces.operands],
        lazy=True,
    )


def rows_sum(pieces, buffer, left):
    return jnp.concatenate(
        [dot_rows(left, pieces.block(buffer, index)) for index in range(QUARTERS)], axis=1
    )


def shifted(values, amount):
    return values if amount == 0 else pltpu.roll(values, amount % values.shape[0], 0)


def merge_kernel(pieces, ready, place, values, mixed, *refs):
    weight, (out, buffer, sems) = refs[:-3], refs[-3:]
    whole_weight(pieces, ready, place, weight, buffer, sems)
    for index in range(QUARTERS):
        column = slice(index * pieces.part, (index + 1) * pieces.part)
        out[:, column] = values[:, column] + dot_rows(mixed[1], pieces.block(buffer, index))


def merge_step(order, place, gather, index, values, mixed):
    pieces = Pieces(gather, index)
    return order.call(
        functools.partial(merge_kernel, pieces),
        [jax.ShapeDtypeStruct(values.shape, jnp.float32)],
        [SMEM_SPACE] + [VMEM_SPACE] * 2 + [ANY_SPACE] * len(pieces.operands),
        [VMEM_SPACE],
        pieces.scratch,
        [place, values, mixed, *pieces.operands],
        lazy=True,
    )[0]


def conv_kernel(weights, row, ready, place, values, gains, shifts, taps, keep, *refs):
    count = len(weights[0].operands)
    operands = [refs[i * count : (i + 1) * count] for i in range(len(weights))]
    rest = refs[len(weights) * count :]
    done_out, doubled_out, filtered_out, packed = rest[:4]
    scratch = rest[4:]
    buffers = [scratch[2 * i : 2 * i + 2] for i in range(len(weights))]
    steps = [w.load(place, o, *b) for w, o, b in zip(weights, operands, buffers)]
    gating, pointwise = weights
    ready()
    shape, _ = standard(values[...])
    hidden = (shape * gains[row : row + 1] + shifts[row : row + 1]).astype(jnp.bfloat16)
    packed[0] = hidden
    wait_all(steps[0])
    doubled = rows_sum(gating, buffers[0][0], hidden)
    doubled_out[...] = doubled.astype(jnp.bfloat16)
    half = gating.width // 2
    gated = doubled[:, :half] * sigmoid(doubled[:, half:])
    reach = taps.shape[0] // 2
    filtered = None
    for k in range(taps.shape[0]):
        term = shifted(gated, reach - k) * keep[:, k : k + 1] * taps[k : k + 1]
        filtered = term if filtered is None else filtered + term
    filtered_out[...] = filtered
    shape, _ = standard(filtered)
    renormed = shape * gains[row + 1 : row + 2] + shifts[row + 1 : row + 2]
    active = (renormed * sigmoid(renormed)).astype(jnp.bfloat16)
    packed[1] = active
    wait_all(steps[1])
    for index in range(QUARTERS):
        column = slice(index * pointwise.part, (index + 1) * pointwise.part)
        term = dot_rows(active, pointwise.block(buffers[1][0], index))
        done_out[:, column] = values[:, column] + term


def conv_step(order, place, gather, row, values, gains, shifts, taps, keep):
    weights = [Pieces(gather, i) for i in range(2)]
    tokens, width = values.shape
    operands = [o for w in weights for o in w.operands]
    return order.call(
        functools.partial(conv_kernel, weights, row),
        [
            jax.ShapeDtypeStruct((tokens, width), jnp.float32),
            jax.ShapeDtypeStruct((tokens, weights[0].width), jnp.bfloat16),
            jax.ShapeDtypeStruct((tokens, weights[0].width // 2), jnp.float32),
            jax.ShapeDtypeStruct((2, tokens, width), jnp.bfloat16),
        ],
        [SMEM_SPACE] + [VMEM_SPACE] * 5 + [ANY_SPACE] * len(operands),
        [VMEM_SPACE] * 4,
        [s for w in weights for s in w.scratch],
        [place, values, gains, shifts, taps, keep, *operands],
        lazy=True,
    )


def conv_back_kernel(pieces, row, ready, place, gradient, filtered, doubled, gains, shifts, taps, keep, *refs):
    weight, rest = refs[: -6 - CUTS], refs[-6 - CUTS :]
    outs = rest[:CUTS]
    gain_out, shift_out, taps_out, doubled_grad, buffer, sems = rest[CUTS:]
    whole_weight(pieces, ready, place, weight, buffer, sems)
    total = None
    for index in range(QUARTERS):
        column = slice(index * pieces.part, (index + 1) * pieces.part)
        term = dot_cols(gradient[0, :, column], pieces.block(buffer, index))
        total = term if total is None else total + term
    gain = gains[row : row + 1]
    shape, _ = standard(filtered[...])
    renormed = shape * gain + shifts[row : row + 1]
    back, gain_grad, shift_grad = norm_back(filtered[...], silu_back(renormed, total), gain)
    gain_out[...] = gain_grad
    shift_out[...] = shift_grad
    half = doubled.shape[1] // 2
    gate = sigmoid(doubled[:, half:].astype(jnp.float32))
    gated = doubled[:, :half].astype(jnp.float32) * gate
    reach = taps.shape[0] // 2
    gated_grad = None
    for k in range(taps.shape[0]):
        kept = back * keep[:, k : k + 1]
        taps_out[k : k + 1] = jnp.sum(kept * shifted(gated, reach - k), axis=0, keepdims=True)
        term = shifted(kept, k - reach) * taps[k : k + 1]
        gated_grad = term if gated_grad is None else gated_grad + term
    doubled_grad[:, :half] = (gated_grad * gate).astype(jnp.bfloat16)
    doubled_grad[:, half:] = (gated_grad * gated * (1.0 - gate)).astype(jnp.bfloat16)
    to_quarters(place, outs, 0, doubled_grad)


def conv_back_step(order, place, gather, index, row, gradient, filtered, doubled, gains, shifts, taps, keep):
    pieces = Pieces(gather, index)
    width = filtered.shape[1]
    return order.call(
        functools.partial(conv_back_kernel, pieces, row),
        [
            *packed_shapes(QUARTERS, doubled.shape[0], doubled.shape[1] // QUARTERS),
            *vector_shapes(width),
            jax.ShapeDtypeStruct(taps.shape, jnp.float32),
        ],
        [SMEM_SPACE] + [VMEM_SPACE] * 7 + [ANY_SPACE] * len(pieces.operands),
        [VMEM_SPACE] * (3 + CUTS),
        [pltpu.VMEM(doubled.shape, jnp.bfloat16), *pieces.scratch],
        [place, gradient, filtered, doubled, gains, shifts, taps, keep, *pieces.operands],
        lazy=True,
    )


def shards(
    sizes,
    frames,
    lengths,
    languages,
    embedding,
    gains,
    shifts,
    firstup,
    firstdown,
    projection,
    merger,
    gating,
    kernel,
    pointwise,
    secondup,
    seconddown,
    cotangent,
):
    frame_count = frames.shape[0]
    dp_index = lax.axis_index("dp").astype(jnp.int32)
    place = jnp.stack(
        [
            lax.rem(dp_index, jnp.int32(QUARTERS)),
            lax.axis_index("z").astype(jnp.int32),
            lax.axis_index("core").astype(jnp.int32),
        ]
    )
    order = Order(frames)
    order_of_groups = (
        ([firstup], [firstdown]),
        ([projection, merger], [gating, pointwise]),
        ([secondup],),
        ([seconddown],),
    )
    sources = [GatherSet(place, groups) for groups in order_of_groups]
    everything = jnp.concatenate([w for s in order_of_groups for g in s for w in g], axis=1)
    everything_other = swap_core(everything)
    gathers, other_base = [], 0
    for source, groups in zip(sources, order_of_groups):
        base = 0
        for group in groups:
            gathers.append(
                Gather(place, sizes, order, group, source, base, everything_other, other_base)
            )
            base += gathers[-1].width
            other_base += QUARTERS * gathers[-1].width
    table_full, gain_full, shift_full, kernel_full = gather_small(
        [embedding, gains, shifts, kernel]
    )
    segment_all, position_all, language_all = layout(lengths, languages, frame_count)
    segment = segment_all[0]
    language_row = language_all[0]
    cosine, sine = angles(position_all[0])
    cosine = jnp.concatenate([cosine, cosine], axis=-1)[:, 0]
    sine = jnp.concatenate([-sine, sine], axis=-1)[:, 0]
    down, across = segment[:, None], segment[None, :]
    gain_rows = gain_full.astype(jnp.float32)
    shift_rows = shift_full.astype(jnp.float32)
    taps = kernel_full.astype(jnp.float32)
    reach = taps.shape[0] // 2
    segment_pad = jnp.pad(segment, (reach, reach), constant_values=-1)
    keep = jnp.stack(
        [segment_pad[k : k + frame_count] == segment for k in range(taps.shape[0])], axis=1
    ).astype(jnp.float32)
    language_hot = (
        language_row[:, None] == jnp.arange(table_full.shape[0], dtype=jnp.int32)[None, :]
    ).astype(jnp.float32)
    start_sum = frames.astype(jnp.float32) + jnp.dot(
        language_hot.astype(jnp.bfloat16), table_full, preferred_element_type=jnp.float32
    )

    gathers[0].near(40)
    gathers[1].near(32)
    order.wait(everything_other)
    gathers[0].far()
    order.wait(gathers[0].rest)
    gathers[2].near(24)
    gathers[1].far()
    gathers[3].near(16)
    first_expanded, first_packed = up_step(
        order, place, gathers[0], 0, 0, start_sum, gain_rows, shift_rows
    )
    gathers[2].far()
    gathers[4].near(8)
    after_first = down_step(order, place, gathers[1], 0, start_sum, first_packed)
    gathers[3].far()
    gathers[5].near(0)
    turned, totals, attend_packed = attend_step(
        order, place, gathers[2], 0, 1, after_first, gain_rows, shift_rows, cosine, sine, down, across
    )
    after_attention = merge_step(order, place, gathers[2], 1, after_first, attend_packed)
    gathers[4].far()
    after_conv, doubled, filtered, conv_packed = conv_step(
        order, place, gathers[3], 2, after_attention, gain_rows, shift_rows, taps, keep
    )
    gathers[5].far()
    second_expanded, second_packed = up_step(
        order, place, gathers[4], 0, 4, after_conv, gain_rows, shift_rows
    )
    second_forward = Packed(second_packed)
    encoded, grad_second, low_second, final_gain, final_shift = last_step(
        order,
        place,
        gathers[5],
        0,
        5,
        after_conv,
        second_packed,
        cotangent,
        gain_rows,
        shift_rows,
    )
    rounds = Rounds(place, sizes, order)

    low = Packed([low_second])
    down_two = Sums(Factor(low, 0, second_forward, 1, 0, seconddown.shape[1]))
    rounds.step([down_two], margin=80)
    *packed, first_packed_a, first_packed_b = down_back_step(
        order, place, gathers[5], 0, low_second, second_expanded, first_packed
    )
    backward, first_forward = Packed(packed), Packed([first_packed_a, first_packed_b])
    grad_conv, low_conv, second_gain, second_shift, *held = into_norm_step(
        order,
        place,
        gathers[4],
        0,
        0,
        4,
        1.0,
        packed,
        after_conv,
        grad_second,
        gain_rows,
        [conv_packed, attend_packed],
    )
    conv_forward, attend_forward = Packed(held[:1]), Packed(held[1:])
    up_two = Sums(Factor(second_forward, 0, backward, 0, 0, secondup.shape[1]))
    order.wait(*first_forward.all)
    rounds.step([up_two], margin=64)
    low = Packed([low_conv])
    order.wait(*conv_forward.all, *attend_forward.all)
    *packed, inner_gain, inner_shift, taps_grad = conv_back_step(
        order, place, gathers[3], 1, 3, low_conv, filtered, doubled, gain_rows, shift_rows, taps, keep
    )
    backward = Packed(packed)
    grad_attention, low_attention, outer_gain, outer_shift = into_norm_step(
        order,
        place,
        gathers[3],
        0,
        0,
        2,
        1.0,
        packed,
        after_attention,
        grad_conv,
        gain_rows,
    )
    conv = Sums(
        Factor(conv_forward, 0, backward, 0, 0, gating.shape[1]),
        Factor(conv_forward, 1, low, 0, 0, pointwise.shape[1], relative=False),
        Factor(attend_forward, 1, Packed([low_attention]), 0, 0, merger.shape[1], relative=False),
    )
    rounds.step([conv], [down_two], margin=48)
    packed = attend_back_step(
        order, place, gathers[2], 1, low_attention, turned, totals, cosine, sine, down, across
    )
    backward = Packed(packed)
    grad_first, low_first, attend_gain, attend_shift = into_norm_step(
        order,
        place,
        gathers[2],
        0,
        0,
        1,
        0.5,
        packed,
        after_first,
        grad_attention,
        gain_rows,
    )
    projection_factor = Factor(attend_forward, 0, backward, 0, 0, projection.shape[1])
    order.wait(*backward.all)
    low = Packed([low_first])
    packed = down_back_step(order, place, gathers[1], 0, low_first, first_expanded)
    backward = Packed(packed)
    down_one = Sums(Factor(low, 0, first_forward, 1, 0, firstdown.shape[1]))
    (down_two_mine,) = rounds.step([down_one], [up_two], [down_two], margin=32)
    frames_grad, low_start, first_gain, first_shift = into_norm_step(
        order, place, gathers[0], 0, 0, 0, 1.0, packed, start_sum, grad_first, gain_rows
    )
    up_one = Sums(Factor(first_forward, 0, backward, 0, 0, firstup.shape[1]))
    (up_two_mine,) = rounds.step([up_one], [conv], [up_two], margin=16)
    vectors = jnp.concatenate(
        [
            first_gain,
            attend_gain,
            outer_gain,
            inner_gain,
            second_gain,
            final_gain,
            first_shift,
            attend_shift,
            outer_shift,
            inner_shift,
            second_shift,
            final_shift,
            taps_grad,
        ]
    )
    small_packed = Packed([pack_small(language_hot, low_start[0], vectors)])
    last = Sums(
        projection_factor,
        Factor(small_packed, 0, small_packed, 1, 0, QUARTERS * LANES, relative=False),
    )
    order.wait(down_two_mine)
    (conv_mine,) = rounds.step([last], [down_one], [conv], margin=80)
    order.wait(up_two_mine)
    (down_one_mine,) = rounds.step([], [up_one], [down_one])
    order.wait(conv_mine)
    (up_one_mine,) = rounds.step([], [last], [up_one])
    pieces = rounds.share([down_two_mine, up_two_mine])
    order.wait(down_one_mine)
    (last_mine,) = rounds.step([], [], [last])
    middle_pieces = rounds.share([conv_mine, down_one_mine])
    seconddown_grad, secondup_grad = spread(
        order, place, [seconddown.shape[1], secondup.shape[1]], pieces
    )
    up_pieces = rounds.share([up_one_mine])
    middle = [gating, pointwise, merger, firstdown]
    gating_grad, pointwise_grad, merger_grad, firstdown_grad = spread(
        order, place, [w.shape[1] for w in middle], middle_pieces
    )
    pieces = rounds.share([last_mine])
    (firstup_grad,) = spread(order, place, [firstup.shape[1]], up_pieces)
    projection_grad, small = spread(
        order, place, [projection.shape[1], QUARTERS * LANES], pieces
    )
    counts = [embedding.shape[0], gains.shape[0], shifts.shape[0], kernel.shape[0]]
    table_sum, gain_sum, shift_sum, taps_sum = unpack_small(small, counts)
    return (
        encoded,
        frames_grad,
        table_sum,
        gain_sum,
        shift_sum,
        firstup_grad,
        firstdown_grad,
        projection_grad,
        merger_grad,
        gating_grad,
        taps_sum,
        pointwise_grad,
        secondup_grad,
        seconddown_grad,
    )


def solution(mesh):
    dp_size, fsdp_size = mesh.shape["dp"], mesh.shape["fsdp"]
    layers = fsdp_size // 2
    split = Mesh(mesh.devices.reshape(dp_size, layers, 2), ("dp", "z", "core"))
    return jax.shard_map(
        functools.partial(shards, (dp_size, layers)),
        mesh=split,
        in_specs=(
            P(("dp", "z", "core"), None),
            P(("dp", "z", "core"), None),
            P(("dp", "z", "core"), None),
            P(None, ("z", "core")),
            P(None, ("z", "core")),
            P(None, ("z", "core")),
            P(("z", "core"), None),
            P(("z", "core"), None),
            P(("z", "core"), None),
            P(("z", "core"), None),
            P(("z", "core"), None),
            P(None, ("z", "core")),
            P(("z", "core"), None),
            P(("z", "core"), None),
            P(("z", "core"), None),
            P(("dp", "z", "core"), None),
        ),
        out_specs=(
            P(("dp", "z", "core"), None),
            P(("dp", "z", "core"), None),
            P(None, ("z", "core")),
            P(None, ("z", "core")),
            P(None, ("z", "core")),
            P(("z", "core"), None),
            P(("z", "core"), None),
            P(("z", "core"), None),
            P(("z", "core"), None),
            P(("z", "core"), None),
            P(None, ("z", "core")),
            P(("z", "core"), None),
            P(("z", "core"), None),
            P(("z", "core"), None),
        ),
        check_vma=False,
    )
```

```python
import functools

import jax
import jax.numpy as jnp
import numpy as np
from jax import lax
from jax.experimental import pallas as pl
from jax.experimental.pallas import tpu as pltpu
from jax.sharding import Mesh
from jax.sharding import PartitionSpec as P

HEAD_DIM = 128


def layout(lengths, languages, frame_count):
    utterances = jnp.arange(lengths.shape[-1], dtype=jnp.int32)
    earlier = utterances[:, None] <= utterances[None, :]
    finish = jnp.sum(jnp.where(earlier[None], lengths[:, :, None], 0), axis=1)
    begins = finish - lengths
    indices = jnp.arange(frame_count, dtype=jnp.int32)
    segment = jnp.sum((indices[None, :, None] >= finish[:, None, :]).astype(jnp.int32), axis=-1)
    owners = segment[:, :, None] == jnp.arange(lengths.shape[-1], dtype=jnp.int32)[None, None, :]
    first_row = jnp.sum(jnp.where(owners, begins[:, None, :], 0), axis=-1)
    language_row = jnp.sum(jnp.where(owners, languages[:, None, :], 0), axis=-1)
    return (segment, indices[None, :] - first_row, language_row)


def angles(position):
    half_dim = HEAD_DIM // 2
    frequency = 10000.0 ** (-jnp.arange(half_dim, dtype=jnp.float32) / half_dim)
    turned = position.astype(jnp.float32)[..., None] * frequency
    return (jnp.cos(turned)[..., None, :], jnp.sin(turned)[..., None, :])


VMEM_SPACE = pl.BlockSpec(memory_space=pltpu.VMEM)
SMEM_SPACE = pl.BlockSpec(memory_space=pltpu.SMEM)
ANY_SPACE = pl.BlockSpec(memory_space=pl.ANY)


class Order:
    def __init__(self, value):
        self.value, self.waits = value, []

    def wait(self, *arrays):
        self.waits += arrays

    def call(self, kernel, out_shape, in_specs, out_specs, scratch_shapes, operands, through=(), lazy=False):
        after, self.waits = self.waits, []
        carried = [*through, self.value]
        count, outs, extra = len(operands), len(out_shape), len(after)
        held_in = [i for i in range(count) if in_specs[i] is VMEM_SPACE]
        held_out = [i for i in range(outs) if out_specs[i] is VMEM_SPACE]
        buffers = [pltpu.VMEM(operands[i].shape, operands[i].dtype) for i in held_in]
        buffers += [pltpu.VMEM(out_shape[i].shape, out_shape[i].dtype) for i in held_out]
        copies = max(1, len(held_in), len(held_out))

        def body(*refs):
            ins, rest = list(refs[:count]), refs[count + extra + len(carried) :]
            results, rest = list(rest[:outs]), rest[outs + len(carried) :]
            held, scratch, sems = rest[: len(buffers)], rest[len(buffers) : -1], rest[-1]
            moves = []
            for at, i in enumerate(held_in):
                moves.append(pltpu.make_async_copy(ins[i], held[at], sems.at[at]))
                moves[-1].start()
                ins[i] = held[at]
            targets = []
            for at, i in enumerate(held_out):
                targets.append(results[i])
                results[i] = held[len(held_in) + at]
            def ready():
                for move in arriving:
                    move.wait()

            arriving = moves
            if lazy:
                kernel(ready, *ins, *results, *scratch)
            else:
                ready()
                kernel(*ins, *results, *scratch)
            moves = []
            for at, i in enumerate(held_out):
                moves.append(pltpu.make_async_copy(results[i], targets[at], sems.at[at]))
                moves[-1].start()
            for move in moves:
                move.wait()

        result = pl.pallas_call(
            body,
            out_shape=[*out_shape, *[jax.ShapeDtypeStruct(x.shape, x.dtype) for x in carried]],
            in_specs=[ANY_SPACE if s is VMEM_SPACE else s for s in in_specs]
            + [ANY_SPACE] * (extra + len(carried)),
            out_specs=[ANY_SPACE] * (outs + len(carried)),
            scratch_shapes=[*buffers, *scratch_shapes, pltpu.SemaphoreType.DMA((copies,))],
            input_output_aliases={count + extra + i: outs + i for i in range(len(carried))},
            compiler_params=pltpu.CompilerParams(vmem_limit_bytes=VMEM_LIMIT),
        )(*operands, *after, *carried)
        self.value = result[-1]
        return result[:-1]


VMEM_LIMIT = 52 * 1024 * 1024
QUARTERS = 4
LANES = 128
BITS = (0, 1)


def swap_dp(value, bit, size):
    return lax.ppermute(value, "dp", [(i, i ^ (1 << bit)) for i in range(size)])


def swap_core(value):
    return lax.ppermute(value, "core", [(0, 1), (1, 0)])


def swap_pairs(value, flip, size):
    pairs = []
    for i in range(size):
        for core in range(2):
            far = i ^ (1 << BITS[core ^ flip])
            pairs.append((2 * i + core, 2 * far + core))
    return lax.ppermute(value, ("dp", "core"), pairs)


def pick_kernel(layers, base, place, gathered, out, sems):
    layer = place[1]
    rows, copies = gathered.shape[1], []
    for k in range(1, layers):
        for lane in range(2):
            at = 2 * (k - 1) + lane
            row = lax.rem(layer + k, layers) * 2 + lane
            source = gathered.at[row, :, pl.ds(base, out.shape[1])]
            target = out.at[pl.ds(at * rows, rows)]
            copies.append(pltpu.make_async_copy(source, target, sems.at[at]))
            copies[-1].start()
    for copy in copies:
        copy.wait()


def pick(order, place, layers, gathered, base, width, margin):
    blocks = 2 * (layers - 1)
    return order.call(
        functools.partial(pick_kernel, layers, base),
        [jax.ShapeDtypeStruct((blocks * gathered.shape[1] + margin, width), gathered.dtype)],
        [SMEM_SPACE, ANY_SPACE],
        [VMEM_SPACE],
        [pltpu.SemaphoreType.DMA((blocks,))],
        [place, gathered],
    )[0]


def half_kernel(place, piece, out, sems):
    rows = out.shape[0]
    start = pl.multiple_of(place[2] * rows, rows)
    copy = pltpu.make_async_copy(piece.at[pl.ds(start, rows)], out, sems.at[0])
    copy.start()
    copy.wait()


def half(order, place, piece, rows):
    return order.call(
        half_kernel,
        [jax.ShapeDtypeStruct((rows // 2, piece.shape[1]), piece.dtype)],
        [SMEM_SPACE, ANY_SPACE],
        [VMEM_SPACE],
        [pltpu.SemaphoreType.DMA((1,))],
        [place, piece],
    )[0]


def join_kernel(*refs):
    ins, out, sems = refs[:-2], refs[-2], refs[-1]
    at, copies = 0, []
    for k, ref in enumerate(ins):
        target = out.at[:, pl.ds(at, ref.shape[1])]
        copies.append(pltpu.make_async_copy(ref, target, sems.at[k]))
        copies[-1].start()
        at += ref.shape[1]
    for copy in copies:
        copy.wait()


def join(order, arrays):
    width = sum(a.shape[1] for a in arrays)
    return order.call(
        join_kernel,
        [jax.ShapeDtypeStruct((arrays[0].shape[0], width), arrays[0].dtype)],
        [ANY_SPACE] * len(arrays),
        [VMEM_SPACE],
        [pltpu.SemaphoreType.DMA((len(arrays),))],
        arrays,
    )[0]


class Packed:
    def __init__(self, arrays):
        self.own = list(arrays)
        self.all = [*self.own, *[swap_core(a) for a in self.own]]
        self.tokens = sum(a.shape[1] for a in self.all)

    def part(self, index):
        return [(a, index, a.shape[1]) for a in self.all]


class Factor:
    def __init__(self, left, left_index, right, right_index, base, width, relative=True):
        self.left = left.part(left_index)
        self.right, self.right_index, self.base, self.relative = right, right_index, base, relative
        self.width, self.part, self.tokens = width, width // QUARTERS, left.tokens
        self.arrays = [*left.all, *right.all]

    def columns(self, quarter, r, start, width):
        if self.relative:
            index, column = self.right_index + r, pl.ds(self.base + start, width)
        else:
            index = self.right_index
            column = pl.ds(pl.multiple_of((quarter ^ r) * self.part + start, LANES), width)
        return [(a, index, column, count) for a, _, count in self.right.part(0)]


class Sums:
    def __init__(self, *factors):
        self.factors = factors
        self.width = sum(f.part for f in factors)

    def spans(self):
        base = 0
        for i, f in enumerate(self.factors):
            for start in range(0, f.part, TILE):
                yield i, start, min(TILE, f.part - start), base + start
            base += f.part


TILE = 512


def left_width(features, layers):
    return features // 2 if features // (2 * layers) % LANES == 0 else features


def left_spans(features, layers, core):
    rows = features // (2 * layers)
    if rows % LANES:
        return [(pl.ds(0, features), pl.ds(0, features))]
    return [
        (pl.ds(pl.multiple_of((2 * k + core) * rows, rows), rows), pl.ds(k * rows, rows))
        for k in range(layers)
    ]


def own_rows(values, features, layers, core):
    tokens, width = values.shape
    if width < features:
        return values.T
    rows = features // (2 * layers)
    turned = values.T.reshape(layers, 2, rows, tokens)
    return jnp.where(core == 0, turned[:, 0], turned[:, 1]).reshape(layers * rows, tokens)


def round_kernel(layers, plan, tables, place, *refs):
    jobs, lefts, count_in, count_out = plan
    ins, outs = refs[:count_in], refs[count_in : count_in + count_out]
    left_buffer, turned, right_buffer, add_buffer, out_buffer, left_sems, in_sems, out_sems = refs[
        count_in + count_out :
    ]
    quarter, core = place[0], place[2]

    quarters = {"both": 3, "near": 1 + core, "far": 2 - core, "own": 0}

    def start(source, target, sem):
        copy = pltpu.make_async_copy(source, target, sem)
        copy.start()
        return copy

    left_copies = []
    for i, factor in enumerate(lefts):
        at, copies = 0, []
        for k, (array, index, rows) in enumerate(factor.left):
            source = ins[tables[id(array)]].at[index]
            spans = left_spans(source.shape[1], layers, core)
            for number, (columns, there) in enumerate(spans):
                target = left_buffer.at[i, at : at + rows, there]
                sem = left_sems.at[i, k * len(spans) + number]
                copies.append(start(source.at[:, columns], target, sem))
            at += rows
        left_copies.append(copies)
    loads = []
    for number, (i, r, first, width, adds, _) in enumerate(jobs):
        at, copies = 0, []
        for array, index, column, rows in lefts[i].columns(quarter, quarters[r], first, width):
            source = ins[tables[id(array)]].at[index, :, column]
            target = right_buffer.at[number, at : at + rows, pl.ds(0, width)]
            copies.append(start(source, target, in_sems.at[number, len(copies)]))
            at += rows
        for k, (array, column) in enumerate(adds):
            height = add_buffer.shape[2]
            source = ins[tables[id(array)]].at[pl.ds(0, height), pl.ds(column, width)]
            target = add_buffer.at[number, k, :, pl.ds(0, width)]
            copies.append(start(source, target, in_sems.at[number, len(copies)]))
        loads.append(copies)
    for i, factor in enumerate(lefts):
        for copy in left_copies[i]:
            copy.wait()
        turned[i, :, : factor.tokens] = own_rows(
            left_buffer[i, : factor.tokens], factor.left[0][0].shape[2], layers, core
        )
    stores = []
    for number, (i, _, _, width, adds, (out, column)) in enumerate(jobs):
        tokens = lefts[i].tokens
        for copy in loads[number]:
            copy.wait()
        product = jnp.dot(
            turned[i, :, :tokens],
            right_buffer[number, :tokens, :width],
            preferred_element_type=jnp.float32,
        )
        for k in range(len(adds)):
            product += add_buffer[number, k, :, :width].astype(jnp.float32)
        out_buffer[number, :, :width] = product.astype(jnp.bfloat16)
        source = out_buffer.at[number, :, pl.ds(0, width)]
        target = outs[out].at[pl.ds(0, out_buffer.shape[1]), pl.ds(column, width)]
        stores.append(start(source, target, out_sems.at[number]))
    for copy in stores:
        copy.wait()


class Rounds:
    def __init__(self, place, sizes, order):
        self.place, self.order = place, order
        self.dp_size, self.layers = sizes

    def step(self, halves=(), quarters=(), rows=(), margin=0):
        lefts, jobs, widths = [], [], [0] * (2 + len(rows))

        def left(factor):
            if factor not in lefts:
                lefts.append(factor)
            return lefts.index(factor)

        def add(sums, r, out, adds):
            base = widths[out]
            for i, first, width, at in sums.spans():
                mine = [(array, offset + at) for array, offset in adds]
                jobs.append((left(sums.factors[i]), r, first, width, mine, (out, base + at)))
            widths[out] += sums.width
            return base

        sent = []
        for sums in halves:
            sums.near_at = add(sums, "both", 0, [])
            sums.own_at = add(sums, "near", 0, [])
        for sums in quarters:
            sums.far_at = add(sums, "far", 1, [(sums.halves, sums.near_at)])
        for number, sums in enumerate(rows):
            add(sums, "own", 2 + number, [(sums.halves, sums.own_at), (sums.quarters, sums.far_at)])
        slots = [k for k in range(2 + len(rows)) if widths[k]]
        jobs = [job[:5] + ((slots.index(job[5][0]), job[5][1]),) for job in jobs]
        arrays, tables = [], {}
        used = [a for factor in lefts for a in factor.arrays] + [a for job in jobs for a, _ in job[4]]
        for array in used:
            if id(array) not in tables:
                tables[id(array)] = len(arrays)
                arrays.append(array)
        height = lefts[0].left[0][0].shape[2] // 2
        features = lefts[0].left[0][0].shape[2]
        tokens = max(factor.tokens for factor in lefts)
        widest = max(job[3] for job in jobs)
        depth = max(1, max(len(job[4]) for job in jobs))
        pieces = max(len(factor.left) for factor in lefts)
        rights = max(len(factor.right.all) for factor in lefts)
        outs = self.order.call(
            functools.partial(
                round_kernel, self.layers, (jobs, lefts, len(arrays), len(slots)), tables
            ),
            [
                jax.ShapeDtypeStruct((height + (margin if k == 0 else 0), widths[k]), jnp.bfloat16)
                for k in slots
            ],
            [SMEM_SPACE] + [ANY_SPACE] * len(arrays),
            [ANY_SPACE] * len(slots),
            [
                pltpu.VMEM(
                    (len(lefts), tokens, left_width(features, self.layers)), jnp.bfloat16
                ),
                pltpu.VMEM((len(lefts), height, tokens), jnp.bfloat16),
                pltpu.VMEM((len(jobs), tokens, widest), jnp.bfloat16),
                pltpu.VMEM((len(jobs), depth, height, widest), jnp.bfloat16),
                pltpu.VMEM((len(jobs), height, widest), jnp.bfloat16),
                pltpu.SemaphoreType.DMA((len(lefts), pieces * self.layers)),
                pltpu.SemaphoreType.DMA((len(jobs), rights + depth)),
                pltpu.SemaphoreType.DMA((len(jobs),)),
            ],
            [self.place, *arrays],
        )
        moved = {k: swap_pairs(outs[slots.index(k)], k, self.dp_size) for k in slots if k < 2}
        for sums in halves:
            sums.halves = moved[0]
        for sums in quarters:
            sums.quarters = moved[1]
        return [
            lax.psum_scatter(outs[slots.index(k)], "z", scatter_dimension=0, tiled=True)
            for k in slots
            if k >= 2
        ]

    def share(self, mine):
        summed = join(self.order, mine)
        bit = len(BITS)
        while 1 << bit < self.dp_size:
            summed = summed + swap_dp(summed, bit, self.dp_size)
            bit += 1
        near = swap_pairs(summed, 0, self.dp_size)
        far = swap_pairs(summed, 1, self.dp_size)
        return [summed, near, far, swap_pairs(near, 1, self.dp_size)]


def spread_kernel(widths, place, *refs):
    pieces, outs = refs[:QUARTERS], refs[QUARTERS:]
    quarter, core = place[0], place[2]
    base = 0
    for i, width in enumerate(widths):
        part = width // QUARTERS
        for r, place_of in enumerate((0, 1 + core, 2 - core, 3)):
            column = pl.ds(pl.multiple_of((quarter ^ place_of) * part, part), part)
            outs[i][:, column] = pieces[r][:, pl.ds(base, part)].astype(jnp.float32)
        base += part


def spread(order, place, widths, pieces):
    rows = pieces[0].shape[0]
    return order.call(
        functools.partial(spread_kernel, widths),
        [jax.ShapeDtypeStruct((rows, w), jnp.float32) for w in widths],
        [SMEM_SPACE] + [VMEM_SPACE] * QUARTERS,
        [VMEM_SPACE] * len(widths),
        [],
        [place, *pieces],
    )


class GatherSet:
    def __init__(self, place, groups):
        quarter = place[0]
        mine = [
            lax.dynamic_slice_in_dim(w, quarter * (w.shape[1] // QUARTERS), w.shape[1] // QUARTERS, 1)
            for group in groups
            for w in group
        ]
        mine = jnp.concatenate(mine, axis=1) if len(mine) > 1 else mine[0]
        self.gathered = lax.all_gather(mine, ("z", "core"), axis=0, tiled=False)


class Gather:
    def __init__(self, place, sizes, order, group, source, base, other, other_base):
        self.place, self.order, self.group = place, order, group
        self.dp_size, self.layers = sizes
        self.source, self.base, self.other, self.other_base = source, base, other, other_base
        self.width = sum(w.shape[1] for w in group) // QUARTERS
        self.rows = 2 * (self.layers - 1) * group[0].shape[0]

    def near(self, margin):
        piece = pick(
            self.order, self.place, self.layers, self.source.gathered, self.base, self.width, margin
        )
        self.piece = swap_pairs(piece, 0, self.dp_size)
        self.other_piece = swap_core(self.piece)

    def arrived(self):
        return [self.other_piece, self.rest, self.other_rest]

    def far(self):
        self.rest = swap_pairs(half(self.order, self.place, self.piece, self.rows), 1, self.dp_size)
        self.other_rest = swap_core(self.rest)


def gather_small(arrays):
    rows = [a.shape[0] for a in arrays]
    packed = jnp.concatenate(arrays, axis=0)
    packed = jnp.pad(packed, ((0, -packed.shape[0] % 16), (0, 0)))
    full = lax.all_gather(packed, ("z", "core"), axis=0, tiled=False)
    full = full.transpose(1, 0, 2).reshape(packed.shape[0], -1)
    pieces, start = [], 0
    for count in rows:
        pieces.append(full[start : start + count])
        start += count
    return pieces


def pack_small(table_hot, frames_grad, vectors):
    count = table_hot.shape[1]
    extra = -(frames_grad.shape[0] + vectors.shape[0]) % 16
    left = jnp.concatenate([frames_grad, vectors, jnp.zeros((extra, vectors.shape[1]), vectors.dtype)])
    used = count + vectors.shape[0]
    share = -(-used // QUARTERS)
    unit = jnp.eye(vectors.shape[0], dtype=table_hot.dtype)
    right = jnp.block(
        [
            [table_hot, jnp.zeros((table_hot.shape[0], vectors.shape[0]), table_hot.dtype)],
            [jnp.zeros((vectors.shape[0], count), table_hot.dtype), unit],
        ]
    )
    right = jnp.pad(right, ((0, extra), (0, share * QUARTERS - used)))
    right = right.reshape(right.shape[0], QUARTERS, share)
    right = jnp.pad(right, ((0, 0), (0, 0), (0, LANES - share)))
    right = right.reshape(right.shape[0], QUARTERS * LANES)
    right = jnp.pad(right, ((0, 0), (0, left.shape[1] - right.shape[1])))
    return jnp.stack([left.astype(jnp.bfloat16), right.astype(jnp.bfloat16)])


def unpack_small(summed, counts):
    used = sum(counts)
    share = -(-used // QUARTERS)
    rows = summed.reshape(summed.shape[0], QUARTERS, LANES)[:, :, :share]
    rows = rows.reshape(summed.shape[0], QUARTERS * share).T
    pieces, start = [], 0
    for count in counts:
        pieces.append(rows[start : start + count])
        start += count
    return pieces

EPSILON = 1e-05
MASKED = -1000000000.0


def dot_rows(left, right):
    return jnp.dot(left, right, preferred_element_type=jnp.float32)


def dot_cols(left, right):
    return lax.dot_general(
        left, right, (((1,), (1,)), ((), ())), preferred_element_type=jnp.float32
    )


def dot_down(left, right):
    return jnp.dot(left.T, right, preferred_element_type=jnp.float32)


def standard(values):
    centred = values - jnp.mean(values, axis=-1, keepdims=True)
    spread = lax.rsqrt(jnp.mean(centred * centred, axis=-1, keepdims=True) + EPSILON)
    return centred * spread, spread


def norm_back(values, gradient, gain):
    shape, spread = standard(values)
    inner = gradient * gain
    back = spread * (
        inner
        - jnp.mean(inner, axis=-1, keepdims=True)
        - shape * jnp.mean(inner * shape, axis=-1, keepdims=True)
    )
    return (
        back,
        jnp.sum(gradient * shape, axis=0, keepdims=True),
        jnp.sum(gradient, axis=0, keepdims=True),
    )


def sigmoid(values):
    return 1.0 / (1.0 + jnp.exp(-values))


def silu_back(values, gradient):
    gate = sigmoid(values)
    return gradient * gate * (1.0 + values * (1.0 - gate))


CUTS = 2


def packed_shapes(parts, tokens, width):
    return [jax.ShapeDtypeStruct((parts, tokens // CUTS, width), jnp.bfloat16)] * CUTS


def store_part(outs, index, values, column=slice(None)):
    at = 0
    for out in outs:
        out[index, :, column] = values[at : at + out.shape[1]]
        at += out.shape[1]


def load_part(refs, index, width):
    return jnp.concatenate([ref[index, :, :width] for ref in refs], axis=0)


class Pieces:
    def __init__(self, gather, index):
        group = gather.group
        self.layers = gather.layers
        before = sum(w.shape[1] for w in group[:index])
        self.base = before // QUARTERS
        self.set_base = gather.base + self.base
        self.other_base = gather.other_base + before
        self.rows, self.width = group[index].shape
        self.operands = [
            group[index],
            gather.other,
            gather.source.gathered,
            gather.piece,
            gather.other_piece,
            gather.rest,
            gather.other_rest,
        ]

    @property
    def part(self):
        return self.width // QUARTERS

    @property
    def scratch(self):
        copies = 1 + (QUARTERS - 1) * 2 * self.layers
        return [
            pltpu.VMEM((QUARTERS, 2 * self.layers, self.rows, self.part), jnp.bfloat16),
            pltpu.SemaphoreType.DMA((copies,)),
        ]

    def load(self, place, refs, buffer, sems):
        own, other, gathered, piece, other_piece, rest, other_rest = refs
        quarter, layer, core = place[0], place[1], place[2]
        span = pl.ds(self.base, self.part)
        copies = []

        def move(source, target):
            copies.append(pltpu.make_async_copy(source, target, sems.at[len(copies)]))
            copies[-1].start()

        def blocks(source, index, first, count):
            for number in range(count):
                at = first + number
                row = lax.rem(layer + 1 + at // 2, self.layers) * 2 + lax.rem(at, 2)
                move(source.at[pl.ds(number * self.rows, self.rows), span], buffer.at[index, row])

        move(gathered.at[:, :, pl.ds(self.set_base, self.part)], buffer.at[quarter])
        for r in range(1, QUARTERS):
            index = quarter ^ r
            near = pl.multiple_of(index * self.part, LANES)
            far = pl.multiple_of(self.other_base + index * self.part, LANES)
            move(own.at[:, pl.ds(near, self.part)], buffer.at[index, 2 * layer + core])
            move(other.at[:, pl.ds(far, self.part)], buffer.at[index, 2 * layer + 1 - core])
        count = 2 * (self.layers - 1)
        blocks(piece, quarter ^ (1 + core), jnp.int32(0), count)
        blocks(other_piece, quarter ^ (2 - core), jnp.int32(0), count)
        blocks(rest, quarter ^ 3, core * (count // 2), count // 2)
        blocks(other_rest, quarter ^ 3, (1 - core) * (count // 2), count // 2)
        return [(quarter, copies[:1]), (quarter ^ 1, copies[1:]), (quarter ^ 2, []), (quarter ^ 3, [])]

    def block(self, buffer, index):
        return buffer[index].reshape(2 * self.layers * self.rows, self.part)


def wait_all(steps):
    for _, copies in steps:
        for copy in copies:
            copy.wait()


def up_kernel(pieces, row, ready, place, values, gains, shifts, *refs):
    weight, outs, (buffer, sems) = refs[: -3 - CUTS], refs[-3 - CUTS : -2], refs[-2:]
    expanded_out, packed = outs[0], outs[1:]
    steps = pieces.load(place, weight, buffer, sems)
    ready()
    shape, _ = standard(values[...])
    hidden = (shape * gains[row : row + 1] + shifts[row : row + 1]).astype(jnp.bfloat16)
    store_part(packed, 0, hidden)
    for r, (index, copies) in enumerate(steps):
        for copy in copies:
            copy.wait()
        expanded = dot_rows(hidden, pieces.block(buffer, index))
        expanded_out[r] = expanded.astype(jnp.bfloat16)
        store_part(packed, 1 + r, (expanded * sigmoid(expanded)).astype(jnp.bfloat16))


def up_step(order, place, gather, index, row, values, gains, shifts):
    pieces = Pieces(gather, index)
    tokens, width = values.shape
    expanded, *packed = order.call(
        functools.partial(up_kernel, pieces, row),
        [
            jax.ShapeDtypeStruct((QUARTERS, tokens, pieces.part), jnp.bfloat16),
            *packed_shapes(1 + QUARTERS, tokens, width),
        ],
        [SMEM_SPACE] + [VMEM_SPACE] * 3 + [ANY_SPACE] * len(pieces.operands),
        [VMEM_SPACE] * (1 + CUTS),
        pieces.scratch,
        [place, values, gains, shifts, *pieces.operands],
        lazy=True,
    )
    return expanded, packed


def down_sum(pieces, ready, place, packed, first, weight, buffer, sems):
    total, steps = None, pieces.load(place, weight, buffer, sems)
    ready()
    for r, (index, copies) in enumerate(steps):
        for copy in copies:
            copy.wait()
        term = dot_cols(
            load_part(packed, first + r, pieces.part), pieces.block(buffer, index)
        )
        total = term if total is None else total + term
    return total


def down_kernel(pieces, ready, place, values, *refs):
    active, weight, (out, buffer, sems) = refs[:CUTS], refs[CUTS:-3], refs[-3:]
    branch = down_sum(pieces, ready, place, active, 1, weight, buffer, sems)
    out[...] = values[...] + 0.5 * branch


def down_step(order, place, gather, index, values, active):
    pieces = Pieces(gather, index)
    return order.call(
        functools.partial(down_kernel, pieces),
        [jax.ShapeDtypeStruct(values.shape, jnp.float32)],
        [SMEM_SPACE] + [VMEM_SPACE] * (1 + CUTS) + [ANY_SPACE] * len(pieces.operands),
        [VMEM_SPACE],
        pieces.scratch,
        [place, values, *active, *pieces.operands],
        lazy=True,
    )[0]


def last_kernel(pieces, row, ready, place, values, cotangent, gains, shifts, *refs):
    active, weight, outs = refs[:CUTS], refs[CUTS:-7], refs[-7:]
    encoded, grad_out, low_out, gain_out, shift_out, buffer, sems = outs
    branch = down_sum(pieces, ready, place, active, 1, weight, buffer, sems)
    total = values[...] + 0.5 * branch
    gain = gains[row : row + 1]
    shape, _ = standard(total)
    encoded[...] = (shape * gain + shifts[row : row + 1]).astype(jnp.bfloat16)
    back, gain_grad, shift_grad = norm_back(total, cotangent[...].astype(jnp.float32), gain)
    grad_out[...] = back
    low_out[0] = (0.5 * back).astype(jnp.bfloat16)
    gain_out[...] = gain_grad
    shift_out[...] = shift_grad


def vector_shapes(width, count=2):
    return [jax.ShapeDtypeStruct((1, width), jnp.float32)] * count


def last_step(order, place, gather, index, row, values, active, cotangent, gains, shifts):
    pieces = Pieces(gather, index)
    return order.call(
        functools.partial(last_kernel, pieces, row),
        [
            jax.ShapeDtypeStruct(values.shape, jnp.bfloat16),
            jax.ShapeDtypeStruct(values.shape, jnp.float32),
            jax.ShapeDtypeStruct((1, *values.shape), jnp.bfloat16),
            *vector_shapes(values.shape[1]),
        ],
        [SMEM_SPACE] + [VMEM_SPACE] * (4 + CUTS) + [ANY_SPACE] * len(pieces.operands),
        [VMEM_SPACE] * 5,
        pieces.scratch,
        [place, values, cotangent, gains, shifts, *active, *pieces.operands],
        lazy=True,
    )


def down_back_kernel(pieces, ready, place, gradient, expanded, *refs):
    weight, outs, (buffer, sems) = refs[: -2 - CUTS], refs[-2 - CUTS : -2], refs[-2:]
    steps = pieces.load(place, weight, buffer, sems)
    ready()
    for r, (index, copies) in enumerate(steps):
        for copy in copies:
            copy.wait()
        active_grad = dot_rows(gradient[0], pieces.block(buffer, index))
        store_part(outs, r, silu_back(expanded[r].astype(jnp.float32), active_grad).astype(jnp.bfloat16))


def down_back_step(order, place, gather, index, gradient, expanded, through=()):
    pieces = Pieces(gather, index)
    return order.call(
        functools.partial(down_back_kernel, pieces),
        packed_shapes(QUARTERS, gradient.shape[1], pieces.part),
        [SMEM_SPACE] + [VMEM_SPACE] * 2 + [ANY_SPACE] * len(pieces.operands),
        [VMEM_SPACE] * CUTS,
        pieces.scratch,
        [place, gradient, expanded, *pieces.operands],
        through,
        lazy=True,
    )


def into_norm_kernel(pieces, first, row, scale, ready, place, values, residual, gains, *refs):
    gradient, refs = refs[:CUTS], refs[CUTS:]
    weight, (grad_out, low_out, gain_out, shift_out, buffer, sems) = refs[:-6], refs[-6:]
    hidden_grad = down_sum(pieces, ready, place, gradient, first, weight, buffer, sems)
    back, gain_grad, shift_grad = norm_back(values[...], hidden_grad, gains[row : row + 1])
    total = residual[...] + back
    grad_out[...] = total
    low_out[0] = (scale * total).astype(jnp.bfloat16)
    gain_out[...] = gain_grad
    shift_out[...] = shift_grad


def into_norm_step(
    order, place, gather, index, first, row, scale, gradient, values, residual, gains, through=()
):
    pieces = Pieces(gather, index)
    return order.call(
        functools.partial(into_norm_kernel, pieces, first, row, scale),
        [
            jax.ShapeDtypeStruct(values.shape, jnp.float32),
            jax.ShapeDtypeStruct((1, *values.shape), jnp.bfloat16),
            *vector_shapes(values.shape[1]),
        ],
        [SMEM_SPACE] + [VMEM_SPACE] * (3 + CUTS) + [ANY_SPACE] * len(pieces.operands),
        [VMEM_SPACE] * 4,
        pieces.scratch,
        [place, values, residual, gains, *gradient, *pieces.operands],
        through,
        lazy=True,
    )


def whole_weight(pieces, ready, place, weight, buffer, sems):
    steps = pieces.load(place, weight, buffer, sems)
    ready()
    wait_all(steps)


def turn(values, cosine, sine):
    return values * cosine + pltpu.roll(values, HEAD_DIM // 2, 1) * sine


def masked_scores(query, key, matching):
    return jnp.where(matching, dot_cols(query, key), MASKED)


def head(index):
    return slice(index * HEAD_DIM, (index + 1) * HEAD_DIM)


def attend_kernel(pieces, row, ready, place, values, gains, shifts, cosine, sine, down, across, *refs):
    weight, outs = refs[:-6], refs[-6:]
    turned_out, totals_out, packed, projected, buffer, sems = outs
    steps = pieces.load(place, weight, buffer, sems)
    ready()
    shape, _ = standard(values[...])
    hidden = (shape * gains[row : row + 1] + shifts[row : row + 1]).astype(jnp.bfloat16)
    packed[0] = hidden
    for index, copies in steps:
        for copy in copies:
            copy.wait()
        column = pl.ds(pl.multiple_of(index * pieces.part, pieces.part), pieces.part)
        projected[:, column] = dot_rows(hidden, pieces.block(buffer, index))
    heads = pieces.width // (3 * HEAD_DIM)
    matching = down[...] == across[...]
    for h in range(heads):
        query = turn(projected[:, head(h)], cosine[...], sine[...]) * HEAD_DIM ** (-0.5)
        key = turn(projected[:, head(heads + h)], cosine[...], sine[...])
        query, key = query.astype(jnp.bfloat16), key.astype(jnp.bfloat16)
        value = projected[:, head(2 * heads + h)].astype(jnp.bfloat16)
        turned_out[:, head(h)] = query
        turned_out[:, head(heads + h)] = key
        turned_out[:, head(2 * heads + h)] = value
        scores = masked_scores(query, key, matching)
        highest = jnp.max(scores, axis=-1, keepdims=True)
        powers = jnp.exp(scores - highest)
        total = jnp.sum(powers, axis=-1, keepdims=True)
        totals_out[:, h : h + 1] = highest + jnp.log(total)
        probs = (powers / total).astype(jnp.bfloat16)
        packed[1, :, head(h)] = dot_rows(probs, value).astype(jnp.bfloat16)


def attend_step(order, place, gather, index, row, values, gains, shifts, cosine, sine, down, across):
    pieces = Pieces(gather, index)
    tokens, width = values.shape
    heads = pieces.width // (3 * HEAD_DIM)
    return order.call(
        functools.partial(attend_kernel, pieces, row),
        [
            jax.ShapeDtypeStruct((tokens, pieces.width), jnp.bfloat16),
            jax.ShapeDtypeStruct((tokens, heads), jnp.float32),
            jax.ShapeDtypeStruct((2, tokens, width), jnp.bfloat16),
        ],
        [SMEM_SPACE] + [VMEM_SPACE] * 7 + [ANY_SPACE] * len(pieces.operands),
        [VMEM_SPACE] * 3,
        [pltpu.VMEM((tokens, pieces.width), jnp.float32), *pieces.scratch],
        [place, values, gains, shifts, cosine, sine, down, across, *pieces.operands],
        lazy=True,
    )


def to_quarters(place, outs, column, values):
    part = values.shape[1] // QUARTERS
    for r in range(QUARTERS):
        block = values[:, pl.ds(pl.multiple_of((place[0] ^ r) * part, part), part)]
        store_part(outs, r, block, slice(column, column + part))


def attend_back_kernel(pieces, ready, place, gradient, turned, totals, cosine, sine, down, across, *refs):
    weight, rest = refs[: -4 - CUTS], refs[-4 - CUTS :]
    outs, (out, mixed_grad, buffer, sems) = rest[:CUTS], rest[CUTS:]
    heads = turned.shape[1] // (3 * HEAD_DIM)
    whole_weight(pieces, ready, place, weight, buffer, sems)
    total = None
    for index in range(QUARTERS):
        column = slice(index * pieces.part, (index + 1) * pieces.part)
        term = dot_cols(gradient[0, :, column], pieces.block(buffer, index))
        total = term if total is None else total + term
    mixed_grad[...] = total.astype(jnp.bfloat16)
    matching = down[...] == across[...]
    for h in range(heads):
        query = turned[:, head(h)]
        key = turned[:, head(heads + h)]
        value = turned[:, head(2 * heads + h)]
        gradient_h = mixed_grad[:, head(h)]
        probs = jnp.exp(masked_scores(query, key, matching) - totals[:, h : h + 1])
        value_grad = dot_down(probs.astype(jnp.bfloat16), gradient_h)
        probs_grad = dot_cols(gradient_h, value)
        inner = jnp.sum(probs * probs_grad, axis=-1, keepdims=True)
        score_grad = (probs * (probs_grad - inner)).astype(jnp.bfloat16)
        query_grad = dot_rows(score_grad, key) * HEAD_DIM ** (-0.5)
        key_grad = dot_down(score_grad, query)
        out[:, head(h)] = turn(query_grad, cosine[...], -sine[...]).astype(jnp.bfloat16)
        out[:, head(heads + h)] = turn(key_grad, cosine[...], -sine[...]).astype(jnp.bfloat16)
        out[:, head(2 * heads + h)] = value_grad.astype(jnp.bfloat16)
    to_quarters(place, outs, 0, out)


def attend_back_step(order, place, gather, index, gradient, turned, totals, cosine, sine, down, across):
    pieces = Pieces(gather, index)
    return order.call(
        functools.partial(attend_back_kernel, pieces),
        packed_shapes(QUARTERS, turned.shape[0], turned.shape[1] // QUARTERS),
        [SMEM_SPACE] + [VMEM_SPACE] * 7 + [ANY_SPACE] * len(pieces.operands),
        [VMEM_SPACE] * CUTS,
        [
            pltpu.VMEM(turned.shape, jnp.bfloat16),
            pltpu.VMEM(gradient.shape[1:], jnp.bfloat16),
            *pieces.scratch,
        ],
        [place, gradient, turned, totals, cosine, sine, down, across, *pieces.operands],
        lazy=True,
    )


def rows_sum(pieces, buffer, left):
    return jnp.concatenate(
        [dot_rows(left, pieces.block(buffer, index)) for index in range(QUARTERS)], axis=1
    )


def shifted(values, amount):
    return values if amount == 0 else pltpu.roll(values, amount % values.shape[0], 0)


def merge_kernel(pieces, ready, place, values, mixed, *refs):
    weight, (out, buffer, sems) = refs[:-3], refs[-3:]
    whole_weight(pieces, ready, place, weight, buffer, sems)
    for index in range(QUARTERS):
        column = slice(index * pieces.part, (index + 1) * pieces.part)
        out[:, column] = values[:, column] + dot_rows(mixed[1], pieces.block(buffer, index))


def merge_step(order, place, gather, index, values, mixed):
    pieces = Pieces(gather, index)
    return order.call(
        functools.partial(merge_kernel, pieces),
        [jax.ShapeDtypeStruct(values.shape, jnp.float32)],
        [SMEM_SPACE] + [VMEM_SPACE] * 2 + [ANY_SPACE] * len(pieces.operands),
        [VMEM_SPACE],
        pieces.scratch,
        [place, values, mixed, *pieces.operands],
        lazy=True,
    )[0]


def conv_kernel(weights, row, ready, place, values, gains, shifts, taps, keep, *refs):
    count = len(weights[0].operands)
    operands = [refs[i * count : (i + 1) * count] for i in range(len(weights))]
    rest = refs[len(weights) * count :]
    done_out, doubled_out, filtered_out, packed = rest[:4]
    scratch = rest[4:]
    buffers = [scratch[2 * i : 2 * i + 2] for i in range(len(weights))]
    steps = [w.load(place, o, *b) for w, o, b in zip(weights, operands, buffers)]
    gating, pointwise = weights
    ready()
    shape, _ = standard(values[...])
    hidden = (shape * gains[row : row + 1] + shifts[row : row + 1]).astype(jnp.bfloat16)
    packed[0] = hidden
    wait_all(steps[0])
    doubled = rows_sum(gating, buffers[0][0], hidden)
    doubled_out[...] = doubled.astype(jnp.bfloat16)
    half = gating.width // 2
    gated = doubled[:, :half] * sigmoid(doubled[:, half:])
    reach = taps.shape[0] // 2
    filtered = None
    for k in range(taps.shape[0]):
        term = shifted(gated, reach - k) * keep[:, k : k + 1] * taps[k : k + 1]
        filtered = term if filtered is None else filtered + term
    filtered_out[...] = filtered
    shape, _ = standard(filtered)
    renormed = shape * gains[row + 1 : row + 2] + shifts[row + 1 : row + 2]
    active = (renormed * sigmoid(renormed)).astype(jnp.bfloat16)
    packed[1] = active
    wait_all(steps[1])
    for index in range(QUARTERS):
        column = slice(index * pointwise.part, (index + 1) * pointwise.part)
        term = dot_rows(active, pointwise.block(buffers[1][0], index))
        done_out[:, column] = values[:, column] + term


def conv_step(order, place, gather, row, values, gains, shifts, taps, keep):
    weights = [Pieces(gather, i) for i in range(2)]
    tokens, width = values.shape
    operands = [o for w in weights for o in w.operands]
    return order.call(
        functools.partial(conv_kernel, weights, row),
        [
            jax.ShapeDtypeStruct((tokens, width), jnp.float32),
            jax.ShapeDtypeStruct((tokens, weights[0].width), jnp.bfloat16),
            jax.ShapeDtypeStruct((tokens, weights[0].width // 2), jnp.float32),
            jax.ShapeDtypeStruct((2, tokens, width), jnp.bfloat16),
        ],
        [SMEM_SPACE] + [VMEM_SPACE] * 5 + [ANY_SPACE] * len(operands),
        [VMEM_SPACE] * 4,
        [s for w in weights for s in w.scratch],
        [place, values, gains, shifts, taps, keep, *operands],
        lazy=True,
    )


def conv_back_kernel(pieces, row, ready, place, gradient, filtered, doubled, gains, shifts, taps, keep, *refs):
    weight, rest = refs[: -6 - CUTS], refs[-6 - CUTS :]
    outs = rest[:CUTS]
    gain_out, shift_out, taps_out, doubled_grad, buffer, sems = rest[CUTS:]
    whole_weight(pieces, ready, place, weight, buffer, sems)
    total = None
    for index in range(QUARTERS):
        column = slice(index * pieces.part, (index + 1) * pieces.part)
        term = dot_cols(gradient[0, :, column], pieces.block(buffer, index))
        total = term if total is None else total + term
    gain = gains[row : row + 1]
    shape, _ = standard(filtered[...])
    renormed = shape * gain + shifts[row : row + 1]
    back, gain_grad, shift_grad = norm_back(filtered[...], silu_back(renormed, total), gain)
    gain_out[...] = gain_grad
    shift_out[...] = shift_grad
    half = doubled.shape[1] // 2
    gate = sigmoid(doubled[:, half:].astype(jnp.float32))
    gated = doubled[:, :half].astype(jnp.float32) * gate
    reach = taps.shape[0] // 2
    gated_grad = None
    for k in range(taps.shape[0]):
        kept = back * keep[:, k : k + 1]
        taps_out[k : k + 1] = jnp.sum(kept * shifted(gated, reach - k), axis=0, keepdims=True)
        term = shifted(kept, k - reach) * taps[k : k + 1]
        gated_grad = term if gated_grad is None else gated_grad + term
    doubled_grad[:, :half] = (gated_grad * gate).astype(jnp.bfloat16)
    doubled_grad[:, half:] = (gated_grad * gated * (1.0 - gate)).astype(jnp.bfloat16)
    to_quarters(place, outs, 0, doubled_grad)


def conv_back_step(order, place, gather, index, row, gradient, filtered, doubled, gains, shifts, taps, keep):
    pieces = Pieces(gather, index)
    width = filtered.shape[1]
    return order.call(
        functools.partial(conv_back_kernel, pieces, row),
        [
            *packed_shapes(QUARTERS, doubled.shape[0], doubled.shape[1] // QUARTERS),
            *vector_shapes(width),
            jax.ShapeDtypeStruct(taps.shape, jnp.float32),
        ],
        [SMEM_SPACE] + [VMEM_SPACE] * 7 + [ANY_SPACE] * len(pieces.operands),
        [VMEM_SPACE] * (3 + CUTS),
        [pltpu.VMEM(doubled.shape, jnp.bfloat16), *pieces.scratch],
        [place, gradient, filtered, doubled, gains, shifts, taps, keep, *pieces.operands],
        lazy=True,
    )


def shards(
    sizes,
    frames,
    lengths,
    languages,
    embedding,
    gains,
    shifts,
    firstup,
    firstdown,
    projection,
    merger,
    gating,
    kernel,
    pointwise,
    secondup,
    seconddown,
    cotangent,
):
    frame_count = frames.shape[0]
    dp_index = lax.axis_index("dp").astype(jnp.int32)
    place = jnp.stack(
        [
            lax.rem(dp_index, jnp.int32(QUARTERS)),
            lax.axis_index("z").astype(jnp.int32),
            lax.axis_index("core").astype(jnp.int32),
        ]
    )
    order = Order(frames)
    order_of_groups = (
        ([firstup], [firstdown]),
        ([projection, merger], [gating, pointwise]),
        ([secondup],),
        ([seconddown],),
    )
    sources = [GatherSet(place, groups) for groups in order_of_groups]
    everything = jnp.concatenate([w for s in order_of_groups for g in s for w in g], axis=1)
    everything_other = swap_core(everything)
    gathers, other_base = [], 0
    for source, groups in zip(sources, order_of_groups):
        base = 0
        for group in groups:
            gathers.append(
                Gather(place, sizes, order, group, source, base, everything_other, other_base)
            )
            base += gathers[-1].width
            other_base += QUARTERS * gathers[-1].width
    table_full, gain_full, shift_full, kernel_full = gather_small(
        [embedding, gains, shifts, kernel]
    )
    segment_all, position_all, language_all = layout(lengths, languages, frame_count)
    segment = segment_all[0]
    language_row = language_all[0]
    cosine, sine = angles(position_all[0])
    cosine = jnp.concatenate([cosine, cosine], axis=-1)[:, 0]
    sine = jnp.concatenate([-sine, sine], axis=-1)[:, 0]
    down, across = segment[:, None], segment[None, :]
    gain_rows = gain_full.astype(jnp.float32)
    shift_rows = shift_full.astype(jnp.float32)
    taps = kernel_full.astype(jnp.float32)
    reach = taps.shape[0] // 2
    segment_pad = jnp.pad(segment, (reach, reach), constant_values=-1)
    keep = jnp.stack(
        [segment_pad[k : k + frame_count] == segment for k in range(taps.shape[0])], axis=1
    ).astype(jnp.float32)
    language_hot = (
        language_row[:, None] == jnp.arange(table_full.shape[0], dtype=jnp.int32)[None, :]
    ).astype(jnp.float32)
    start_sum = frames.astype(jnp.float32) + jnp.dot(
        language_hot.astype(jnp.bfloat16), table_full, preferred_element_type=jnp.float32
    )

    gathers[0].near(40)
    gathers[1].near(32)
    order.wait(everything_other)
    gathers[0].far()
    order.wait(gathers[0].rest)
    gathers[2].near(24)
    gathers[1].far()
    gathers[3].near(16)
    first_expanded, first_packed = up_step(
        order, place, gathers[0], 0, 0, start_sum, gain_rows, shift_rows
    )
    gathers[2].far()
    gathers[4].near(8)
    after_first = down_step(order, place, gathers[1], 0, start_sum, first_packed)
    gathers[3].far()
    gathers[5].near(0)
    turned, totals, attend_packed = attend_step(
        order, place, gathers[2], 0, 1, after_first, gain_rows, shift_rows, cosine, sine, down, across
    )
    after_attention = merge_step(order, place, gathers[2], 1, after_first, attend_packed)
    gathers[4].far()
    after_conv, doubled, filtered, conv_packed = conv_step(
        order, place, gathers[3], 2, after_attention, gain_rows, shift_rows, taps, keep
    )
    gathers[5].far()
    second_expanded, second_packed = up_step(
        order, place, gathers[4], 0, 4, after_conv, gain_rows, shift_rows
    )
    second_forward = Packed(second_packed)
    encoded, grad_second, low_second, final_gain, final_shift = last_step(
        order,
        place,
        gathers[5],
        0,
        5,
        after_conv,
        second_packed,
        cotangent,
        gain_rows,
        shift_rows,
    )
    rounds = Rounds(place, sizes, order)

    low = Packed([low_second])
    down_two = Sums(Factor(low, 0, second_forward, 1, 0, seconddown.shape[1]))
    rounds.step([down_two], margin=40)
    *packed, first_packed_a, first_packed_b = down_back_step(
        order, place, gathers[5], 0, low_second, second_expanded, first_packed
    )
    backward, first_forward = Packed(packed), Packed([first_packed_a, first_packed_b])
    grad_conv, low_conv, second_gain, second_shift, *held = into_norm_step(
        order,
        place,
        gathers[4],
        0,
        0,
        4,
        1.0,
        packed,
        after_conv,
        grad_second,
        gain_rows,
        [conv_packed, attend_packed],
    )
    conv_forward, attend_forward = Packed(held[:1]), Packed(held[1:])
    up_two = Sums(Factor(second_forward, 0, backward, 0, 0, secondup.shape[1]))
    order.wait(*first_forward.all)
    rounds.step([up_two], margin=32)
    low = Packed([low_conv])
    order.wait(*conv_forward.all, *attend_forward.all)
    *packed, inner_gain, inner_shift, taps_grad = conv_back_step(
        order, place, gathers[3], 1, 3, low_conv, filtered, doubled, gain_rows, shift_rows, taps, keep
    )
    backward = Packed(packed)
    grad_attention, low_attention, outer_gain, outer_shift = into_norm_step(
        order,
        place,
        gathers[3],
        0,
        0,
        2,
        1.0,
        packed,
        after_attention,
        grad_conv,
        gain_rows,
    )
    conv = Sums(
        Factor(conv_forward, 0, backward, 0, 0, gating.shape[1]),
        Factor(conv_forward, 1, low, 0, 0, pointwise.shape[1], relative=False),
        Factor(attend_forward, 1, Packed([low_attention]), 0, 0, merger.shape[1], relative=False),
    )
    rounds.step([conv], [down_two], margin=24)
    packed = attend_back_step(
        order, place, gathers[2], 1, low_attention, turned, totals, cosine, sine, down, across
    )
    backward = Packed(packed)
    grad_first, low_first, attend_gain, attend_shift = into_norm_step(
        order,
        place,
        gathers[2],
        0,
        0,
        1,
        0.5,
        packed,
        after_first,
        grad_attention,
        gain_rows,
    )
    projection_factor = Factor(attend_forward, 0, backward, 0, 0, projection.shape[1])
    order.wait(*backward.all)
    low = Packed([low_first])
    packed = down_back_step(order, place, gathers[1], 0, low_first, first_expanded)
    backward = Packed(packed)
    down_one = Sums(Factor(low, 0, first_forward, 1, 0, firstdown.shape[1]))
    (down_two_mine,) = rounds.step([down_one], [up_two], [down_two], margin=16)
    frames_grad, low_start, first_gain, first_shift = into_norm_step(
        order, place, gathers[0], 0, 0, 0, 1.0, packed, start_sum, grad_first, gain_rows
    )
    up_one = Sums(Factor(first_forward, 0, backward, 0, 0, firstup.shape[1]))
    (up_two_mine,) = rounds.step([up_one], [conv], [up_two], margin=8)
    vectors = jnp.concatenate(
        [
            first_gain,
            attend_gain,
            outer_gain,
            inner_gain,
            second_gain,
            final_gain,
            first_shift,
            attend_shift,
            outer_shift,
            inner_shift,
            second_shift,
            final_shift,
            taps_grad,
        ]
    )
    small_packed = Packed([pack_small(language_hot, low_start[0], vectors)])
    last = Sums(
        projection_factor,
        Factor(small_packed, 0, small_packed, 1, 0, QUARTERS * LANES, relative=False),
    )
    order.wait(down_two_mine)
    (conv_mine,) = rounds.step([last], [down_one], [conv], margin=80)
    order.wait(up_two_mine)
    (down_one_mine,) = rounds.step([], [up_one], [down_one])
    order.wait(conv_mine)
    (up_one_mine,) = rounds.step([], [last], [up_one])
    pieces = rounds.share([down_two_mine, up_two_mine])
    order.wait(down_one_mine)
    (last_mine,) = rounds.step([], [], [last])
    middle_pieces = rounds.share([conv_mine, down_one_mine])
    seconddown_grad, secondup_grad = spread(
        order, place, [seconddown.shape[1], secondup.shape[1]], pieces
    )
    up_pieces = rounds.share([up_one_mine])
    middle = [gating, pointwise, merger, firstdown]
    gating_grad, pointwise_grad, merger_grad, firstdown_grad = spread(
        order, place, [w.shape[1] for w in middle], middle_pieces
    )
    pieces = rounds.share([last_mine])
    (firstup_grad,) = spread(order, place, [firstup.shape[1]], up_pieces)
    projection_grad, small = spread(
        order, place, [projection.shape[1], QUARTERS * LANES], pieces
    )
    counts = [embedding.shape[0], gains.shape[0], shifts.shape[0], kernel.shape[0]]
    table_sum, gain_sum, shift_sum, taps_sum = unpack_small(small, counts)
    return (
        encoded,
        frames_grad,
        table_sum,
        gain_sum,
        shift_sum,
        firstup_grad,
        firstdown_grad,
        projection_grad,
        merger_grad,
        gating_grad,
        taps_sum,
        pointwise_grad,
        secondup_grad,
        seconddown_grad,
    )


def solution(mesh):
    dp_size, fsdp_size = mesh.shape["dp"], mesh.shape["fsdp"]
    layers = fsdp_size // 2
    split = Mesh(mesh.devices.reshape(dp_size, layers, 2), ("dp", "z", "core"))
    return jax.shard_map(
        functools.partial(shards, (dp_size, layers)),
        mesh=split,
        in_specs=(
            P(("dp", "z", "core"), None),
            P(("dp", "z", "core"), None),
            P(("dp", "z", "core"), None),
            P(None, ("z", "core")),
            P(None, ("z", "core")),
            P(None, ("z", "core")),
            P(("z", "core"), None),
            P(("z", "core"), None),
            P(("z", "core"), None),
            P(("z", "core"), None),
            P(("z", "core"), None),
            P(None, ("z", "core")),
            P(("z", "core"), None),
            P(("z", "core"), None),
            P(("z", "core"), None),
            P(("dp", "z", "core"), None),
        ),
        out_specs=(
            P(("dp", "z", "core"), None),
            P(("dp", "z", "core"), None),
            P(None, ("z", "core")),
            P(None, ("z", "core")),
            P(None, ("z", "core")),
            P(("z", "core"), None),
            P(("z", "core"), None),
            P(("z", "core"), None),
            P(("z", "core"), None),
            P(("z", "core"), None),
            P(None, ("z", "core")),
            P(("z", "core"), None),
            P(("z", "core"), None),
            P(("z", "core"), None),
        ),
        check_vma=False,
    )
```
